512 devices in a mesh: segment: 4 (over x), dp: 128 (over z, y, core).
Axes of the slice: x: 4, y: 8, z: 8, core: 2. Of those that a mesh axis runs over, the one named last changes fastest.
Arguments:
- events: bfloat16 [512, 64, 512], P('dp'), may hold values from -6 to 6
- lengths: int32 [512], P('dp'), may hold values from 8 to 64, as said below
- balance_plan: int32 [512], P('dp'), may hold values from 0 to 7, as said below
- routes: int32 [512, 1], P('dp'), may hold values from 0 to 127; in each aligned block of 512 rows (0 to 511, 512 to 1023, ...) at most 8 rows name the same one
- w_uvqk: bfloat16 [4, 512, 2048], P('segment'), may hold values from -0.25 to 0.25
- w_out: bfloat16 [4, 512, 512], P('segment'), may hold values from -0.25 to 0.25
- rel_bias: float32 [4, 8, 64], P('segment'), may hold values from -4 to 4
- state_cotangent: bfloat16 [128, 8, 512], P('dp', None, 'segment'), may hold values from -6 to 6
Outputs:
- served: bfloat16 [128, 8, 512], P('dp', None, 'segment')
- segment_grads: bfloat16 [4, 512, 64, 512], P('segment', 'dp')
- weight_grads: float32 [4, 512, 512], P('segment', 'dp')
The draws below stay inside these ranges and needn't reach their ends.
Inputs may be any that keep to these rules, and one draw needn't show every extreme that they name: `lengths`: every device's block of 4 consecutive histories holds at least one history of 64 events. `balance_plan`: device i and device i + 64 form a pair (i below 64); over the 8 histories of a pair each value appears once. `routes`: no owner is named more than 8 times over all histories, a bound that some block reaches.
All inputs are finite; a program needn't handle non-finite values.
Results may differ from the reference program's by a relative error of at most 0.034.
Values may be sent and summed in bfloat16 or wider, within the bound.
No kernel may reach another device: no remote copies, remote signals or barrier semaphores. Data moves between devices by JAX's collectives and lax.ppermute only.
A program may use at most 128 MiB of HBM per device.

```python
import math
import jax
import jax.numpy as jnp
import numpy as np
from jax import lax

D = 512
HEADS = 8
LMAX = 64
HIST_DEV = 4
CAP = 8
HIST = 512
N_SEGMENT = 4
N_DP = 128


def draw_lengths(key, part):
    key = jax.random.fold_in(key, 11)
    first_key, second_key = jax.random.split(key)
    base = jax.random.randint(first_key, (N_DP, HIST_DEV), LMAX // 8, LMAX + 1)
    full_at = jax.random.randint(second_key, (N_DP, 1), 0, HIST_DEV)
    filled = jnp.where(jnp.arange(HIST_DEV)[None, :] == full_at, LMAX, base)
    return filled.reshape(HIST).astype(jnp.int32)


def draw_balance_plan(key, part):
    key = jax.random.fold_in(key, 23)
    pair_keys = jax.random.split(key, N_DP // 2)
    orders = jax.vmap(lambda one_key: jax.random.permutation(one_key, 2 * HIST_DEV))(pair_keys)
    lower = orders[:, :HIST_DEV].reshape(-1)
    higher = orders[:, HIST_DEV:].reshape(-1)
    return jnp.concatenate([lower, higher]).astype(jnp.int32)


def level_of(own_key, dims, cuts, least, high):
    factor_of = 1.0
    for axis_at, parts in cuts:
        draws = jax.random.uniform(jax.random.fold_in(jax.random.fold_in(own_key, 6), axis_at), (parts,), jnp.float32, least / len(cuts), high / len(cuts))
        factor_of = factor_of * jnp.repeat(jnp.exp(draws), dims[axis_at] // parts).reshape((-1,) + (1,) * (len(dims) - 1 - axis_at))
    return factor_of


def assign_block(stream_key, own, number, rows, number_of, top, reach, skew):
    order = jax.random.permutation(stream_key, number_of)
    crowded, common = portions_of(number_of, rows * top, reach, skew, True), portions_of(number_of, rows * top, reach, skew, False)
    places = jnp.arange(number_of)

    def named(tallies, offset_by):
        used = int((tallies > 0).sum())
        fixed = max(1, used // 4)
        shifted = fixed + (places - fixed + offset_by * (used - fixed)) % max(1, number_of - fixed)
        return jnp.zeros((number_of,), jnp.int32).at[order[jnp.where(places < fixed, places, shifted)]].set(jnp.asarray(tallies, jnp.int32))

    tallies = jnp.where(number % 4 == 0, named(crowded, number // 4), named(common, number - number // 4 - 1))
    mixed = jax.random.permutation(jax.random.fold_in(own, 3), number_of)
    source_of, taker = mixed[0:number_of // 2 * 2:2], mixed[1:number_of // 2 * 2:2]
    slack = jnp.minimum(tallies[source_of] - 1, reach - tallies[taker]) // 2
    slack = jnp.where((source_of == order[0]) | (taker == order[0]) | (tallies[taker] == 0), 0, jnp.maximum(slack, 0))
    shifted = jax.random.randint(jax.random.fold_in(own, 4), (number_of // 2,), 0, 1 << 20) % (slack + 1)
    tallies = tallies.at[source_of].add(-shifted).at[taker].add(shifted)
    labels = jnp.searchsorted(jnp.cumsum(tallies), jnp.arange(rows * top), side="right").astype(jnp.int32)
    grid = labels.reshape(top, rows).T
    grid = grid[jax.random.permutation(jax.random.fold_in(own, 1), rows)]
    offset_by = jax.random.randint(jax.random.fold_in(own, 2), (rows, 1), 0, top)
    return jnp.take_along_axis(grid, (jnp.arange(top)[None, :] + offset_by) % top, axis=1)


def portions_of(number_of, total, reach, lean, full):
    portions = [(1 << 20) // math.isqrt(rank ** lean) + 1 for rank in range(1, number_of + 1)]
    largest = reach if full else min(reach, max(-(-total // number_of), total * portions[0] // sum(portions)))
    least = 1 if total - largest >= number_of - 1 else 0
    holding, spare = [largest] + [least] * (number_of - 1), total - largest - least * (number_of - 1)
    while spare > 0:
        candidates = [i for i in range(1, number_of) if holding[i] < largest] or [i for i in range(1, number_of) if holding[i] < reach]
        whole, budget = sum([portions[i] for i in candidates]), spare
        for i in candidates:
            more = min(reach - holding[i], max(1, budget * portions[i] // whole), spare)
            holding[i] = holding[i] + more
            spare = spare - more
    return np.array(holding)


def bell_draw(stream_key, shape, width, most, shards=(), kind=jnp.bfloat16):
    gain = level_of(stream_key, shape, shards, -0.22, 0.18) if shards else 1.0
    result = jax.random.normal(stream_key, shape, jnp.float32) * width * gain
    return jnp.minimum(jnp.maximum(result, -most), most).astype(kind)


def setup_inputs(seed: int = 0) -> dict:
    streams_of = jax.random.split(jax.random.key(seed), 9)
    events = bell_draw(streams_of[0], (HIST, LMAX, D), 1.0, 6.0, ((0, 128),))
    lengths = draw_lengths(jax.random.fold_in(streams_of[8], 71), 0)
    balance_plan = draw_balance_plan(jax.random.fold_in(streams_of[8], 71), 0)
    routes_keys = jax.random.split(jax.random.fold_in(streams_of[3], 1), HIST // HIST)
    routes_turns = jax.random.permutation(jax.random.fold_in(streams_of[3], 3), HIST // HIST)
    routes = jax.vmap(lambda own, number: assign_block(jax.random.fold_in(streams_of[3], 2), own, number, HIST, N_DP, 1, CAP, 2))(routes_keys, routes_turns).reshape((HIST, 1))
    w_uvqk = bell_draw(streams_of[4], (N_SEGMENT, D, 4 * D), D ** -0.5, 0.25, ((0, 4),))
    w_out = bell_draw(streams_of[5], (N_SEGMENT, D, D), D ** -0.5, 0.25, ((0, 4),))
    rel_bias = bell_draw(streams_of[6], (N_SEGMENT, HEADS, LMAX), 1.0, 4.0, ((0, 4),), jnp.float32)
    state_cotangent = bell_draw(streams_of[7], (N_DP, CAP, D), 1.0, 6.0, ((0, 128), (2, 4)))
    return dict(events=events, lengths=lengths, balance_plan=balance_plan, routes=routes, w_uvqk=w_uvqk, w_out=w_out, rel_bias=rel_bias, state_cotangent=state_cotangent)


def normalize(values_in):
    average = lax.optimization_barrier(jnp.mean(values_in, axis=-1, keepdims=True))
    centred = values_in - average
    return centred * lax.rsqrt(lax.optimization_barrier(jnp.mean(centred * centred, axis=-1, keepdims=True)) + 1e-06)

def hstu_layer(inputs, seq_lengths, w_uvqk, w_out, rel_bias):
    histories, positions, features = inputs.shape
    head_count = rel_bias.shape[0]
    head_size = features // head_count
    flat_rows = inputs.reshape(histories * positions, features).astype(jnp.float32)
    normed = normalize(flat_rows).astype(jnp.bfloat16)
    projected = jax.nn.silu(jnp.dot(normed, w_uvqk, preferred_element_type=jnp.float32)).astype(jnp.bfloat16)
    gate_rows = projected[:, :features]
    value_rows = projected[:, features:2 * features].reshape(histories, positions, head_count, head_size)
    queries = projected[:, 2 * features:3 * features].reshape(histories, positions, head_count, head_size)
    key_rows = projected[:, 3 * features:].reshape(histories, positions, head_count, head_size)
    scores = jnp.einsum('bihe,bjhe->bhij', queries.astype(jnp.float32), key_rows.astype(jnp.float32)) * head_size ** (-0.5)
    row_pos = jnp.arange(positions, dtype=jnp.int32)
    offset = row_pos[:, None] - row_pos[None, :]
    pos_bias = jnp.take(rel_bias, jnp.clip(offset, 0, positions - 1), axis=1)
    allowed = (offset >= 0)[None, None] & (row_pos[None, None, None, :] < seq_lengths[:, None, None, None])
    weights = jnp.where(allowed, jax.nn.silu(scores + pos_bias[None]), 0.0).astype(jnp.bfloat16)
    attended = jnp.einsum('bhij,bjhe->bihe', weights.astype(jnp.float32), value_rows.astype(jnp.float32))
    attended = attended.reshape(histories * positions, features)
    branch = (normalize(attended) * gate_rows.astype(jnp.float32)).astype(jnp.bfloat16)
    output = (flat_rows + jnp.dot(branch, w_out, preferred_element_type=jnp.float32)).astype(jnp.bfloat16)
    return (output.reshape(histories, positions, features), branch)

def reference(events, lengths, balance_plan, routes, w_uvqk, w_out, rel_bias, state_cotangent):
    order_all = jnp.arange(HIST, dtype=jnp.int32)
    device_of = order_all // HIST_DEV
    half_count = N_DP // 2
    owner_dev = device_of % half_count + (balance_plan >= HIST_DEV).astype(jnp.int32) * half_count
    target = owner_dev * HIST_DEV + balance_plan % HIST_DEV
    balanced = jnp.zeros_like(events).at[target].set(events)
    balanced_lengths = jnp.zeros((HIST,), jnp.int32).at[target].set(lengths)
    blocked_lengths = balanced_lengths.reshape(N_DP, HIST_DEV)
    acts = balanced
    segment_inputs = []
    for segment_no in range(N_SEGMENT):
        segment_inputs.append(acts)

        def forward_block(packed, segment_no=segment_no):
            return hstu_layer(packed[0], packed[1], w_uvqk[segment_no], w_out[segment_no], rel_bias[segment_no])[0]
        acts = lax.map(forward_block, (acts.reshape(N_DP, HIST_DEV, LMAX, D), blocked_lengths)).reshape(HIST, LMAX, D)
    last_event = jnp.arange(LMAX, dtype=jnp.int32)[None, :] == balanced_lengths[:, None] - 1
    states = jnp.einsum('al,ald->ad', last_event.astype(jnp.float32), acts.astype(jnp.float32)).astype(jnp.bfloat16)
    owner_of = routes[:, 0]
    same_owner = (owner_of[:, None] == owner_of[None, :]) & (order_all[None, :] < order_all[:, None])
    slot_col = lax.optimization_barrier(jnp.sum(same_owner.astype(jnp.int32), axis=1)).astype(jnp.int32)
    served = jnp.zeros((N_DP, CAP, D), jnp.bfloat16).at[owner_of, slot_col].set(states)
    final_cot = state_cotangent[owner_of, slot_col]
    cotan = jnp.where(last_event[:, :, None], final_cot[:, None, :], jnp.zeros((), jnp.bfloat16))
    grads = [None] * N_SEGMENT
    w_grads = [None] * N_SEGMENT
    for segment_no in reversed(range(N_SEGMENT)):

        def backward_block(packed, segment_no=segment_no):
            block_in, block_len, block_cot = packed
            produced, pull_back, branch = jax.vjp(lambda value_in: hstu_layer(value_in, block_len, w_uvqk[segment_no], w_out[segment_no], rel_bias[segment_no]), block_in, has_aux=True)
            term = jnp.dot(branch.T, block_cot.reshape(-1, D), preferred_element_type=jnp.float32)
            return (pull_back(block_cot)[0], term)
        input_grad, terms = lax.map(backward_block, (segment_inputs[segment_no].reshape(N_DP, HIST_DEV, LMAX, D), blocked_lengths, cotan.reshape(N_DP, HIST_DEV, LMAX, D)))
        grads[segment_no] = input_grad.reshape(HIST, LMAX, D)
        w_grads[segment_no] = lax.optimization_barrier(jnp.sum(terms, axis=0))
        cotan = grads[segment_no]
    return (served, jnp.stack(grads), jnp.stack(w_grads))
```

```python
import functools

import jax
import jax.numpy as jnp
from jax import lax
from jax.experimental import pallas as pl
from jax.experimental.pallas import tpu as pltpu
from jax.sharding import Mesh, PartitionSpec as P

BF = jnp.bfloat16
F32 = jnp.float32
DP = ("z", "y", "core")
DEV_HIST = 4
ROWS = 64
WIDTH = 512
HEAD_COLS = 64
PAIRS = 4
LAYERS = 4
SLOTS = 8
MSG = 208
NN = (((1,), (0,)), ((), ()))
NT = (((1,), (1,)), ((), ()))
TN = (((0,), (0,)), ((), ()))


def mm(a, b, dims=NN):
    return lax.dot_general(a, b, dims, preferred_element_type=F32)


def iota(shape, dim):
    return lax.broadcasted_iota(jnp.int32, shape, dim)


def row_mean(a):
    return jnp.mean(a, axis=-1, keepdims=True)


def sigmoid(a):
    return 0.5 * jnp.tanh(0.5 * a) + 0.5


def dp_place():
    ny, nc = lax.axis_size("y"), lax.axis_size("core")
    return (lax.axis_index("z") * ny + lax.axis_index("y")) * nc + lax.axis_index("core")


def wanted_value():
    upper = (lax.axis_index("z") >= lax.axis_size("z") // 2).astype(jnp.int32)
    return upper * DEV_HIST + lax.axis_index("segment")


def routing_kernel(block_rows, own_rows, table_ref, seg_ref, payload_ref, hot_ref, count_ref):
    n_dp = table_ref.shape[0]
    hist = n_dp * DEV_HIST
    me = dp_place()
    segment = lax.axis_index("segment")
    table = table_ref[...].astype(F32).astype(BF)
    spread = mm(table, (iota((128, hist), 0) == iota((128, hist), 1) % DEV_HIST).astype(BF))
    own = iota((n_dp, hist), 1) // DEV_HIST == iota((n_dp, hist), 0)
    routes = jnp.sum(jnp.where(own, spread, 0.0), axis=0, keepdims=True)
    hit = jnp.broadcast_to((routes == me.astype(F32)).astype(F32), (16, hist))
    earlier = (iota((hist, hist), 0) < iota((hist, hist), 1)).astype(BF)
    slot = mm(hit.astype(BF), earlier)
    hot = jnp.where(slot == iota((16, hist), 0).astype(F32), hit, 0.0).astype(BF)
    mine = (iota((hist, n_dp), 0) == iota((hist, n_dp), 1) * DEV_HIST + segment).astype(BF)
    picks = mm(hot, mine).astype(BF)
    cotangent = jnp.concatenate([seg_ref[q, 0:16, :] for q in range(LAYERS)], axis=1)
    payload_ref[...] = mm(picks, cotangent, TN).astype(BF)
    total = hot_ref.shape[2]
    place, history = iota((hist, total), 1), iota((hist, total), 0)
    within = place % block_rows - own_rows
    first = ((place // block_rows) * 2 + within) * DEV_HIST
    valid = (within >= 0) & (within < 2)
    for h in range(DEV_HIST):
        move = jnp.where(valid & (history == first + h), 1.0, 0.0).astype(BF)
        hot_ref[h] = mm(hot, move).astype(BF)
    other = lax.rem(me + n_dp // 2, n_dp)
    pair = jnp.concatenate([table_ref[pl.ds(me, 1), :], table_ref[pl.ds(other, 1), :]], axis=0)
    lane = iota((2, 128), 1)
    fits = (lane >= 4) & (lane < 8) & (pair // 128 == wanted_value())
    length = jnp.sum(jnp.where(fits, (pair % 128).astype(F32), 0.0), axis=1, keepdims=True)
    length = jnp.sum(length, axis=0, keepdims=True)
    count_ref[...] = jnp.broadcast_to(length, count_ref.shape).astype(jnp.int32)


def layers_kernel(
    plan_ref, events_ref, other_ref, count_ref, cot_ref, seg_ref,
    w_in_ref, w_out_ref, near_a, near_b, swap_a, swap_b, far_a, far_b,
    out_ref,
    weights, proj_s, dsilu_s, normed_s, rstd_s, norm_o_s, rstd_o_s, bias_s, att_s, datt_s, sems,
):
    segment, core = lax.axis_index("segment"), lax.axis_index("core")
    half = WIDTH // 2
    near = lax.rem(segment + 1 + 2 * core, LAYERS)
    swap = lax.rem(segment + 3 + 2 * core, LAYERS)
    far = lax.rem(segment + 2, LAYERS)
    low = pl.ds(pl.multiple_of(core * half, half), half)
    high = pl.ds(pl.multiple_of((1 - core) * half, half), half)
    pltpu.make_async_copy(w_in_ref, weights.at[segment, :, pl.ds(0, 4 * WIDTH)], sems.at[segment]).start()
    pltpu.make_async_copy(w_out_ref, weights.at[segment, :, pl.ds(4 * WIDTH, WIDTH)], sems.at[segment]).start()
    pltpu.make_async_copy(near_a, weights.at[near, low], sems.at[near]).start()
    pltpu.make_async_copy(near_b, weights.at[near, high], sems.at[near]).start()
    pltpu.make_async_copy(swap_a, weights.at[swap, high], sems.at[swap]).start()
    pltpu.make_async_copy(swap_b, weights.at[swap, low], sems.at[swap]).start()
    pltpu.make_async_copy(far_a, weights.at[far, low], sems.at[far]).start()
    pltpu.make_async_copy(far_b, weights.at[far, high], sems.at[far]).start()

    lane, row = iota((ROWS, 128), 1), iota((ROWS, 128), 0)
    left = (lane < HEAD_COLS).astype(F32)
    left_b, right_b = left.astype(BF), (1.0 - left).astype(BF)
    column = jnp.where(lane < HEAD_COLS, lane, lane - HEAD_COLS)
    count = count_ref[...]
    allowed = (column <= row) & (column < count)

    for l in range(LAYERS):
        table = seg_ref[l, 16:32, :].astype(F32)
        table = table[0:4] + table[4:8] + table[8:12]
        for p in range(PAIRS):
            wide = jnp.broadcast_to(table[p : p + 1], (ROWS, 128))
            bias_s[l, p] = pltpu.roll(wide, 0, 1, stride=1, stride_axis=0)

    def block_diagonal(a):
        return jnp.concatenate([a * left_b, a * right_b], axis=0)

    def merge(a):
        return jnp.where(lane < HEAD_COLS, a[:ROWS], a[ROWS:])

    def part(kind, p):
        return pl.ds(kind * WIDTH + p * 128, 128)

    value = wanted_value()
    found = jnp.int32(0)
    acts = jnp.zeros((ROWS, WIDTH), F32)
    for h in range(DEV_HIST):
        same = (plan_ref[h] == value).astype(jnp.int32)
        found = found + same
        acts = jnp.where(same == 1, events_ref[h].astype(F32), acts)
    acts = jnp.where(found > 0, acts, other_ref[...].astype(F32))

    for l in range(LAYERS):
        average = row_mean(acts)
        centred = acts - average
        rstd = lax.rsqrt(row_mean(centred * centred) + 1e-6)
        normed = centred * rstd
        normed_s[l] = normed
        rstd_s[l] = jnp.broadcast_to(rstd, (ROWS, 128))
        pltpu.make_async_copy(weights.at[l], weights.at[l], sems.at[l]).wait()
        normed_b = normed.astype(BF)
        for kind in range(4):
            cols = pl.ds(kind * WIDTH, WIDTH)
            pre = mm(normed_b, weights[l, :, cols])
            gated = sigmoid(pre)
            silu = pre * gated
            proj_s[l, :, cols] = silu.astype(BF)
            dsilu_s[l, :, cols] = gated + silu * (1.0 - gated)
        outs = []
        for p in range(PAIRS):
            keys = block_diagonal(proj_s[l, :, part(3, p)])
            score = mm(proj_s[l, :, part(2, p)], keys, NT) * 0.125 + bias_s[l, p]
            gated = sigmoid(score)
            silu = score * gated
            att = jnp.where(allowed, silu, 0.0).astype(BF)
            att_s[l, p] = att
            datt_s[l, p] = jnp.where(allowed, gated + silu * (1.0 - gated), 0.0) * 0.125
            outs.append(mm(att, block_diagonal(proj_s[l, :, part(1, p)])))
        mixed = jnp.concatenate(outs, axis=1)
        centred = mixed - row_mean(mixed)
        rstd = lax.rsqrt(row_mean(centred * centred) + 1e-6)
        norm_o = centred * rstd
        norm_o_s[l] = norm_o
        rstd_o_s[l] = jnp.broadcast_to(rstd, (ROWS, 128))
        branch = (norm_o * proj_s[l, :, pl.ds(0, WIDTH)].astype(F32)).astype(BF)
        out_ref[l, 64:128, :] = branch
        acts = (acts + mm(branch, weights[l, :, pl.ds(4 * WIDTH, WIDTH)])).astype(BF).astype(F32)

    last = iota((ROWS, WIDTH), 0) == count[:, 0:1] - 1
    state = jnp.sum(jnp.where(last, acts, 0.0), axis=0, keepdims=True)
    for q in range(LAYERS):
        quarter = jnp.broadcast_to(state[:, 128 * q : 128 * q + 128], (16, 128))
        out_ref[q, 192:208, :] = jnp.concatenate([quarter] * 4, axis=1).astype(BF)
    seed = jnp.sum(cot_ref[...].astype(F32), axis=0, keepdims=True)
    cot = jnp.where(last, jnp.broadcast_to(seed, (ROWS, WIDTH)), 0.0).astype(BF)

    for l in reversed(range(LAYERS)):
        out_ref[l, 128:192, :] = cot
        d_branch = mm(cot, weights[l, :, pl.ds(4 * WIDTH, WIDTH)], NT).astype(BF).astype(F32)
        norm_o = norm_o_s[l]
        d_gate = (d_branch * norm_o).astype(BF)
        d_norm = d_branch * proj_s[l, :, pl.ds(0, WIDTH)].astype(F32)
        d_mixed = rstd_o_s[l][:, 0:1] * (d_norm - row_mean(d_norm) - norm_o * row_mean(d_norm * norm_o))
        d_mixed = d_mixed.astype(BF)
        d_value, d_query, d_key = [], [], []
        for p in range(PAIRS):
            d_out = d_mixed[:, 128 * p : 128 * p + 128]
            d_att = mm(d_out, block_diagonal(proj_s[l, :, part(1, p)]), NT).astype(BF).astype(F32)
            d_value.append(merge(mm(att_s[l, p], d_out, TN)))
            d_score = (d_att * datt_s[l, p]).astype(BF)
            d_query.append(mm(d_score, block_diagonal(proj_s[l, :, part(3, p)])))
            d_key.append(merge(mm(d_score, proj_s[l, :, part(2, p)], TN)))
        d_normed = jnp.zeros((ROWS, WIDTH), F32)
        for kind, pieces in enumerate(([d_gate], d_value, d_query, d_key)):
            cols = pl.ds(kind * WIDTH, WIDTH)
            whole = pieces[0] if len(pieces) == 1 else jnp.concatenate(pieces, axis=1)
            d_pre = whole.astype(BF).astype(F32) * dsilu_s[l, :, cols]
            d_normed = d_normed + mm(d_pre.astype(BF), weights[l, :, cols], NT)
        d_normed = d_normed.astype(BF).astype(F32)
        normed = normed_s[l]
        d_in = rstd_s[l][:, 0:1] * (d_normed - row_mean(d_normed) - normed * row_mean(d_normed * normed))
        cot = (d_in + cot.astype(F32)).astype(BF)
        out_ref[l, 0:64, :] = cot


def gradient_kernel(own_rows, got_ref, grads_ref, keep_ref, send_ref):
    core = lax.axis_index("core")
    for t in range(LAYERS):
        grads_ref[t] = got_ref[t, 0:64, :]
    branch = jnp.concatenate([got_ref[t, 64:128, :] for t in range(LAYERS)], axis=0)
    cot = jnp.concatenate([got_ref[t, 128:192, :] for t in range(LAYERS)], axis=0)
    half = WIDTH // 2
    to, source = iota((WIDTH, WIDTH), 1), iota((WIDTH, WIDTH), 0)
    side = jnp.where(to < half, core, 1 - core)
    within = jnp.where(to < half, to, to - half)
    wanted = (within // own_rows) * (2 * own_rows) + side * own_rows + within % own_rows
    order = (source == wanted).astype(F32).astype(BF)
    ordered = mm(branch, order).astype(BF)
    keep_ref[...] = mm(ordered[:, :half], cot, TN)
    send_ref[0:half, :] = mm(ordered[:, half:], cot, TN).astype(BF)
    states = [got_ref[t, 192:208, 0:128] for t in range(LAYERS)]
    send_ref[half : half + 16, :] = jnp.concatenate(states, axis=1)


def packing_kernel(block_rows, own_rows, keep_ref, send_ref, got_ref, out_ref):
    half = WIDTH // 2
    core = lax.axis_index("core")
    total = (keep_ref[...] + got_ref[0:half, :].astype(F32)).astype(BF)
    rows = out_ref.shape[0]
    place, source = iota((rows, half), 0), iota((rows, half), 1)
    within = place % block_rows
    pick = (within < own_rows) & (source == (place // block_rows) * own_rows + within)
    laid = mm(pick.astype(F32).astype(BF), total)
    own = send_ref[half : half + 16, :].astype(F32)[0:1]
    other = got_ref[half : half + 16, :].astype(F32)[0:1]
    first = jnp.where(core == 0, own, other)
    second = jnp.where(core == 0, other, own)
    at = iota((rows, WIDTH), 0) % block_rows
    laid = laid + jnp.where(at == own_rows, first, 0.0) + jnp.where(at == own_rows + 1, second, 0.0)
    out_ref[...] = laid.astype(BF)


def result_kernel(block_rows, got_ref, hot_ref, served_ref, weight_ref):
    rows = got_ref.shape[0]
    out_rows = weight_ref.shape[0]
    lead = max(16, out_rows)
    pick = (iota((lead, rows), 1) % block_rows == iota((lead, rows), 0)).astype(F32).astype(BF)
    got = got_ref[...]
    weight_ref[...] = mm(pick, got)[0:out_rows]
    served = jnp.zeros((16, 128), F32)
    for h in range(DEV_HIST):
        served = served + mm(hot_ref[h], got[:, 128 * h : 128 * h + 128])
    served_ref[...] = served[0:SLOTS].astype(BF)


def shape(dims, dtype):
    return jax.ShapeDtypeStruct(dims, dtype)


def call(kernel, outs, scratch=(), in_specs=None, limit=48):
    specs = {} if in_specs is None else {"in_specs": in_specs}
    return pl.pallas_call(
        kernel,
        out_shape=outs,
        scratch_shapes=scratch,
        **specs,
        compiler_params=pltpu.CompilerParams(vmem_limit_bytes=limit * 1024 * 1024),
    )


def body(events, lengths, balance_plan, routes, w_uvqk, w_out, rel_bias, state_cotangent):
    n_z, n_y, n_core = (lax.axis_size(a) for a in DP)
    n_dp = n_z * n_y * n_core
    chips = n_z * n_y
    core = lax.axis_index("core")
    own_rows = WIDTH // n_dp
    block_rows = -(-(own_rows + 2) // 8) * 8
    half = WIDTH // 2

    with jax.named_scope("section_weights"):
        ring = [(s * 2, (s - 1) % LAYERS * 2) for s in range(LAYERS)]
        ring += [(s * 2 + 1, (s + 1) % LAYERS * 2 + 1) for s in range(LAYERS)]
        swap = [(0, 1), (1, 0)]
        w_in, w_back = w_uvqk[0], w_out[0]
        upper = jnp.concatenate([w_in[:half], w_back[:half]], axis=1)
        lower = jnp.concatenate([w_in[half:], w_back[half:]], axis=1)
        first = jnp.where(core == 0, upper, lower)
        second = jnp.where(core == 0, lower, upper)
        near_a = lax.ppermute(first, ("segment", "core"), ring)
        near_b = lax.ppermute(second, ("segment", "core"), ring)
        far_a = lax.ppermute(near_a, ("segment", "core"), ring)
        swap_a = lax.ppermute(near_a, "core", swap)
        swap_b = lax.ppermute(near_b, "core", swap)
        far_b = lax.ppermute(far_a, "core", swap)

    with jax.named_scope("events"):
        partner_value = DEV_HIST + 2 * lax.axis_index("segment") - wanted_value()
        chosen = (balance_plan == partner_value)[:, None, None]
        outgoing = jnp.sum(jnp.where(chosen, events, jnp.zeros((), BF)), axis=0, dtype=BF)
        other_events = lax.ppermute(outgoing, "z", [(i, (i + n_z // 2) % n_z) for i in range(n_z)])

    with jax.named_scope("routing"):
        packed = balance_plan * 128 + lengths
        facts = jnp.concatenate([routes[:, 0], packed, jnp.zeros((120,), jnp.int32)])
        table = lax.all_gather(facts, DP)
        table = table.reshape(n_dp, 128)
        even, odd = rel_bias[0, 0::2], rel_bias[0, 1::2]
        base = jnp.concatenate([even[:, 0:1], odd[:, ::-1], even[:, :0:-1]], axis=1)
        high = lax.reduce_precision(base, 8, 7)
        middle = lax.reduce_precision(base - high, 8, 7)
        low = base - high - middle
        cot = jnp.concatenate(
            [state_cotangent[0], jnp.zeros((8, 128), BF)]
            + [a.astype(BF) for a in (high, middle, low)]
            + [jnp.zeros((4, 128), BF)]
        )
        seg_facts = lax.all_gather(cot, "segment")
        payload, hot, count = call(
            functools.partial(routing_kernel, block_rows, own_rows),
            (
                shape((n_dp, WIDTH), BF),
                shape((DEV_HIST, 16, chips * block_rows), BF),
                shape((ROWS, 128), jnp.int32),
            ),
        )(table, seg_facts)
        cot_rows = lax.all_to_all(payload.reshape(n_dp, 1, WIDTH), DP, 0, 0, tiled=True)
        cot_rows = cot_rows.reshape(n_dp, WIDTH)

    any_spec, vmem = pl.BlockSpec(memory_space=pl.ANY), pl.BlockSpec(memory_space=pltpu.VMEM)
    with jax.named_scope("layers"):
        message = call(
            layers_kernel,
            shape((LAYERS, MSG, WIDTH), BF),
            scratch=[
                pltpu.VMEM((LAYERS, WIDTH, 5 * WIDTH), BF),
                pltpu.VMEM((LAYERS, ROWS, 4 * WIDTH), BF),
                pltpu.VMEM((LAYERS, ROWS, 4 * WIDTH), F32),
                pltpu.VMEM((LAYERS, ROWS, WIDTH), F32),
                pltpu.VMEM((LAYERS, ROWS, 128), F32),
                pltpu.VMEM((LAYERS, ROWS, WIDTH), F32),
                pltpu.VMEM((LAYERS, ROWS, 128), F32),
                pltpu.VMEM((LAYERS, PAIRS, ROWS, 128), F32),
                pltpu.VMEM((LAYERS, PAIRS, ROWS, 128), BF),
                pltpu.VMEM((LAYERS, PAIRS, ROWS, 128), F32),
                pltpu.SemaphoreType.DMA((LAYERS,)),
            ],
            in_specs=[pl.BlockSpec(memory_space=pltpu.SMEM)] + [vmem] * 5 + [any_spec] * 8,
        )(
            balance_plan, events, other_events, count, cot_rows, seg_facts,
            w_in, w_back, near_a, near_b, swap_a, swap_b, far_a, far_b,
        )

    with jax.named_scope("section_exchange"):
        arrived = lax.all_to_all(message, "segment", 0, 0, tiled=True)
    with jax.named_scope("weight_gradient"):
        grads, keep, send = call(
            functools.partial(gradient_kernel, own_rows),
            (
                shape((LAYERS, ROWS, WIDTH), BF),
                shape((half, WIDTH), F32),
                shape((half + 16, WIDTH), BF),
            ),
        )(arrived)
        partner = lax.ppermute(send, "core", swap)
        blocks = call(
            functools.partial(packing_kernel, block_rows, own_rows),
            shape((chips * block_rows, WIDTH), BF),
        )(keep, send, partner)
        blocks = lax.all_to_all(
            blocks.reshape(chips, block_rows, WIDTH), ("z", "y"), 0, 0, tiled=True
        )
        served, weight = call(
            functools.partial(result_kernel, block_rows),
            (shape((SLOTS, 128), BF), shape((own_rows, WIDTH), F32)),
        )(blocks.reshape(chips * block_rows, WIDTH), hot)
    return served[None], grads[None], weight[None]


def solution(mesh):
    devices = mesh.devices
    n_segment, n_dp = devices.shape
    side = 1
    while side * side * 2 < n_dp:
        side *= 2
    fine = Mesh(
        devices.reshape(n_segment, n_dp // (2 * side), side, 2), ("segment",) + DP
    )
    return jax.shard_map(
        body,
        mesh=fine,
        in_specs=(
            P(DP, None, None),
            P(DP),
            P(DP),
            P(DP, None),
            P("segment", None, None),
            P("segment", None, None),
            P("segment", None, None),
            P(DP, None, "segment"),
        ),
        out_specs=(
            P(DP, None, "segment"),
            P("segment", DP, None, None),
            P("segment", DP, None),
        ),
        check_vma=False,
    )
```

```python
import functools

import jax
import jax.numpy as jnp
from jax import lax
from jax.experimental import pallas as pl
from jax.experimental.pallas import tpu as pltpu
from jax.sharding import Mesh, PartitionSpec as P

BF = jnp.bfloat16
F32 = jnp.float32
DP = ("z", "y", "core")
DEV_HIST = 4
ROWS = 64
WIDTH = 512
HEAD_COLS = 64
PAIRS = 4
LAYERS = 4
SLOTS = 8
MSG = 208
NN = (((1,), (0,)), ((), ()))
NT = (((1,), (1,)), ((), ()))
TN = (((0,), (0,)), ((), ()))


def mm(a, b, dims=NN):
    return lax.dot_general(a, b, dims, preferred_element_type=F32)


def iota(shape, dim):
    return lax.broadcasted_iota(jnp.int32, shape, dim)


def row_mean(a):
    return jnp.mean(a, axis=-1, keepdims=True)


def sigmoid(a):
    return 0.5 * jnp.tanh(0.5 * a) + 0.5


def dp_place():
    ny, nc = lax.axis_size("y"), lax.axis_size("core")
    return (lax.axis_index("z") * ny + lax.axis_index("y")) * nc + lax.axis_index("core")


def wanted_value():
    upper = (lax.axis_index("z") >= lax.axis_size("z") // 2).astype(jnp.int32)
    return upper * DEV_HIST + lax.axis_index("segment")


def whole_part(a, d):
    if d & (d - 1) == 0:
        return a // d
    return jnp.floor((a.astype(F32) + 0.5) * (1.0 / d)).astype(jnp.int32)


def routing_kernel(block_rows, own_rows, table_ref, seeds_ref, hot_ref, count_ref):
    n_dp = table_ref.shape[0]
    hist = n_dp * DEV_HIST
    me = dp_place()
    facts = table_ref[:, SLOTS * 128 : SLOTS * 128 + 128]
    spread = mm(facts, (iota((128, hist), 0) == iota((128, hist), 1) % DEV_HIST).astype(F32).astype(BF))
    own = iota((n_dp, hist), 1) // DEV_HIST == iota((n_dp, hist), 0)
    routes = jnp.sum(jnp.where(own, spread, 0.0), axis=0, keepdims=True)

    routes_wide = jnp.broadcast_to(routes, (16, hist))
    history, mine = iota((16, hist), 1), me * DEV_HIST + iota((16, hist), 0)
    route = jnp.sum(jnp.where(history == mine, routes_wide, 0.0), axis=1, keepdims=True)
    before = (routes_wide == route) & (history < mine)
    slot = jnp.sum(before.astype(F32), axis=1, keepdims=True)
    source = iota((16, n_dp), 1).astype(F32)
    seeds = jnp.zeros((16, 128), F32)
    for k in range(SLOTS):
        pick = jnp.where((source == route) & (slot == float(k)), 1.0, 0.0).astype(BF)
        seeds = seeds + mm(pick, table_ref[:, 128 * k : 128 * k + 128])
    for q in range(LAYERS):
        seeds_ref[q] = jnp.broadcast_to(seeds[q : q + 1], (16, 128)).astype(BF)

    hit = jnp.broadcast_to((routes == me.astype(F32)).astype(F32), (16, hist))
    earlier = (iota((hist, hist), 0) < iota((hist, hist), 1)).astype(F32).astype(BF)
    place_of = mm(hit.astype(BF), earlier)
    hot = jnp.where(place_of == iota((16, hist), 0).astype(F32), hit, 0.0).astype(BF)
    total = hot_ref.shape[2]
    place, history = iota((hist, total), 1), iota((hist, total), 0)
    chip = whole_part(place, block_rows)
    within = place - chip * block_rows - own_rows
    first = (chip * 2 + within) * DEV_HIST
    valid = (within >= 0) & (within < 2)
    for h in range(DEV_HIST):
        move = jnp.where(valid & (history == first + h), 1.0, 0.0).astype(BF)
        hot_ref[h] = mm(hot, move).astype(BF)

    other = lax.rem(me + n_dp // 2, n_dp)
    known = facts.astype(F32)
    ahead = pltpu.roll(known, 124, 1)
    row, lane = iota((n_dp, 128), 0), iota((n_dp, 128), 1)
    fits = ((row == me) | (row == other)) & (lane >= 4) & (lane < 8)
    fits = fits & (known == wanted_value().astype(F32))
    length = jnp.sum(jnp.where(fits, ahead, 0.0), axis=1, keepdims=True)
    length = jnp.sum(length, axis=0, keepdims=True)
    count_ref[...] = jnp.broadcast_to(length, count_ref.shape).astype(jnp.int32)


def layers_kernel(
    plan_ref, events_ref, other_ref, count_ref, cot_ref, gathered_ref,
    out_ref,
    weights, tables, proj_s, dsilu_s, normed_s, rstd_s, norm_o_s, rstd_o_s, bias_s, att_s, datt_s, sems, table_sem,
):
    half = WIDTH // 2
    for l in range(LAYERS):
        pltpu.make_async_copy(
            gathered_ref.at[l, 0, pl.ds(half, 16), pl.ds(0, 128)], tables.at[l], table_sem.at[l]
        ).start()
    for l in range(LAYERS):
        for c in range(2):
            pltpu.make_async_copy(
                gathered_ref.at[l, c, pl.ds(0, half)], weights.at[l, pl.ds(c * half, half)], sems.at[l, c]
            ).start()

    lane, row = iota((ROWS, 128), 1), iota((ROWS, 128), 0)
    left = (lane < HEAD_COLS).astype(F32)
    left_b, right_b = left.astype(BF), (1.0 - left).astype(BF)
    column = jnp.where(lane < HEAD_COLS, lane, lane - HEAD_COLS)
    count = count_ref[...]
    allowed = (column <= row) & (column < count)

    for l in range(LAYERS):
        pltpu.make_async_copy(tables.at[l], tables.at[l], table_sem.at[l]).wait()
        table = tables[l].astype(F32)
        table = table[0:4] + table[4:8] + table[8:12]
        for p in range(PAIRS):
            wide = jnp.broadcast_to(table[p : p + 1], (ROWS, 128))
            bias_s[l, p] = pltpu.roll(wide, 0, 1, stride=1, stride_axis=0)

    def block_diagonal(a):
        return jnp.concatenate([a * left_b, a * right_b], axis=0)

    def merge(a):
        return jnp.where(lane < HEAD_COLS, a[:ROWS], a[ROWS:])

    def part(kind, p):
        return pl.ds(kind * WIDTH + p * 128, 128)

    value = wanted_value()
    found = jnp.int32(0)
    acts = jnp.zeros((ROWS, WIDTH), F32)
    for h in range(DEV_HIST):
        same = (plan_ref[h] == value).astype(jnp.int32)
        found = found + same
        acts = jnp.where(same == 1, events_ref[h].astype(F32), acts)
    acts = jnp.where(found > 0, acts, other_ref[...].astype(F32))

    for l in range(LAYERS):
        average = row_mean(acts)
        centred = acts - average
        rstd = lax.rsqrt(row_mean(centred * centred) + 1e-6)
        normed = centred * rstd
        normed_s[l] = normed
        rstd_s[l] = jnp.broadcast_to(rstd, (ROWS, 128))
        for c in range(2):
            piece = weights.at[l, pl.ds(c * half, half)]
            pltpu.make_async_copy(piece, piece, sems.at[l, c]).wait()
        normed_b = normed.astype(BF)
        for kind in range(4):
            cols = pl.ds(kind * WIDTH, WIDTH)
            pre = mm(normed_b, weights[l, :, cols])
            gated = sigmoid(pre)
            silu = pre * gated
            proj_s[l, :, cols] = silu.astype(BF)
            dsilu_s[l, :, cols] = gated + silu * (1.0 - gated)
        outs = []
        for p in range(PAIRS):
            keys = block_diagonal(proj_s[l, :, part(3, p)])
            score = mm(proj_s[l, :, part(2, p)], keys, NT) * 0.125 + bias_s[l, p]
            gated = sigmoid(score)
            silu = score * gated
            att = jnp.where(allowed, silu, 0.0).astype(BF)
            att_s[l, p] = att
            datt_s[l, p] = jnp.where(allowed, gated + silu * (1.0 - gated), 0.0) * 0.125
            outs.append(mm(att, block_diagonal(proj_s[l, :, part(1, p)])))
        mixed = jnp.concatenate(outs, axis=1)
        centred = mixed - row_mean(mixed)
        rstd = lax.rsqrt(row_mean(centred * centred) + 1e-6)
        norm_o = centred * rstd
        norm_o_s[l] = norm_o
        rstd_o_s[l] = jnp.broadcast_to(rstd, (ROWS, 128))
        branch = (norm_o * proj_s[l, :, pl.ds(0, WIDTH)].astype(F32)).astype(BF)
        out_ref[l, 64:128, :] = branch
        acts = (acts + mm(branch, weights[l, :, pl.ds(4 * WIDTH, WIDTH)])).astype(BF).astype(F32)

    last = iota((ROWS, WIDTH), 0) == count[:, 0:1] - 1
    state = jnp.sum(jnp.where(last, acts, 0.0), axis=0, keepdims=True)
    for q in range(LAYERS):
        quarter = jnp.broadcast_to(state[:, 128 * q : 128 * q + 128], (16, 128))
        out_ref[q, 192:208, :] = jnp.concatenate([quarter] * 4, axis=1).astype(BF)
    seed = jnp.concatenate([cot_ref[q].astype(F32)[0:1] for q in range(LAYERS)], axis=1)
    cot = jnp.where(last, jnp.broadcast_to(seed, (ROWS, WIDTH)), 0.0).astype(BF)

    for l in reversed(range(LAYERS)):
        out_ref[l, 128:192, :] = cot
        d_branch = mm(cot, weights[l, :, pl.ds(4 * WIDTH, WIDTH)], NT).astype(BF).astype(F32)
        norm_o = norm_o_s[l]
        d_gate = (d_branch * norm_o).astype(BF)
        d_norm = d_branch * proj_s[l, :, pl.ds(0, WIDTH)].astype(F32)
        d_mixed = rstd_o_s[l][:, 0:1] * (d_norm - row_mean(d_norm) - norm_o * row_mean(d_norm * norm_o))
        d_mixed = d_mixed.astype(BF)
        d_value, d_query, d_key = [], [], []
        for p in range(PAIRS):
            d_out = d_mixed[:, 128 * p : 128 * p + 128]
            d_att = mm(d_out, block_diagonal(proj_s[l, :, part(1, p)]), NT).astype(BF).astype(F32)
            d_value.append(merge(mm(att_s[l, p], d_out, TN)))
            d_score = (d_att * datt_s[l, p]).astype(BF)
            d_query.append(mm(d_score, block_diagonal(proj_s[l, :, part(3, p)])))
            d_key.append(merge(mm(d_score, proj_s[l, :, part(2, p)], TN)))
        d_normed = jnp.zeros((ROWS, WIDTH), F32)
        for kind, pieces in enumerate(([d_gate], d_value, d_query, d_key)):
            cols = pl.ds(kind * WIDTH, WIDTH)
            whole = pieces[0] if len(pieces) == 1 else jnp.concatenate(pieces, axis=1)
            d_pre = whole.astype(BF).astype(F32) * dsilu_s[l, :, cols]
            d_normed = d_normed + mm(d_pre.astype(BF), weights[l, :, cols], NT)
        d_normed = d_normed.astype(BF).astype(F32)
        normed = normed_s[l]
        d_in = rstd_s[l][:, 0:1] * (d_normed - row_mean(d_normed) - normed * row_mean(d_normed * normed))
        cot = (d_in + cot.astype(F32)).astype(BF)
        out_ref[l, 0:64, :] = cot


def gradient_kernel(own_rows, got_ref, grads_ref, keep_ref, send_ref):
    core = lax.axis_index("core")
    for t in range(LAYERS):
        grads_ref[t] = got_ref[t, 0:64, :]
    branch = jnp.concatenate([got_ref[t, 64:128, :] for t in range(LAYERS)], axis=0)
    cot = jnp.concatenate([got_ref[t, 128:192, :] for t in range(LAYERS)], axis=0)
    half = WIDTH // 2
    to, source = iota((WIDTH, WIDTH), 1), iota((WIDTH, WIDTH), 0)
    side = jnp.where(to < half, core, 1 - core)
    within = jnp.where(to < half, to, to - half)
    wanted = (within // own_rows) * (2 * own_rows) + side * own_rows + within % own_rows
    order = (source == wanted).astype(F32).astype(BF)
    ordered = mm(branch, order).astype(BF)
    keep_ref[...] = mm(ordered[:, :half], cot, TN)
    send_ref[0:half, :] = mm(ordered[:, half:], cot, TN).astype(BF)
    states = [got_ref[t, 192:208, 0:128] for t in range(LAYERS)]
    send_ref[half : half + 16, :] = jnp.concatenate(states, axis=1)


def packing_kernel(block_rows, own_rows, keep_ref, send_ref, got_ref, out_ref):
    half = WIDTH // 2
    core = lax.axis_index("core")
    total = (keep_ref[...] + got_ref[0:half, :].astype(F32)).astype(BF)
    rows = out_ref.shape[0]
    place, source = iota((rows, half), 0), iota((rows, half), 1)
    chip = whole_part(place, block_rows)
    within = place - chip * block_rows
    pick = (within < own_rows) & (source == chip * own_rows + within)
    laid = mm(pick.astype(F32).astype(BF), total)
    own = send_ref[half : half + 16, :].astype(F32)[0:1]
    other = got_ref[half : half + 16, :].astype(F32)[0:1]
    first = jnp.where(core == 0, own, other)
    second = jnp.where(core == 0, other, own)
    place = iota((rows, WIDTH), 0)
    at = place - whole_part(place, block_rows) * block_rows
    laid = laid + jnp.where(at == own_rows, first, 0.0) + jnp.where(at == own_rows + 1, second, 0.0)
    out_ref[...] = laid.astype(BF)


def result_kernel(block_rows, got_ref, hot_ref, served_ref, weight_ref):
    rows = got_ref.shape[0]
    out_rows = weight_ref.shape[0]
    lead = max(16, out_rows)
    place = iota((lead, rows), 1)
    within = place - whole_part(place, block_rows) * block_rows
    pick = ((within == iota((lead, rows), 0)) & (within < out_rows)).astype(F32).astype(BF)
    got = got_ref[...]
    weight_ref[...] = mm(pick, got)[0:out_rows]
    served = jnp.zeros((16, 128), F32)
    for h in range(DEV_HIST):
        served = served + mm(hot_ref[h], got[:, 128 * h : 128 * h + 128])
    served_ref[...] = served[0:SLOTS].astype(BF)


def shape(dims, dtype):
    return jax.ShapeDtypeStruct(dims, dtype)


def call(kernel, outs, scratch=(), in_specs=None, limit=48):
    specs = {} if in_specs is None else {"in_specs": in_specs}
    return pl.pallas_call(
        kernel,
        out_shape=outs,
        scratch_shapes=scratch,
        **specs,
        compiler_params=pltpu.CompilerParams(vmem_limit_bytes=limit * 1024 * 1024),
    )


def body(events, lengths, balance_plan, routes, w_uvqk, w_out, rel_bias, state_cotangent):
    n_z, n_y, n_core = (lax.axis_size(a) for a in DP)
    n_dp = n_z * n_y * n_core
    chips = n_z * n_y
    core = lax.axis_index("core")
    own_rows = WIDTH // n_dp
    block_rows = own_rows + 2
    half = WIDTH // 2

    with jax.named_scope("section_weights"):
        even, odd = rel_bias[0, 0::2], rel_bias[0, 1::2]
        base = jnp.concatenate([even[:, 0:1], odd[:, ::-1], even[:, :0:-1]], axis=1)
        high = lax.reduce_precision(base, 8, 7)
        middle = lax.reduce_precision(base - high, 8, 7)
        low = base - high - middle
        table = jnp.concatenate([a.astype(BF) for a in (high, middle, low)])
        table = jnp.pad(table, ((0, 4), (0, 5 * WIDTH - 128)))
        w_in = lax.dynamic_slice_in_dim(w_uvqk[0], core * half, half, 0)
        w_back = lax.dynamic_slice_in_dim(w_out[0], core * half, half, 0)
        mine = jnp.concatenate([jnp.concatenate([w_in, w_back], axis=1), table])
        gathered = lax.all_gather(mine, ("segment", "core"))
        gathered = gathered.reshape(LAYERS, 2, half + 16, 5 * WIDTH)

    with jax.named_scope("events"):
        partner_value = DEV_HIST + 2 * lax.axis_index("segment") - wanted_value()
        chosen = (balance_plan == partner_value)[:, None, None]
        outgoing = jnp.sum(jnp.where(chosen, events, jnp.zeros((), BF)), axis=0, dtype=BF)
        other_events = lax.ppermute(outgoing, "z", [(i, (i + n_z // 2) % n_z) for i in range(n_z)])

    with jax.named_scope("routing"):
        facts = jnp.concatenate([routes[:, 0], balance_plan, lengths, jnp.zeros((116,), jnp.int32)])
        facts = jnp.concatenate([state_cotangent[0].reshape(SLOTS * 128), facts.astype(BF)])
        facts = jnp.broadcast_to(facts[None], (n_dp, (SLOTS + 1) * 128))
        facts = lax.all_to_all(facts, DP, 0, 0, tiled=True)
        seeds, hot, count = call(
            functools.partial(routing_kernel, block_rows, own_rows),
            (
                shape((LAYERS, 16, 128), BF),
                shape((DEV_HIST, 16, chips * block_rows), BF),
                shape((ROWS, 128), jnp.int32),
            ),
        )(facts)
        seeds = lax.all_to_all(seeds, "segment", 0, 0, tiled=True)

    any_spec, vmem = pl.BlockSpec(memory_space=pl.ANY), pl.BlockSpec(memory_space=pltpu.VMEM)
    with jax.named_scope("layers"):
        message = call(
            layers_kernel,
            shape((LAYERS, MSG, WIDTH), BF),
            scratch=[
                pltpu.VMEM((LAYERS, WIDTH, 5 * WIDTH), BF),
                pltpu.VMEM((LAYERS, 16, 128), BF),
                pltpu.VMEM((LAYERS, ROWS, 4 * WIDTH), BF),
                pltpu.VMEM((LAYERS, ROWS, 4 * WIDTH), F32),
                pltpu.VMEM((LAYERS, ROWS, WIDTH), F32),
                pltpu.VMEM((LAYERS, ROWS, 128), F32),
                pltpu.VMEM((LAYERS, ROWS, WIDTH), F32),
                pltpu.VMEM((LAYERS, ROWS, 128), F32),
                pltpu.VMEM((LAYERS, PAIRS, ROWS, 128), F32),
                pltpu.VMEM((LAYERS, PAIRS, ROWS, 128), BF),
                pltpu.VMEM((LAYERS, PAIRS, ROWS, 128), F32),
                pltpu.SemaphoreType.DMA((LAYERS, 2)),
                pltpu.SemaphoreType.DMA((LAYERS,)),
            ],
            in_specs=[pl.BlockSpec(memory_space=pltpu.SMEM)] + [vmem] * 4 + [any_spec],
        )(balance_plan, events, other_events, count, seeds, gathered)

    with jax.named_scope("section_exchange"):
        arrived = lax.all_to_all(message, "segment", 0, 0, tiled=True)
    swap = [(0, 1), (1, 0)]
    with jax.named_scope("weight_gradient"):
        grads, keep, send = call(
            functools.partial(gradient_kernel, own_rows),
            (
                shape((LAYERS, ROWS, WIDTH), BF),
                shape((half, WIDTH), F32),
                shape((half + 16, WIDTH), BF),
            ),
        )(arrived)
        partner = lax.ppermute(send, "core", swap)
        blocks = call(
            functools.partial(packing_kernel, block_rows, own_rows),
            shape((chips * block_rows, WIDTH), BF),
        )(keep, send, partner)
        blocks = lax.all_to_all(
            blocks.reshape(chips, block_rows, WIDTH), ("z", "y"), 0, 0, tiled=True
        )
        served, weight = call(
            functools.partial(result_kernel, block_rows),
            (shape((SLOTS, 128), BF), shape((own_rows, WIDTH), F32)),
        )(blocks.reshape(chips * block_rows, WIDTH), hot)
    return served[None], grads[None], weight[None]


def solution(mesh):
    devices = mesh.devices
    n_segment, n_dp = devices.shape
    side = 1
    while side * side * 2 < n_dp:
        side *= 2
    fine = Mesh(
        devices.reshape(n_segment, n_dp // (2 * side), side, 2), ("segment",) + DP
    )
    return jax.shard_map(
        body,
        mesh=fine,
        in_specs=(
            P(DP, None, None),
            P(DP),
            P(DP),
            P(DP, None),
            P("segment", None, None),
            P("segment", None, None),
            P("segment", None, None),
            P(DP, None, "segment"),
        ),
        out_specs=(
            P(DP, None, "segment"),
            P("segment", DP, None, None),
            P("segment", DP, None),
        ),
        check_vma=False,
    )
```

```python
import functools

import jax
import jax.numpy as jnp
from jax import lax
from jax.experimental import pallas as pl
from jax.experimental.pallas import tpu as pltpu
from jax.sharding import Mesh, PartitionSpec as P

BF = jnp.bfloat16
F32 = jnp.float32
DP = ("z", "y", "core")
DEV_HIST = 4
ROWS = 64
WIDTH = 512
HEAD_COLS = 64
PAIRS = 4
LAYERS = 4
SLOTS = 8
MSG = 208
NN = (((1,), (0,)), ((), ()))
NT = (((1,), (1,)), ((), ()))
TN = (((0,), (0,)), ((), ()))


def mm(a, b, dims=NN):
    return lax.dot_general(a, b, dims, preferred_element_type=F32)


def iota(shape, dim):
    return lax.broadcasted_iota(jnp.int32, shape, dim)


def row_mean(a):
    return jnp.mean(a, axis=-1, keepdims=True)


def sigmoid(a):
    return 0.5 * jnp.tanh(0.5 * a) + 0.5


def dp_place():
    ny, nc = lax.axis_size("y"), lax.axis_size("core")
    return (lax.axis_index("z") * ny + lax.axis_index("y")) * nc + lax.axis_index("core")


def wanted_value():
    upper = (lax.axis_index("z") >= lax.axis_size("z") // 2).astype(jnp.int32)
    return upper * DEV_HIST + lax.axis_index("segment")


def packing_start(
    plan_ref, routes_ref, lengths_ref, w_in_ref, w_out_ref, events_ref, bias_ref, cot_ref,
    first_ref, second_ref, outgoing_ref, facts_ref,
    table, sems,
):
    core = lax.axis_index("core")
    half = WIDTH // 2
    copies = []
    for side, dest in ((core, first_ref), (1 - core, second_ref)):
        rows = pl.ds(pl.multiple_of(side * half, half), half)
        copies.append((w_in_ref.at[0, rows], dest.at[pl.ds(0, half), pl.ds(0, 4 * WIDTH)]))
        copies.append((w_out_ref.at[0, rows], dest.at[pl.ds(0, half), pl.ds(4 * WIDTH, WIDTH)]))
    partner_value = DEV_HIST + 2 * lax.axis_index("segment") - wanted_value()
    chosen = jnp.int32(0)
    for h in range(DEV_HIST):
        chosen = chosen + jnp.where(plan_ref[h] == partner_value, h, 0)
    copies.append((events_ref.at[chosen], outgoing_ref))
    copies = [pltpu.make_async_copy(*c, sems.at[n]) for n, c in enumerate(copies)]
    for c in copies:
        c.start()

    bias = bias_ref[0]
    high = bias.astype(BF).astype(F32)
    middle = (bias - high).astype(BF).astype(F32)
    low = bias - high - middle
    pieces = jnp.concatenate([high, middle, low, jnp.zeros((8, ROWS), F32)]).astype(BF)
    row, head = iota((16, 32), 0), iota((16, 32), 1)
    even = (row // 4) * 8 + 2 * (row % 4)
    used = row < 12
    pick_even = (used & (head == even)).astype(F32).astype(BF)
    pick_odd = (used & (head == even + 1)).astype(F32).astype(BF)
    distance, place = iota((ROWS, 128), 0), iota((ROWS, 128), 1)
    to_even = (place == (128 - distance) % 128).astype(F32).astype(BF)
    to_odd = (place == ROWS - distance).astype(F32).astype(BF)
    base = mm(mm(pick_even, pieces).astype(BF), to_even) + mm(mm(pick_odd, pieces).astype(BF), to_odd)
    table[...] = base.astype(BF)
    copy = pltpu.make_async_copy(table, first_ref.at[pl.ds(half, 16), pl.ds(0, 128)], sems.at[len(copies)])
    copy.start()

    lane = iota((1, 128), 1)
    facts = jnp.zeros((1, 128), F32)
    for j, ref in enumerate((routes_ref, plan_ref, lengths_ref)):
        for h in range(DEV_HIST):
            facts = jnp.where(lane == 4 * j + h, ref[h].astype(F32), facts)
    cot = cot_ref[0].astype(F32)
    blocks = [cot[k : k + 1] for k in range(SLOTS)] + [facts, jnp.zeros((1, 128), F32)]
    lines = [jnp.concatenate(blocks[k : k + 5], axis=1) for k in (0, 5)]
    facts_ref[...] = jnp.broadcast_to(jnp.concatenate(lines).astype(BF)[None], facts_ref.shape)
    for c in copies:
        c.wait()
    copy.wait()


def whole_part(a, d):
    if d & (d - 1) == 0:
        return a // d
    return jnp.floor((a.astype(F32) + 0.5) * (1.0 / d)).astype(jnp.int32)


def routing_kernel(block_rows, own_rows, table_ref, seeds_ref, hot_ref, count_ref):
    n_dp = table_ref.shape[0]
    hist = n_dp * DEV_HIST
    me = dp_place()
    facts = table_ref[:, SLOTS * 128 : SLOTS * 128 + 128]
    spread = mm(facts, (iota((128, hist), 0) == iota((128, hist), 1) % DEV_HIST).astype(F32).astype(BF))
    own = iota((n_dp, hist), 1) // DEV_HIST == iota((n_dp, hist), 0)
    routes = jnp.sum(jnp.where(own, spread, 0.0), axis=0, keepdims=True)

    routes_wide = jnp.broadcast_to(routes, (16, hist))
    history, mine = iota((16, hist), 1), me * DEV_HIST + iota((16, hist), 0)
    route = jnp.sum(jnp.where(history == mine, routes_wide, 0.0), axis=1, keepdims=True)
    before = (routes_wide == route) & (history < mine)
    slot = jnp.sum(before.astype(F32), axis=1, keepdims=True)
    source = iota((16, n_dp), 1).astype(F32)
    seeds = jnp.zeros((16, 128), F32)
    for k in range(SLOTS):
        pick = jnp.where((source == route) & (slot == float(k)), 1.0, 0.0).astype(BF)
        seeds = seeds + mm(pick, table_ref[:, 128 * k : 128 * k + 128])
    for q in range(LAYERS):
        seeds_ref[q] = jnp.broadcast_to(seeds[q : q + 1], (16, 128)).astype(BF)

    hit = jnp.broadcast_to((routes == me.astype(F32)).astype(F32), (16, hist))
    earlier = (iota((hist, hist), 0) < iota((hist, hist), 1)).astype(F32).astype(BF)
    place_of = mm(hit.astype(BF), earlier)
    hot = jnp.where(place_of == iota((16, hist), 0).astype(F32), hit, 0.0).astype(BF)
    total = hot_ref.shape[2]
    place, history = iota((hist, total), 1), iota((hist, total), 0)
    chip = whole_part(place, block_rows)
    within = place - chip * block_rows - own_rows
    first = (chip * 2 + within) * DEV_HIST
    valid = (within >= 0) & (within < 2)
    for h in range(DEV_HIST):
        move = jnp.where(valid & (history == first + h), 1.0, 0.0).astype(BF)
        hot_ref[h] = mm(hot, move).astype(BF)

    other = lax.rem(me + n_dp // 2, n_dp)
    known = facts.astype(F32)
    ahead = pltpu.roll(known, 124, 1)
    row, lane = iota((n_dp, 128), 0), iota((n_dp, 128), 1)
    fits = ((row == me) | (row == other)) & (lane >= 4) & (lane < 8)
    fits = fits & (known == wanted_value().astype(F32))
    length = jnp.sum(jnp.where(fits, ahead, 0.0), axis=1, keepdims=True)
    length = jnp.sum(length, axis=0, keepdims=True)
    count_ref[...] = jnp.broadcast_to(length, count_ref.shape).astype(jnp.int32)


def layers_kernel(
    plan_ref, events_ref, other_ref, count_ref, cot_ref,
    first, second, near_a, near_b, swap_a, swap_b, far_a, far_b,
    out_ref,
    weights, tables, proj_s, dsilu_s, normed_s, rstd_s, norm_o_s, rstd_o_s, bias_s, att_s, datt_s, sems, table_sem,
):
    half = WIDTH // 2
    segment, core = lax.axis_index("segment"), lax.axis_index("core")
    near = lax.rem(segment + 1 + 2 * core, LAYERS)
    swap = lax.rem(segment + 3 + 2 * core, LAYERS)
    far = lax.rem(segment + 2, LAYERS)
    for piece, l in ((first, segment), (near_a, near), (swap_a, swap), (far_a, far)):
        pltpu.make_async_copy(
            piece.at[pl.ds(half, 16), pl.ds(0, 128)], tables.at[l], table_sem.at[l]
        ).start()
    for piece, l, side in (
        (first, segment, core), (second, segment, 1 - core), (near_a, near, core), (near_b, near, 1 - core),
        (swap_a, swap, 1 - core), (swap_b, swap, core), (far_a, far, core), (far_b, far, 1 - core),
    ):
        rows = pl.ds(pl.multiple_of(side * half, half), half)
        pltpu.make_async_copy(piece.at[pl.ds(0, half)], weights.at[l, rows], sems.at[l, side]).start()

    lane, row = iota((ROWS, 128), 1), iota((ROWS, 128), 0)
    left = (lane < HEAD_COLS).astype(F32)
    left_b, right_b = left.astype(BF), (1.0 - left).astype(BF)
    column = jnp.where(lane < HEAD_COLS, lane, lane - HEAD_COLS)
    count = count_ref[...]
    allowed = (column <= row) & (column < count)

    for l in range(LAYERS):
        pltpu.make_async_copy(tables.at[l], tables.at[l], table_sem.at[l]).wait()
        table = tables[l].astype(F32)
        table = table[0:4] + table[4:8] + table[8:12]
        for p in range(PAIRS):
            wide = jnp.broadcast_to(table[p : p + 1], (ROWS, 128))
            bias_s[l, p] = pltpu.roll(wide, 0, 1, stride=1, stride_axis=0)

    def block_diagonal(a):
        return jnp.concatenate([a * left_b, a * right_b], axis=0)

    def merge(a):
        return jnp.where(lane < HEAD_COLS, a[:ROWS], a[ROWS:])

    def part(kind, p):
        return pl.ds(kind * WIDTH + p * 128, 128)

    value = wanted_value()
    found = jnp.int32(0)
    acts = jnp.zeros((ROWS, WIDTH), F32)
    for h in range(DEV_HIST):
        same = (plan_ref[h] == value).astype(jnp.int32)
        found = found + same
        acts = jnp.where(same == 1, events_ref[h].astype(F32), acts)
    acts = jnp.where(found > 0, acts, other_ref[...].astype(F32))

    for l in range(LAYERS):
        average = row_mean(acts)
        centred = acts - average
        rstd = lax.rsqrt(row_mean(centred * centred) + 1e-6)
        normed = centred * rstd
        normed_s[l] = normed
        rstd_s[l] = jnp.broadcast_to(rstd, (ROWS, 128))
        for c in range(2):
            piece = weights.at[l, pl.ds(c * half, half)]
            pltpu.make_async_copy(piece, piece, sems.at[l, c]).wait()
        normed_b = normed.astype(BF)
        for kind in range(4):
            cols = pl.ds(kind * WIDTH, WIDTH)
            pre = mm(normed_b, weights[l, :, cols])
            gated = sigmoid(pre)
            silu = pre * gated
            proj_s[l, :, cols] = silu.astype(BF)
            dsilu_s[l, :, cols] = gated + silu * (1.0 - gated)
        outs = []
        for p in range(PAIRS):
            keys = block_diagonal(proj_s[l, :, part(3, p)])
            score = mm(proj_s[l, :, part(2, p)], keys, NT) * 0.125 + bias_s[l, p]
            gated = sigmoid(score)
            silu = score * gated
            att = jnp.where(allowed, silu, 0.0).astype(BF)
            att_s[l, p] = att
            datt_s[l, p] = jnp.where(allowed, gated + silu * (1.0 - gated), 0.0) * 0.125
            outs.append(mm(att, block_diagonal(proj_s[l, :, part(1, p)])))
        mixed = jnp.concatenate(outs, axis=1)
        centred = mixed - row_mean(mixed)
        rstd = lax.rsqrt(row_mean(centred * centred) + 1e-6)
        norm_o = centred * rstd
        norm_o_s[l] = norm_o
        rstd_o_s[l] = jnp.broadcast_to(rstd, (ROWS, 128))
        branch = (norm_o * proj_s[l, :, pl.ds(0, WIDTH)].astype(F32)).astype(BF)
        out_ref[l, 64:128, :] = branch
        acts = (acts + mm(branch, weights[l, :, pl.ds(4 * WIDTH, WIDTH)])).astype(BF).astype(F32)

    last = iota((ROWS, WIDTH), 0) == count[:, 0:1] - 1
    state = jnp.sum(jnp.where(last, acts, 0.0), axis=0, keepdims=True)
    for q in range(LAYERS):
        quarter = jnp.broadcast_to(state[:, 128 * q : 128 * q + 128], (16, 128))
        out_ref[q, 192:208, :] = jnp.concatenate([quarter] * 4, axis=1).astype(BF)
    seed = jnp.concatenate([cot_ref[q].astype(F32)[0:1] for q in range(LAYERS)], axis=1)
    cot = jnp.where(last, jnp.broadcast_to(seed, (ROWS, WIDTH)), 0.0).astype(BF)

    for l in reversed(range(LAYERS)):
        out_ref[l, 128:192, :] = cot
        d_branch = mm(cot, weights[l, :, pl.ds(4 * WIDTH, WIDTH)], NT).astype(BF).astype(F32)
        norm_o = norm_o_s[l]
        d_gate = (d_branch * norm_o).astype(BF)
        d_norm = d_branch * proj_s[l, :, pl.ds(0, WIDTH)].astype(F32)
        d_mixed = rstd_o_s[l][:, 0:1] * (d_norm - row_mean(d_norm) - norm_o * row_mean(d_norm * norm_o))
        d_mixed = d_mixed.astype(BF)
        d_value, d_query, d_key = [], [], []
        for p in range(PAIRS):
            d_out = d_mixed[:, 128 * p : 128 * p + 128]
            d_att = mm(d_out, block_diagonal(proj_s[l, :, part(1, p)]), NT).astype(BF).astype(F32)
            d_value.append(merge(mm(att_s[l, p], d_out, TN)))
            d_score = (d_att * datt_s[l, p]).astype(BF)
            d_query.append(mm(d_score, block_diagonal(proj_s[l, :, part(3, p)])))
            d_key.append(merge(mm(d_score, proj_s[l, :, part(2, p)], TN)))
        d_normed = jnp.zeros((ROWS, WIDTH), F32)
        for kind, pieces in enumerate(([d_gate], d_value, d_query, d_key)):
            cols = pl.ds(kind * WIDTH, WIDTH)
            whole = pieces[0] if len(pieces) == 1 else jnp.concatenate(pieces, axis=1)
            d_pre = whole.astype(BF).astype(F32) * dsilu_s[l, :, cols]
            d_normed = d_normed + mm(d_pre.astype(BF), weights[l, :, cols], NT)
        d_normed = d_normed.astype(BF).astype(F32)
        normed = normed_s[l]
        d_in = rstd_s[l][:, 0:1] * (d_normed - row_mean(d_normed) - normed * row_mean(d_normed * normed))
        cot = (d_in + cot.astype(F32)).astype(BF)
        out_ref[l, 0:64, :] = cot


def gradient_kernel(own_rows, got_ref, grads_ref, keep_ref, send_ref):
    core = lax.axis_index("core")
    for t in range(LAYERS):
        grads_ref[t] = got_ref[t, 0:64, :]
    branch = jnp.concatenate([got_ref[t, 64:128, :] for t in range(LAYERS)], axis=0)
    cot = jnp.concatenate([got_ref[t, 128:192, :] for t in range(LAYERS)], axis=0)
    half = WIDTH // 2
    to, source = iota((WIDTH, WIDTH), 1), iota((WIDTH, WIDTH), 0)
    side = jnp.where(to < half, core, 1 - core)
    within = jnp.where(to < half, to, to - half)
    wanted = (within // own_rows) * (2 * own_rows) + side * own_rows + within % own_rows
    order = (source == wanted).astype(F32).astype(BF)
    ordered = mm(branch, order).astype(BF)
    keep_ref[...] = mm(ordered[:, :half], cot, TN)
    send_ref[0:half, :] = mm(ordered[:, half:], cot, TN).astype(BF)
    states = [got_ref[t, 192:208, 0:128] for t in range(LAYERS)]
    send_ref[half : half + 16, :] = jnp.concatenate(states, axis=1)


def packing_kernel(block_rows, own_rows, keep_ref, send_ref, got_ref, out_ref):
    half = WIDTH // 2
    core = lax.axis_index("core")
    total = (keep_ref[...] + got_ref[0:half, :].astype(F32)).astype(BF)
    rows = out_ref.shape[0]
    place, source = iota((rows, half), 0), iota((rows, half), 1)
    chip = whole_part(place, block_rows)
    within = place - chip * block_rows
    pick = (within < own_rows) & (source == chip * own_rows + within)
    laid = mm(pick.astype(F32).astype(BF), total)
    own = send_ref[half : half + 16, :].astype(F32)[0:1]
    other = got_ref[half : half + 16, :].astype(F32)[0:1]
    first = jnp.where(core == 0, own, other)
    second = jnp.where(core == 0, other, own)
    place = iota((rows, WIDTH), 0)
    at = place - whole_part(place, block_rows) * block_rows
    laid = laid + jnp.where(at == own_rows, first, 0.0) + jnp.where(at == own_rows + 1, second, 0.0)
    out_ref[...] = laid.astype(BF)


def result_kernel(block_rows, got_ref, hot_ref, served_ref, weight_ref):
    rows = got_ref.shape[0]
    out_rows = weight_ref.shape[0]
    lead = max(16, out_rows)
    place = iota((lead, rows), 1)
    within = place - whole_part(place, block_rows) * block_rows
    pick = ((within == iota((lead, rows), 0)) & (within < out_rows)).astype(F32).astype(BF)
    got = got_ref[...]
    weight_ref[...] = mm(pick, got)[0:out_rows]
    served = jnp.zeros((16, 128), F32)
    for h in range(DEV_HIST):
        served = served + mm(hot_ref[h], got[:, 128 * h : 128 * h + 128])
    served_ref[...] = served[0:SLOTS].astype(BF)


def shape(dims, dtype):
    return jax.ShapeDtypeStruct(dims, dtype)


def call(kernel, outs, scratch=(), in_specs=None, out_specs=None, limit=48):
    specs = {} if in_specs is None else {"in_specs": in_specs}
    specs |= {} if out_specs is None else {"out_specs": out_specs}
    return pl.pallas_call(
        kernel,
        out_shape=outs,
        scratch_shapes=scratch,
        **specs,
        compiler_params=pltpu.CompilerParams(vmem_limit_bytes=limit * 1024 * 1024),
    )


def body(events, lengths, balance_plan, routes, w_uvqk, w_out, rel_bias, state_cotangent):
    n_z, n_y, n_core = (lax.axis_size(a) for a in DP)
    n_dp = n_z * n_y * n_core
    chips = n_z * n_y
    own_rows = WIDTH // n_dp
    block_rows = own_rows + 2
    half = WIDTH // 2

    any_spec, vmem = pl.BlockSpec(memory_space=pl.ANY), pl.BlockSpec(memory_space=pltpu.VMEM)
    smem = pl.BlockSpec(memory_space=pltpu.SMEM)
    with jax.named_scope("packing"):
        first, second, outgoing, facts = call(
            packing_start,
            (
                shape((half + 16, 5 * WIDTH), BF),
                shape((half, 5 * WIDTH), BF),
                shape((ROWS, WIDTH), BF),
                shape((n_dp, 2, (SLOTS + 2) * 64), BF),
            ),
            scratch=[pltpu.VMEM((16, 128), BF), pltpu.SemaphoreType.DMA((6,))],
            in_specs=[smem] * 3 + [any_spec] * 3 + [vmem] * 2,
            out_specs=(any_spec, any_spec, any_spec, vmem),
        )(balance_plan, routes.reshape(DEV_HIST), lengths, w_uvqk, w_out, events, rel_bias, state_cotangent)

    with jax.named_scope("section_weights"):
        ring = [(s * 2, (s - 1) % LAYERS * 2) for s in range(LAYERS)]
        ring += [(s * 2 + 1, (s + 1) % LAYERS * 2 + 1) for s in range(LAYERS)]
        swap = [(0, 1), (1, 0)]
        near_a = lax.ppermute(first, ("segment", "core"), ring)
        near_b = lax.ppermute(second, ("segment", "core"), ring)

    with jax.named_scope("events"):
        other_events = lax.ppermute(outgoing, "z", [(i, (i + n_z // 2) % n_z) for i in range(n_z)])

    with jax.named_scope("routing"):
        facts = lax.all_to_all(facts, DP, 0, 0, tiled=True)
        near_a, near_b, facts = lax.optimization_barrier((near_a, near_b, facts))
        facts = facts.reshape(n_dp, (SLOTS + 2) * 128)

    with jax.named_scope("section_weights"):
        far_a = lax.ppermute(near_a, ("segment", "core"), ring)
        swap_a = lax.ppermute(near_a, "core", swap)
        swap_b = lax.ppermute(near_b, "core", swap)

    with jax.named_scope("routing"):
        seeds, hot, count = call(
            functools.partial(routing_kernel, block_rows, own_rows),
            (
                shape((LAYERS, 16, 128), BF),
                shape((DEV_HIST, 16, chips * block_rows), BF),
                shape((ROWS, 128), jnp.int32),
            ),
        )(facts)
        seeds = lax.all_to_all(seeds, "segment", 0, 0, tiled=True)
        far_a, swap_a, swap_b, seeds, other_events = lax.optimization_barrier(
            (far_a, swap_a, swap_b, seeds, other_events)
        )
    with jax.named_scope("section_weights"):
        far_b = lax.ppermute(far_a, "core", swap)

    with jax.named_scope("layers"):
        message = call(
            layers_kernel,
            shape((LAYERS, MSG, WIDTH), BF),
            scratch=[
                pltpu.VMEM((LAYERS, WIDTH, 5 * WIDTH), BF),
                pltpu.VMEM((LAYERS, 16, 128), BF),
                pltpu.VMEM((LAYERS, ROWS, 4 * WIDTH), BF),
                pltpu.VMEM((LAYERS, ROWS, 4 * WIDTH), F32),
                pltpu.VMEM((LAYERS, ROWS, WIDTH), F32),
                pltpu.VMEM((LAYERS, ROWS, 128), F32),
                pltpu.VMEM((LAYERS, ROWS, WIDTH), F32),
                pltpu.VMEM((LAYERS, ROWS, 128), F32),
                pltpu.VMEM((LAYERS, PAIRS, ROWS, 128), F32),
                pltpu.VMEM((LAYERS, PAIRS, ROWS, 128), BF),
                pltpu.VMEM((LAYERS, PAIRS, ROWS, 128), F32),
                pltpu.SemaphoreType.DMA((LAYERS, 2)),
                pltpu.SemaphoreType.DMA((LAYERS,)),
            ],
            in_specs=[smem] + [vmem] * 4 + [any_spec] * 8,
        )(
            balance_plan, events, other_events, count, seeds,
            first, second, near_a, near_b, swap_a, swap_b, far_a, far_b,
        )

    with jax.named_scope("section_exchange"):
        arrived = lax.all_to_all(message, "segment", 0, 0, tiled=True)
    with jax.named_scope("weight_gradient"):
        grads, keep, send = call(
            functools.partial(gradient_kernel, own_rows),
            (
                shape((LAYERS, ROWS, WIDTH), BF),
                shape((half, WIDTH), F32),
                shape((half + 16, WIDTH), BF),
            ),
        )(arrived)
        partner = lax.ppermute(send, "core", swap)
        blocks = call(
            functools.partial(packing_kernel, block_rows, own_rows),
            shape((chips * block_rows, WIDTH), BF),
        )(keep, send, partner)
        blocks = lax.all_to_all(
            blocks.reshape(chips, block_rows, WIDTH), ("z", "y"), 0, 0, tiled=True
        )
        served, weight = call(
            functools.partial(result_kernel, block_rows),
            (shape((SLOTS, 128), BF), shape((own_rows, WIDTH), F32)),
        )(blocks.reshape(chips * block_rows, WIDTH), hot)
    return served[None], grads[None], weight[None]


def solution(mesh):
    devices = mesh.devices
    n_segment, n_dp = devices.shape
    side = 1
    while side * side * 2 < n_dp:
        side *= 2
    fine = Mesh(
        devices.reshape(n_segment, n_dp // (2 * side), side, 2), ("segment",) + DP
    )
    return jax.shard_map(
        body,
        mesh=fine,
        in_specs=(
            P(DP, None, None),
            P(DP),
            P(DP),
            P(DP, None),
            P("segment", None, None),
            P("segment", None, None),
            P("segment", None, None),
            P(DP, None, "segment"),
        ),
        out_specs=(
            P(DP, None, "segment"),
            P("segment", DP, None, None),
            P("segment", DP, None),
        ),
        check_vma=False,
    )
```

```python
import functools

import jax
import jax.numpy as jnp
from jax import lax
from jax.experimental import pallas as pl
from jax.experimental.pallas import tpu as pltpu
from jax.sharding import Mesh, PartitionSpec as P

BF = jnp.bfloat16
F32 = jnp.float32
DP = ("z", "y", "core")
DEV_HIST = 4
ROWS = 64
WIDTH = 512
HEAD_COLS = 64
PAIRS = 4
LAYERS = 4
SLOTS = 8
MSG = 208
NN = (((1,), (0,)), ((), ()))
NT = (((1,), (1,)), ((), ()))
TN = (((0,), (0,)), ((), ()))


def mm(a, b, dims=NN):
    return lax.dot_general(a, b, dims, preferred_element_type=F32)


def iota(shape, dim):
    return lax.broadcasted_iota(jnp.int32, shape, dim)


def row_mean(a):
    return jnp.mean(a, axis=-1, keepdims=True)


def sigmoid(a):
    return 0.5 * jnp.tanh(0.5 * a) + 0.5


def dp_place():
    ny, nc = lax.axis_size("y"), lax.axis_size("core")
    return (lax.axis_index("z") * ny + lax.axis_index("y")) * nc + lax.axis_index("core")


def wanted_value():
    upper = (lax.axis_index("z") >= lax.axis_size("z") // 2).astype(jnp.int32)
    return upper * DEV_HIST + lax.axis_index("segment")


def packing_start(
    plan_ref, routes_ref, lengths_ref, w_in_ref, w_out_ref, events_ref, bias_ref, cot_ref,
    first_ref, second_ref, outgoing_ref, facts_ref,
    plan, routes, lengths, bias_s, cot_s, table, sems,
):
    core = lax.axis_index("core")
    half = WIDTH // 2
    small = [(plan_ref, plan), (routes_ref, routes), (lengths_ref, lengths), (bias_ref.at[0], bias_s), (cot_ref.at[0], cot_s)]
    small = [pltpu.make_async_copy(*c, sems.at[n]) for n, c in enumerate(small)]
    for c in small:
        c.start()
    copies = []
    for side, dest in ((core, first_ref), (1 - core, second_ref)):
        for part in range(2):
            rows = pl.ds(pl.multiple_of(side * half + part * (half // 2), half // 2), half // 2)
            to = pl.ds(part * (half // 2), half // 2)
            copies.append((w_in_ref.at[0, rows], dest.at[to, pl.ds(0, 4 * WIDTH)]))
            copies.append((w_out_ref.at[0, rows], dest.at[to, pl.ds(4 * WIDTH, WIDTH)]))
    copies = [pltpu.make_async_copy(*c, sems.at[len(small) + n]) for n, c in enumerate(copies)]
    for c in copies:
        c.start()
    for c in small:
        c.wait()
    partner_value = DEV_HIST + 2 * lax.axis_index("segment") - wanted_value()
    chosen = jnp.int32(0)
    for h in range(DEV_HIST):
        chosen = chosen + jnp.where(plan[h] == partner_value, h, 0)
    copies.append(pltpu.make_async_copy(events_ref.at[chosen], outgoing_ref, sems.at[len(small) + len(copies)]))
    copies[-1].start()

    bias = bias_s[...]
    high = bias.astype(BF).astype(F32)
    middle = (bias - high).astype(BF).astype(F32)
    low = bias - high - middle
    pieces = jnp.concatenate([high, middle, low, jnp.zeros((8, ROWS), F32)]).astype(BF)
    row, head = iota((16, 32), 0), iota((16, 32), 1)
    even = (row // 4) * 8 + 2 * (row % 4)
    used = row < 12
    pick_even = (used & (head == even)).astype(F32).astype(BF)
    pick_odd = (used & (head == even + 1)).astype(F32).astype(BF)
    distance, place = iota((ROWS, 128), 0), iota((ROWS, 128), 1)
    to_even = (place == (128 - distance) % 128).astype(F32).astype(BF)
    to_odd = (place == ROWS - distance).astype(F32).astype(BF)
    base = mm(mm(pick_even, pieces).astype(BF), to_even) + mm(mm(pick_odd, pieces).astype(BF), to_odd)
    table[...] = base.astype(BF)
    copy = pltpu.make_async_copy(table, first_ref.at[pl.ds(half, 16), pl.ds(0, 128)], sems.at[len(small) + len(copies)])
    copy.start()

    lane = iota((1, 128), 1)
    facts = jnp.zeros((1, 128), F32)
    for j, ref in enumerate((routes, plan, lengths)):
        for h in range(DEV_HIST):
            facts = jnp.where(lane == 4 * j + h, ref[h].astype(F32), facts)
    cot = cot_s[...].astype(F32)
    blocks = [cot[k : k + 1] for k in range(SLOTS)] + [facts, jnp.zeros((1, 128), F32)]
    lines = [jnp.concatenate(blocks[k : k + 5], axis=1) for k in (0, 5)]
    facts_ref[...] = jnp.broadcast_to(jnp.concatenate(lines).astype(BF)[None], facts_ref.shape)
    for c in copies:
        c.wait()
    copy.wait()


def whole_part(a, d):
    if d & (d - 1) == 0:
        return a // d
    return jnp.floor((a.astype(F32) + 0.5) * (1.0 / d)).astype(jnp.int32)


def routing_kernel(block_rows, own_rows, table_ref, seeds_ref, hot_ref, count_ref):
    n_dp = table_ref.shape[0]
    hist = n_dp * DEV_HIST
    me = dp_place()
    facts = table_ref[:, SLOTS * 128 : SLOTS * 128 + 128]
    spread = mm(facts, (iota((128, hist), 0) == iota((128, hist), 1) % DEV_HIST).astype(F32).astype(BF))
    own = iota((n_dp, hist), 1) // DEV_HIST == iota((n_dp, hist), 0)
    routes = jnp.sum(jnp.where(own, spread, 0.0), axis=0, keepdims=True)

    routes_wide = jnp.broadcast_to(routes, (16, hist))
    history, mine = iota((16, hist), 1), me * DEV_HIST + iota((16, hist), 0)
    route = jnp.sum(jnp.where(history == mine, routes_wide, 0.0), axis=1, keepdims=True)
    before = (routes_wide == route) & (history < mine)
    slot = jnp.sum(before.astype(F32), axis=1, keepdims=True)
    source = iota((16, n_dp), 1).astype(F32)
    seeds = jnp.zeros((16, 128), F32)
    for k in range(SLOTS):
        pick = jnp.where((source == route) & (slot == float(k)), 1.0, 0.0).astype(BF)
        seeds = seeds + mm(pick, table_ref[:, 128 * k : 128 * k + 128])
    for q in range(LAYERS):
        seeds_ref[q] = jnp.broadcast_to(seeds[q : q + 1], (16, 128)).astype(BF)

    hit = jnp.broadcast_to((routes == me.astype(F32)).astype(F32), (16, hist))
    earlier = (iota((hist, hist), 0) < iota((hist, hist), 1)).astype(F32).astype(BF)
    place_of = mm(hit.astype(BF), earlier)
    hot = jnp.where(place_of == iota((16, hist), 0).astype(F32), hit, 0.0).astype(BF)
    total = hot_ref.shape[2]
    place, history = iota((hist, total), 1), iota((hist, total), 0)
    chip = whole_part(place, block_rows)
    within = place - chip * block_rows - own_rows
    first = (chip * 2 + within) * DEV_HIST
    valid = (within >= 0) & (within < 2)
    for h in range(DEV_HIST):
        move = jnp.where(valid & (history == first + h), 1.0, 0.0).astype(BF)
        hot_ref[h] = mm(hot, move).astype(BF)

    other = lax.rem(me + n_dp // 2, n_dp)
    known = facts.astype(F32)
    ahead = pltpu.roll(known, 124, 1)
    row, lane = iota((n_dp, 128), 0), iota((n_dp, 128), 1)
    fits = ((row == me) | (row == other)) & (lane >= 4) & (lane < 8)
    fits = fits & (known == wanted_value().astype(F32))
    length = jnp.sum(jnp.where(fits, ahead, 0.0), axis=1, keepdims=True)
    length = jnp.sum(length, axis=0, keepdims=True)
    count_ref[...] = jnp.broadcast_to(length, count_ref.shape).astype(jnp.int32)


def layers_kernel(
    plan_ref, events_ref, other_ref, count_ref, cot_ref,
    first, second, near_a, near_b, swap_a, swap_b, far_a, far_b,
    out_ref,
    weights, tables, proj_s, dsilu_s, normed_s, rstd_s, norm_o_s, rstd_o_s, bias_s, att_s, datt_s, sems, table_sem,
):
    half = WIDTH // 2
    segment, core = lax.axis_index("segment"), lax.axis_index("core")
    near = lax.rem(segment + 1 + 2 * core, LAYERS)
    swap = lax.rem(segment + 3 + 2 * core, LAYERS)
    far = lax.rem(segment + 2, LAYERS)
    held = (
        (segment, first, core, second, 1 - core),
        (near, near_a, core, near_b, 1 - core),
        (swap, swap_a, 1 - core, swap_b, core),
        (far, far_a, core, far_b, 1 - core),
    )
    for l in range(LAYERS):
        for slot, one, side, two, other_side in held:

            @pl.when(slot == l)
            def _():
                pltpu.make_async_copy(
                    one.at[pl.ds(half, 16), pl.ds(0, 128)], tables.at[l], table_sem.at[l]
                ).start()
                for piece, at in ((one, side), (two, other_side)):
                    rows = pl.ds(pl.multiple_of(at * half, half), half)
                    pltpu.make_async_copy(piece.at[pl.ds(0, half)], weights.at[l, rows], sems.at[l, at]).start()

    lane, row = iota((ROWS, 128), 1), iota((ROWS, 128), 0)
    left = (lane < HEAD_COLS).astype(F32)
    left_b, right_b = left.astype(BF), (1.0 - left).astype(BF)
    column = jnp.where(lane < HEAD_COLS, lane, lane - HEAD_COLS)
    count = count_ref[...]
    allowed = (column <= row) & (column < count)

    def block_diagonal(a):
        return jnp.concatenate([a * left_b, a * right_b], axis=0)

    def merge(a):
        return jnp.where(lane < HEAD_COLS, a[:ROWS], a[ROWS:])

    def part(kind, p):
        return pl.ds(kind * WIDTH + p * 128, 128)

    value = wanted_value()
    found = jnp.int32(0)
    acts = jnp.zeros((ROWS, WIDTH), F32)
    for h in range(DEV_HIST):
        same = (plan_ref[h] == value).astype(jnp.int32)
        found = found + same
        acts = jnp.where(same == 1, events_ref[h].astype(F32), acts)
    acts = jnp.where(found > 0, acts, other_ref[...].astype(F32))

    for l in range(LAYERS):
        average = row_mean(acts)
        centred = acts - average
        rstd = lax.rsqrt(row_mean(centred * centred) + 1e-6)
        normed = centred * rstd
        normed_s[l] = normed
        rstd_s[l] = jnp.broadcast_to(rstd, (ROWS, 128))
        for c in range(2):
            piece = weights.at[l, pl.ds(c * half, half)]
            pltpu.make_async_copy(piece, piece, sems.at[l, c]).wait()
        pltpu.make_async_copy(tables.at[l], tables.at[l], table_sem.at[l]).wait()
        table = tables[l].astype(F32)
        table = table[0:4] + table[4:8] + table[8:12]
        for p in range(PAIRS):
            wide = jnp.broadcast_to(table[p : p + 1], (ROWS, 128))
            bias_s[l, p] = pltpu.roll(wide, 0, 1, stride=1, stride_axis=0)
        normed_b = normed.astype(BF)
        for kind in range(4):
            cols = pl.ds(kind * WIDTH, WIDTH)
            pre = mm(normed_b, weights[l, :, cols])
            gated = sigmoid(pre)
            silu = pre * gated
            proj_s[l, :, cols] = silu.astype(BF)
            dsilu_s[l, :, cols] = gated + silu * (1.0 - gated)
        outs = []
        for p in range(PAIRS):
            keys = block_diagonal(proj_s[l, :, part(3, p)])
            score = mm(proj_s[l, :, part(2, p)], keys, NT) * 0.125 + bias_s[l, p]
            gated = sigmoid(score)
            silu = score * gated
            att = jnp.where(allowed, silu, 0.0).astype(BF)
            att_s[l, p] = att
            datt_s[l, p] = jnp.where(allowed, gated + silu * (1.0 - gated), 0.0) * 0.125
            outs.append(mm(att, block_diagonal(proj_s[l, :, part(1, p)])))
        mixed = jnp.concatenate(outs, axis=1)
        centred = mixed - row_mean(mixed)
        rstd = lax.rsqrt(row_mean(centred * centred) + 1e-6)
        norm_o = centred * rstd
        norm_o_s[l] = norm_o
        rstd_o_s[l] = jnp.broadcast_to(rstd, (ROWS, 128))
        branch = (norm_o * proj_s[l, :, pl.ds(0, WIDTH)].astype(F32)).astype(BF)
        out_ref[l, 64:128, :] = branch
        acts = (acts + mm(branch, weights[l, :, pl.ds(4 * WIDTH, WIDTH)])).astype(BF).astype(F32)

    last = iota((ROWS, WIDTH), 0) == count[:, 0:1] - 1
    state = jnp.sum(jnp.where(last, acts, 0.0), axis=0, keepdims=True)
    for q in range(LAYERS):
        quarter = jnp.broadcast_to(state[:, 128 * q : 128 * q + 128], (16, 128))
        out_ref[q, 192:208, :] = jnp.concatenate([quarter] * 4, axis=1).astype(BF)
    seed = jnp.concatenate([cot_ref[q].astype(F32)[0:1] for q in range(LAYERS)], axis=1)
    cot = jnp.where(last, jnp.broadcast_to(seed, (ROWS, WIDTH)), 0.0).astype(BF)

    for l in reversed(range(LAYERS)):
        out_ref[l, 128:192, :] = cot
        d_branch = mm(cot, weights[l, :, pl.ds(4 * WIDTH, WIDTH)], NT).astype(BF).astype(F32)
        norm_o = norm_o_s[l]
        d_gate = (d_branch * norm_o).astype(BF)
        d_norm = d_branch * proj_s[l, :, pl.ds(0, WIDTH)].astype(F32)
        d_mixed = rstd_o_s[l][:, 0:1] * (d_norm - row_mean(d_norm) - norm_o * row_mean(d_norm * norm_o))
        d_mixed = d_mixed.astype(BF)
        d_value, d_query, d_key = [], [], []
        for p in range(PAIRS):
            d_out = d_mixed[:, 128 * p : 128 * p + 128]
            d_att = mm(d_out, block_diagonal(proj_s[l, :, part(1, p)]), NT).astype(BF).astype(F32)
            d_value.append(merge(mm(att_s[l, p], d_out, TN)))
            d_score = (d_att * datt_s[l, p]).astype(BF)
            d_query.append(mm(d_score, block_diagonal(proj_s[l, :, part(3, p)])))
            d_key.append(merge(mm(d_score, proj_s[l, :, part(2, p)], TN)))
        d_normed = jnp.zeros((ROWS, WIDTH), F32)
        for kind, pieces in enumerate(([d_gate], d_value, d_query, d_key)):
            cols = pl.ds(kind * WIDTH, WIDTH)
            whole = pieces[0] if len(pieces) == 1 else jnp.concatenate(pieces, axis=1)
            d_pre = whole.astype(BF).astype(F32) * dsilu_s[l, :, cols]
            d_normed = d_normed + mm(d_pre.astype(BF), weights[l, :, cols], NT)
        d_normed = d_normed.astype(BF).astype(F32)
        normed = normed_s[l]
        d_in = rstd_s[l][:, 0:1] * (d_normed - row_mean(d_normed) - normed * row_mean(d_normed * normed))
        cot = (d_in + cot.astype(F32)).astype(BF)
        out_ref[l, 0:64, :] = cot


def gradient_kernel(own_rows, got_ref, grads_ref, keep_ref, send_ref):
    core = lax.axis_index("core")
    for t in range(LAYERS):
        grads_ref[t] = got_ref[t, 0:64, :]
    branch = jnp.concatenate([got_ref[t, 64:128, :] for t in range(LAYERS)], axis=0)
    cot = jnp.concatenate([got_ref[t, 128:192, :] for t in range(LAYERS)], axis=0)
    half = WIDTH // 2
    to, source = iota((WIDTH, WIDTH), 1), iota((WIDTH, WIDTH), 0)
    side = jnp.where(to < half, core, 1 - core)
    within = jnp.where(to < half, to, to - half)
    wanted = (within // own_rows) * (2 * own_rows) + side * own_rows + within % own_rows
    order = (source == wanted).astype(F32).astype(BF)
    ordered = mm(branch, order).astype(BF)
    keep_ref[...] = mm(ordered[:, :half], cot, TN)
    send_ref[0:half, :] = mm(ordered[:, half:], cot, TN).astype(BF)
    states = [got_ref[t, 192:208, 0:128] for t in range(LAYERS)]
    send_ref[half : half + 16, :] = jnp.concatenate(states, axis=1)


def packing_kernel(block_rows, own_rows, keep_ref, send_ref, got_ref, out_ref):
    half = WIDTH // 2
    core = lax.axis_index("core")
    total = (keep_ref[...] + got_ref[0:half, :].astype(F32)).astype(BF)
    rows = out_ref.shape[0]
    place, source = iota((rows, half), 0), iota((rows, half), 1)
    chip = whole_part(place, block_rows)
    within = place - chip * block_rows
    pick = (within < own_rows) & (source == chip * own_rows + within)
    laid = mm(pick.astype(F32).astype(BF), total)
    own = send_ref[half : half + 16, :].astype(F32)[0:1]
    other = got_ref[half : half + 16, :].astype(F32)[0:1]
    first = jnp.where(core == 0, own, other)
    second = jnp.where(core == 0, other, own)
    place = iota((rows, WIDTH), 0)
    at = place - whole_part(place, block_rows) * block_rows
    laid = laid + jnp.where(at == own_rows, first, 0.0) + jnp.where(at == own_rows + 1, second, 0.0)
    out_ref[...] = laid.astype(BF)


def result_kernel(block_rows, got_ref, hot_ref, served_ref, weight_ref):
    rows = got_ref.shape[0]
    out_rows = weight_ref.shape[0]
    lead = max(16, out_rows)
    place = iota((lead, rows), 1)
    within = place - whole_part(place, block_rows) * block_rows
    pick = ((within == iota((lead, rows), 0)) & (within < out_rows)).astype(F32).astype(BF)
    got = got_ref[...]
    weight_ref[...] = mm(pick, got)[0:out_rows]
    served = jnp.zeros((16, 128), F32)
    for h in range(DEV_HIST):
        served = served + mm(hot_ref[h], got[:, 128 * h : 128 * h + 128])
    served_ref[...] = served[0:SLOTS].astype(BF)


def shape(dims, dtype):
    return jax.ShapeDtypeStruct(dims, dtype)


def call(kernel, outs, scratch=(), in_specs=None, out_specs=None, limit=48):
    specs = {} if in_specs is None else {"in_specs": in_specs}
    specs |= {} if out_specs is None else {"out_specs": out_specs}
    return pl.pallas_call(
        kernel,
        out_shape=outs,
        scratch_shapes=scratch,
        **specs,
        compiler_params=pltpu.CompilerParams(vmem_limit_bytes=limit * 1024 * 1024),
    )


def body(events, lengths, balance_plan, routes, w_uvqk, w_out, rel_bias, state_cotangent):
    n_z, n_y, n_core = (lax.axis_size(a) for a in DP)
    n_dp = n_z * n_y * n_core
    chips = n_z * n_y
    own_rows = WIDTH // n_dp
    block_rows = own_rows + 2
    half = WIDTH // 2

    any_spec, vmem = pl.BlockSpec(memory_space=pl.ANY), pl.BlockSpec(memory_space=pltpu.VMEM)
    smem = pl.BlockSpec(memory_space=pltpu.SMEM)
    with jax.named_scope("packing"):
        first, second, outgoing, facts = call(
            packing_start,
            (
                shape((half + 16, 5 * WIDTH), BF),
                shape((half, 5 * WIDTH), BF),
                shape((ROWS, WIDTH), BF),
                shape((n_dp, 2, (SLOTS + 2) * 64), BF),
            ),
            scratch=[
                pltpu.SMEM((DEV_HIST,), jnp.int32),
                pltpu.SMEM((DEV_HIST,), jnp.int32),
                pltpu.SMEM((DEV_HIST,), jnp.int32),
                pltpu.VMEM((8, ROWS), F32),
                pltpu.VMEM((SLOTS, 128), BF),
                pltpu.VMEM((16, 128), BF),
                pltpu.SemaphoreType.DMA((15,)),
            ],
            in_specs=[any_spec] * 8,
            out_specs=(any_spec, any_spec, any_spec, vmem),
            limit=58,
        )(balance_plan, routes.reshape(DEV_HIST), lengths, w_uvqk, w_out, events, rel_bias, state_cotangent)

    with jax.named_scope("section_weights"):
        ring = [(s * 2, (s - 1) % LAYERS * 2) for s in range(LAYERS)]
        ring += [(s * 2 + 1, (s + 1) % LAYERS * 2 + 1) for s in range(LAYERS)]
        swap = [(0, 1), (1, 0)]
        near_a = lax.ppermute(first, ("segment", "core"), ring)
        near_b = lax.ppermute(second, ("segment", "core"), ring)

    with jax.named_scope("events"):
        other_events = lax.ppermute(outgoing, "z", [(i, (i + n_z // 2) % n_z) for i in range(n_z)])

    with jax.named_scope("routing"):
        facts = lax.all_to_all(facts, DP, 0, 0, tiled=True)
        near_a, other_events, facts = lax.optimization_barrier((near_a, other_events, facts))
        near_b, facts = lax.optimization_barrier((near_b, facts))
        facts = facts.reshape(n_dp, (SLOTS + 2) * 128)

    with jax.named_scope("section_weights"):
        far_a = lax.ppermute(near_a, ("segment", "core"), ring)
        swap_a = lax.ppermute(near_a, "core", swap)
        swap_b = lax.ppermute(near_b, "core", swap)

    with jax.named_scope("routing"):
        seeds, hot, count = call(
            functools.partial(routing_kernel, block_rows, own_rows),
            (
                shape((LAYERS, 16, 128), BF),
                shape((DEV_HIST, 16, chips * block_rows), BF),
                shape((ROWS, 128), jnp.int32),
            ),
        )(facts)
        seeds = lax.all_to_all(seeds, "segment", 0, 0, tiled=True)
        far_a, swap_a, swap_b, seeds = lax.optimization_barrier((far_a, swap_a, swap_b, seeds))
    with jax.named_scope("section_weights"):
        far_b = lax.ppermute(far_a, "core", swap)

    with jax.named_scope("layers"):
        message = call(
            layers_kernel,
            shape((LAYERS, MSG, WIDTH), BF),
            scratch=[
                pltpu.VMEM((LAYERS, WIDTH, 5 * WIDTH), BF),
                pltpu.VMEM((LAYERS, 16, 128), BF),
                pltpu.VMEM((LAYERS, ROWS, 4 * WIDTH), BF),
                pltpu.VMEM((LAYERS, ROWS, 4 * WIDTH), F32),
                pltpu.VMEM((LAYERS, ROWS, WIDTH), F32),
                pltpu.VMEM((LAYERS, ROWS, 128), F32),
                pltpu.VMEM((LAYERS, ROWS, WIDTH), F32),
                pltpu.VMEM((LAYERS, ROWS, 128), F32),
                pltpu.VMEM((LAYERS, PAIRS, ROWS, 128), F32),
                pltpu.VMEM((LAYERS, PAIRS, ROWS, 128), BF),
                pltpu.VMEM((LAYERS, PAIRS, ROWS, 128), F32),
                pltpu.SemaphoreType.DMA((LAYERS, 2)),
                pltpu.SemaphoreType.DMA((LAYERS,)),
            ],
            in_specs=[smem] + [vmem] * 4 + [any_spec] * 8,
            limit=28,
        )(
            balance_plan, events, other_events, count, seeds,
            first, second, near_a, near_b, swap_a, swap_b, far_a, far_b,
        )

    with jax.named_scope("section_exchange"):
        arrived = lax.all_to_all(message, "segment", 0, 0, tiled=True)
    with jax.named_scope("weight_gradient"):
        grads, keep, send = call(
            functools.partial(gradient_kernel, own_rows),
            (
                shape((LAYERS, ROWS, WIDTH), BF),
                shape((half, WIDTH), F32),
                shape((half + 16, WIDTH), BF),
            ),
        )(arrived)
        partner = lax.ppermute(send, "core", swap)
        blocks = call(
            functools.partial(packing_kernel, block_rows, own_rows),
            shape((chips * block_rows, WIDTH), BF),
        )(keep, send, partner)
        blocks = lax.all_to_all(
            blocks.reshape(chips, block_rows, WIDTH), ("z", "y"), 0, 0, tiled=True
        )
        served, weight = call(
            functools.partial(result_kernel, block_rows),
            (shape((SLOTS, 128), BF), shape((own_rows, WIDTH), F32)),
        )(blocks.reshape(chips * block_rows, WIDTH), hot)
    return served[None], grads[None], weight[None]


def solution(mesh):
    devices = mesh.devices
    n_segment, n_dp = devices.shape
    side = 1
    while side * side * 2 < n_dp:
        side *= 2
    fine = Mesh(
        devices.reshape(n_segment, n_dp // (2 * side), side, 2), ("segment",) + DP
    )
    return jax.shard_map(
        body,
        mesh=fine,
        in_specs=(
            P(DP, None, None),
            P(DP),
            P(DP),
            P(DP, None),
            P("segment", None, None),
            P("segment", None, None),
            P("segment", None, None),
            P(DP, None, "segment"),
        ),
        out_specs=(
            P(DP, None, "segment"),
            P("segment", DP, None, None),
            P("segment", DP, None),
        ),
        check_vma=False,
    )
```

```python
import functools

import jax
import jax.numpy as jnp
from jax import lax
from jax.experimental import pallas as pl
from jax.experimental.pallas import tpu as pltpu
from jax.sharding import Mesh, PartitionSpec as P

BF = jnp.bfloat16
F32 = jnp.float32
DP = ("z", "y", "core")
DEV_HIST = 4
ROWS = 64
WIDTH = 512
HEAD_COLS = 64
PAIRS = 4
LAYERS = 4
SLOTS = 8
MSG = 208
NN = (((1,), (0,)), ((), ()))
NT = (((1,), (1,)), ((), ()))
TN = (((0,), (0,)), ((), ()))


def mm(a, b, dims=NN):
    return lax.dot_general(a, b, dims, preferred_element_type=F32)


def iota(shape, dim):
    return lax.broadcasted_iota(jnp.int32, shape, dim)


def row_mean(a):
    return jnp.mean(a, axis=-1, keepdims=True)


def sigmoid(a):
    return 0.5 * jnp.tanh(0.5 * a) + 0.5


def dp_place():
    ny, nc = lax.axis_size("y"), lax.axis_size("core")
    return (lax.axis_index("z") * ny + lax.axis_index("y")) * nc + lax.axis_index("core")


def wanted_value():
    upper = (lax.axis_index("z") >= lax.axis_size("z") // 2).astype(jnp.int32)
    return upper * DEV_HIST + lax.axis_index("segment")


def packing_start(
    plan_ref, routes_ref, lengths_ref, w_in_ref, w_out_ref, events_ref, bias_ref, cot_ref,
    first_ref, second_ref, outgoing_ref, facts_ref,
    plan, routes, lengths, bias_s, cot_s, sems,
):
    core = lax.axis_index("core")
    half = WIDTH // 2
    small = [(plan_ref, plan), (routes_ref, routes), (lengths_ref, lengths), (bias_ref.at[0], bias_s), (cot_ref.at[0], cot_s)]
    small = [pltpu.make_async_copy(*c, sems.at[n]) for n, c in enumerate(small)]
    for c in small:
        c.start()
    copies = []
    for side, dest in ((core, first_ref), (1 - core, second_ref)):
        for part in range(2):
            rows = pl.ds(pl.multiple_of(side * half + part * (half // 2), half // 2), half // 2)
            to = pl.ds(part * (half // 2), half // 2)
            copies.append((w_in_ref.at[0, rows], dest.at[to, pl.ds(0, 4 * WIDTH)]))
            copies.append((w_out_ref.at[0, rows], dest.at[to, pl.ds(4 * WIDTH, WIDTH)]))
    copies = [pltpu.make_async_copy(*c, sems.at[len(small) + n]) for n, c in enumerate(copies)]
    for c in copies:
        c.start()
    for c in small:
        c.wait()
    partner_value = DEV_HIST + 2 * lax.axis_index("segment") - wanted_value()
    chosen = jnp.int32(0)
    for h in range(DEV_HIST):
        chosen = chosen + jnp.where(plan[h] == partner_value, h, 0)
    copies.append(pltpu.make_async_copy(events_ref.at[chosen], outgoing_ref, sems.at[len(small) + len(copies)]))
    copies[-1].start()

    bias = bias_s[...]
    high = bias.astype(BF).astype(F32)
    middle = (bias - high).astype(BF).astype(F32)
    low = bias - high - middle
    pieces = jnp.concatenate([high, middle, low, jnp.zeros((8, ROWS), F32)]).astype(BF)
    row, head = iota((16, 32), 0), iota((16, 32), 1)
    even = (row // 4) * 8 + 2 * (row % 4)
    used = row < 12
    pick_even = (used & (head == even)).astype(F32).astype(BF)
    pick_odd = (used & (head == even + 1)).astype(F32).astype(BF)
    distance, place = iota((ROWS, 128), 0), iota((ROWS, 128), 1)
    to_even = (place == (128 - distance) % 128).astype(F32).astype(BF)
    to_odd = (place == ROWS - distance).astype(F32).astype(BF)
    base = mm(mm(pick_even, pieces).astype(BF), to_even) + mm(mm(pick_odd, pieces).astype(BF), to_odd)
    first_ref[half : half + 16, 0:128] = base.astype(BF)
    first_ref[half : half + 16, 128 : 5 * WIDTH] = jnp.zeros((16, 5 * WIDTH - 128), BF)

    lane = iota((1, 128), 1)
    facts = jnp.zeros((1, 128), F32)
    for j, ref in enumerate((routes, plan, lengths)):
        for h in range(DEV_HIST):
            facts = jnp.where(lane == 4 * j + h, ref[h].astype(F32), facts)
    cot = cot_s[...].astype(F32)
    blocks = [cot[k : k + 1] for k in range(SLOTS)] + [facts, jnp.zeros((1, 128), F32)]
    lines = [jnp.concatenate(blocks[k : k + 5], axis=1) for k in (0, 5)]
    facts_ref[...] = jnp.broadcast_to(jnp.concatenate(lines).astype(BF)[None], facts_ref.shape)
    for c in copies:
        c.wait()


def whole_part(a, d):
    if d & (d - 1) == 0:
        return a // d
    return jnp.floor((a.astype(F32) + 0.5) * (1.0 / d)).astype(jnp.int32)


def routing_kernel(block_rows, own_rows, table_ref, seeds_ref, hot_ref, count_ref):
    n_dp = table_ref.shape[0]
    hist = n_dp * DEV_HIST
    me = dp_place()
    facts = table_ref[:, SLOTS * 128 : SLOTS * 128 + 128]
    spread = mm(facts, (iota((128, hist), 0) == iota((128, hist), 1) % DEV_HIST).astype(F32).astype(BF))
    own = iota((n_dp, hist), 1) // DEV_HIST == iota((n_dp, hist), 0)
    routes = jnp.sum(jnp.where(own, spread, 0.0), axis=0, keepdims=True)

    routes_wide = jnp.broadcast_to(routes, (16, hist))
    history, mine = iota((16, hist), 1), me * DEV_HIST + iota((16, hist), 0)
    route = jnp.sum(jnp.where(history == mine, routes_wide, 0.0), axis=1, keepdims=True)
    before = (routes_wide == route) & (history < mine)
    slot = jnp.sum(before.astype(F32), axis=1, keepdims=True)
    source = iota((16, n_dp), 1).astype(F32)
    seeds = jnp.zeros((16, 128), F32)
    for k in range(SLOTS):
        pick = jnp.where((source == route) & (slot == float(k)), 1.0, 0.0).astype(BF)
        seeds = seeds + mm(pick, table_ref[:, 128 * k : 128 * k + 128])
    for q in range(LAYERS):
        seeds_ref[q] = jnp.broadcast_to(seeds[q : q + 1], (16, 128)).astype(BF)

    hit = jnp.broadcast_to((routes == me.astype(F32)).astype(F32), (16, hist))
    earlier = (iota((hist, hist), 0) < iota((hist, hist), 1)).astype(F32).astype(BF)
    place_of = mm(hit.astype(BF), earlier)
    hot = jnp.where(place_of == iota((16, hist), 0).astype(F32), hit, 0.0).astype(BF)
    total = hot_ref.shape[2]
    place, history = iota((hist, total), 1), iota((hist, total), 0)
    chip = whole_part(place, block_rows)
    within = place - chip * block_rows - own_rows
    first = (chip * 2 + within) * DEV_HIST
    valid = (within >= 0) & (within < 2)
    for h in range(DEV_HIST):
        move = jnp.where(valid & (history == first + h), 1.0, 0.0).astype(BF)
        hot_ref[h] = mm(hot, move).astype(BF)

    other = lax.rem(me + n_dp // 2, n_dp)
    known = facts.astype(F32)
    ahead = pltpu.roll(known, 124, 1)
    row, lane = iota((n_dp, 128), 0), iota((n_dp, 128), 1)
    fits = ((row == me) | (row == other)) & (lane >= 4) & (lane < 8)
    fits = fits & (known == wanted_value().astype(F32))
    length = jnp.sum(jnp.where(fits, ahead, 0.0), axis=1, keepdims=True)
    length = jnp.sum(length, axis=0, keepdims=True)
    count_ref[...] = jnp.broadcast_to(length, count_ref.shape).astype(jnp.int32)


def layers_kernel(
    plan_ref, events_ref, other_ref, count_ref, cot_ref,
    first, second, near_a, near_b, swap_a, swap_b, far_a, far_b,
    out_ref,
    weights, tables, proj_s, dsilu_s, normed_s, rstd_s, norm_o_s, rstd_o_s, bias_s, att_s, datt_s, sems, table_sem,
):
    half = WIDTH // 2
    segment, core = lax.axis_index("segment"), lax.axis_index("core")
    near = lax.rem(segment + 1 + 2 * core, LAYERS)
    swap = lax.rem(segment + 3 + 2 * core, LAYERS)
    far = lax.rem(segment + 2, LAYERS)
    held = (
        (segment, first, core, second, 1 - core),
        (near, near_a, core, near_b, 1 - core),
        (swap, swap_a, 1 - core, swap_b, core),
        (far, far_a, core, far_b, 1 - core),
    )
    for l in range(LAYERS):
        for slot, one, side, two, other_side in held:

            @pl.when(slot == l)
            def _():
                pltpu.make_async_copy(
                    one.at[pl.ds(half, 16), pl.ds(0, 128)], tables.at[l], table_sem.at[l]
                ).start()
                for piece, at in ((one, side), (two, other_side)):
                    rows = pl.ds(pl.multiple_of(at * half, half), half)
                    pltpu.make_async_copy(piece.at[pl.ds(0, half)], weights.at[l, rows], sems.at[l, at]).start()

    lane, row = iota((ROWS, 128), 1), iota((ROWS, 128), 0)
    left = (lane < HEAD_COLS).astype(F32)
    left_b, right_b = left.astype(BF), (1.0 - left).astype(BF)
    column = jnp.where(lane < HEAD_COLS, lane, lane - HEAD_COLS)
    count = count_ref[...]
    allowed = (column <= row) & (column < count)

    def block_diagonal(a):
        return jnp.concatenate([a * left_b, a * right_b], axis=0)

    def merge(a):
        return jnp.where(lane < HEAD_COLS, a[:ROWS], a[ROWS:])

    def part(kind, p):
        return pl.ds(kind * WIDTH + p * 128, 128)

    value = wanted_value()
    found = jnp.int32(0)
    acts = jnp.zeros((ROWS, WIDTH), F32)
    for h in range(DEV_HIST):
        same = (plan_ref[h] == value).astype(jnp.int32)
        found = found + same
        acts = jnp.where(same == 1, events_ref[h].astype(F32), acts)
    acts = jnp.where(found > 0, acts, other_ref[...].astype(F32))

    for l in range(LAYERS):
        average = row_mean(acts)
        centred = acts - average
        rstd = lax.rsqrt(row_mean(centred * centred) + 1e-6)
        normed = centred * rstd
        normed_s[l] = normed
        rstd_s[l] = jnp.broadcast_to(rstd, (ROWS, 128))
        for c in range(2):
            piece = weights.at[l, pl.ds(c * half, half)]
            pltpu.make_async_copy(piece, piece, sems.at[l, c]).wait()
        pltpu.make_async_copy(tables.at[l], tables.at[l], table_sem.at[l]).wait()
        table = tables[l].astype(F32)
        table = table[0:4] + table[4:8] + table[8:12]
        for p in range(PAIRS):
            wide = jnp.broadcast_to(table[p : p + 1], (ROWS, 128))
            bias_s[l, p] = pltpu.roll(wide, 0, 1, stride=1, stride_axis=0)
        normed_b = normed.astype(BF)
        for kind in range(4):
            cols = pl.ds(kind * WIDTH, WIDTH)
            pre = mm(normed_b, weights[l, :, cols])
            gated = sigmoid(pre)
            silu = pre * gated
            proj_s[l, :, cols] = silu.astype(BF)
            dsilu_s[l, :, cols] = gated + silu * (1.0 - gated)
        outs = []
        for p in range(PAIRS):
            keys = block_diagonal(proj_s[l, :, part(3, p)])
            score = mm(proj_s[l, :, part(2, p)], keys, NT) * 0.125 + bias_s[l, p]
            gated = sigmoid(score)
            silu = score * gated
            att = jnp.where(allowed, silu, 0.0).astype(BF)
            att_s[l, p] = att
            datt_s[l, p] = jnp.where(allowed, gated + silu * (1.0 - gated), 0.0) * 0.125
            outs.append(mm(att, block_diagonal(proj_s[l, :, part(1, p)])))
        mixed = jnp.concatenate(outs, axis=1)
        centred = mixed - row_mean(mixed)
        rstd = lax.rsqrt(row_mean(centred * centred) + 1e-6)
        norm_o = centred * rstd
        norm_o_s[l] = norm_o
        rstd_o_s[l] = jnp.broadcast_to(rstd, (ROWS, 128))
        branch = (norm_o * proj_s[l, :, pl.ds(0, WIDTH)].astype(F32)).astype(BF)
        out_ref[l, 64:128, :] = branch
        acts = (acts + mm(branch, weights[l, :, pl.ds(4 * WIDTH, WIDTH)])).astype(BF).astype(F32)

    last = iota((ROWS, WIDTH), 0) == count[:, 0:1] - 1
    state = jnp.sum(jnp.where(last, acts, 0.0), axis=0, keepdims=True)
    for q in range(LAYERS):
        quarter = jnp.broadcast_to(state[:, 128 * q : 128 * q + 128], (16, 128))
        out_ref[q, 192:208, :] = jnp.concatenate([quarter] * 4, axis=1).astype(BF)
    seed = jnp.concatenate([cot_ref[q].astype(F32)[0:1] for q in range(LAYERS)], axis=1)
    cot = jnp.where(last, jnp.broadcast_to(seed, (ROWS, WIDTH)), 0.0).astype(BF)

    for l in reversed(range(LAYERS)):
        out_ref[l, 128:192, :] = cot
        d_branch = mm(cot, weights[l, :, pl.ds(4 * WIDTH, WIDTH)], NT).astype(BF).astype(F32)
        norm_o = norm_o_s[l]
        d_gate = (d_branch * norm_o).astype(BF)
        d_norm = d_branch * proj_s[l, :, pl.ds(0, WIDTH)].astype(F32)
        d_mixed = rstd_o_s[l][:, 0:1] * (d_norm - row_mean(d_norm) - norm_o * row_mean(d_norm * norm_o))
        d_mixed = d_mixed.astype(BF)
        d_value, d_query, d_key = [], [], []
        for p in range(PAIRS):
            d_out = d_mixed[:, 128 * p : 128 * p + 128]
            d_att = mm(d_out, block_diagonal(proj_s[l, :, part(1, p)]), NT).astype(BF).astype(F32)
            d_value.append(merge(mm(att_s[l, p], d_out, TN)))
            d_score = (d_att * datt_s[l, p]).astype(BF)
            d_query.append(mm(d_score, block_diagonal(proj_s[l, :, part(3, p)])))
            d_key.append(merge(mm(d_score, proj_s[l, :, part(2, p)], TN)))
        d_normed = jnp.zeros((ROWS, WIDTH), F32)
        for kind, pieces in enumerate(([d_gate], d_value, d_query, d_key)):
            cols = pl.ds(kind * WIDTH, WIDTH)
            whole = pieces[0] if len(pieces) == 1 else jnp.concatenate(pieces, axis=1)
            d_pre = whole.astype(BF).astype(F32) * dsilu_s[l, :, cols]
            d_normed = d_normed + mm(d_pre.astype(BF), weights[l, :, cols], NT)
        d_normed = d_normed.astype(BF).astype(F32)
        normed = normed_s[l]
        d_in = rstd_s[l][:, 0:1] * (d_normed - row_mean(d_normed) - normed * row_mean(d_normed * normed))
        cot = (d_in + cot.astype(F32)).astype(BF)
        out_ref[l, 0:64, :] = cot


def gradient_kernel(own_rows, got_ref, grads_ref, keep_ref, send_ref):
    core = lax.axis_index("core")
    for t in range(LAYERS):
        grads_ref[t] = got_ref[t, 0:64, :]
    branch = jnp.concatenate([got_ref[t, 64:128, :] for t in range(LAYERS)], axis=0)
    cot = jnp.concatenate([got_ref[t, 128:192, :] for t in range(LAYERS)], axis=0)
    half = WIDTH // 2
    to, source = iota((WIDTH, WIDTH), 1), iota((WIDTH, WIDTH), 0)
    side = jnp.where(to < half, core, 1 - core)
    within = jnp.where(to < half, to, to - half)
    wanted = (within // own_rows) * (2 * own_rows) + side * own_rows + within % own_rows
    order = (source == wanted).astype(F32).astype(BF)
    ordered = mm(branch, order).astype(BF)
    keep_ref[...] = mm(ordered[:, :half], cot, TN)
    send_ref[0:half, :] = mm(ordered[:, half:], cot, TN).astype(BF)
    states = [got_ref[t, 192:208, 0:128] for t in range(LAYERS)]
    send_ref[half : half + 16, :] = jnp.concatenate(states, axis=1)


def packing_kernel(block_rows, own_rows, keep_ref, send_ref, got_ref, out_ref):
    half = WIDTH // 2
    core = lax.axis_index("core")
    total = (keep_ref[...] + got_ref[0:half, :].astype(F32)).astype(BF)
    rows = out_ref.shape[0]
    place, source = iota((rows, half), 0), iota((rows, half), 1)
    chip = whole_part(place, block_rows)
    within = place - chip * block_rows
    pick = (within < own_rows) & (source == chip * own_rows + within)
    laid = mm(pick.astype(F32).astype(BF), total)
    own = send_ref[half : half + 16, :].astype(F32)[0:1]
    other = got_ref[half : half + 16, :].astype(F32)[0:1]
    first = jnp.where(core == 0, own, other)
    second = jnp.where(core == 0, other, own)
    place = iota((rows, WIDTH), 0)
    at = place - whole_part(place, block_rows) * block_rows
    laid = laid + jnp.where(at == own_rows, first, 0.0) + jnp.where(at == own_rows + 1, second, 0.0)
    out_ref[...] = laid.astype(BF)


def result_kernel(block_rows, got_ref, hot_ref, served_ref, weight_ref):
    rows = got_ref.shape[0]
    out_rows = weight_ref.shape[0]
    lead = max(16, out_rows)
    place = iota((lead, rows), 1)
    within = place - whole_part(place, block_rows) * block_rows
    pick = ((within == iota((lead, rows), 0)) & (within < out_rows)).astype(F32).astype(BF)
    got = got_ref[...]
    weight_ref[...] = mm(pick, got)[0:out_rows]
    served = jnp.zeros((16, 128), F32)
    for h in range(DEV_HIST):
        served = served + mm(hot_ref[h], got[:, 128 * h : 128 * h + 128])
    served_ref[...] = served[0:SLOTS].astype(BF)


def shape(dims, dtype):
    return jax.ShapeDtypeStruct(dims, dtype)


def call(kernel, outs, scratch=(), in_specs=None, out_specs=None, limit=48):
    specs = {} if in_specs is None else {"in_specs": in_specs}
    specs |= {} if out_specs is None else {"out_specs": out_specs}
    return pl.pallas_call(
        kernel,
        out_shape=outs,
        scratch_shapes=scratch,
        **specs,
        compiler_params=pltpu.CompilerParams(vmem_limit_bytes=limit * 1024 * 1024),
    )


def body(events, lengths, balance_plan, routes, w_uvqk, w_out, rel_bias, state_cotangent):
    n_z, n_y, n_core = (lax.axis_size(a) for a in DP)
    n_dp = n_z * n_y * n_core
    chips = n_z * n_y
    own_rows = WIDTH // n_dp
    block_rows = own_rows + 2
    half = WIDTH // 2

    any_spec, vmem = pl.BlockSpec(memory_space=pl.ANY), pl.BlockSpec(memory_space=pltpu.VMEM)
    smem = pl.BlockSpec(memory_space=pltpu.SMEM)
    with jax.named_scope("packing"):
        first, second, outgoing, facts = call(
            packing_start,
            (
                shape((half + 16, 5 * WIDTH), BF),
                shape((half, 5 * WIDTH), BF),
                shape((ROWS, WIDTH), BF),
                shape((n_dp, 2, (SLOTS + 2) * 64), BF),
            ),
            scratch=[
                pltpu.SMEM((DEV_HIST,), jnp.int32),
                pltpu.SMEM((DEV_HIST,), jnp.int32),
                pltpu.SMEM((DEV_HIST,), jnp.int32),
                pltpu.VMEM((8, ROWS), F32),
                pltpu.VMEM((SLOTS, 128), BF),
                pltpu.SemaphoreType.DMA((14,)),
            ],
            in_specs=[any_spec] * 8,
            limit=58,
        )(balance_plan, routes.reshape(DEV_HIST), lengths, w_uvqk, w_out, events, rel_bias, state_cotangent)

    with jax.named_scope("section_weights"):
        ring = [(s * 2, (s - 1) % LAYERS * 2) for s in range(LAYERS)]
        ring += [(s * 2 + 1, (s + 1) % LAYERS * 2 + 1) for s in range(LAYERS)]
        swap = [(0, 1), (1, 0)]
        near_a = lax.ppermute(first, ("segment", "core"), ring)
        near_b = lax.ppermute(second, ("segment", "core"), ring)

    with jax.named_scope("events"):
        other_events = lax.ppermute(outgoing, "z", [(i, (i + n_z // 2) % n_z) for i in range(n_z)])

    with jax.named_scope("routing"):
        facts = lax.all_to_all(facts, DP, 0, 0, tiled=True)
        near_a, other_events, facts = lax.optimization_barrier((near_a, other_events, facts))
        near_b, facts = lax.optimization_barrier((near_b, facts))
        facts = facts.reshape(n_dp, (SLOTS + 2) * 128)

    with jax.named_scope("section_weights"):
        far_a = lax.ppermute(near_a, ("segment", "core"), ring)
        swap_a = lax.ppermute(near_a, "core", swap)
        swap_b = lax.ppermute(near_b, "core", swap)

    with jax.named_scope("routing"):
        seeds, hot, count = call(
            functools.partial(routing_kernel, block_rows, own_rows),
            (
                shape((LAYERS, 16, 128), BF),
                shape((DEV_HIST, 16, chips * block_rows), BF),
                shape((ROWS, 128), jnp.int32),
            ),
        )(facts)
        seeds = lax.all_to_all(seeds, "segment", 0, 0, tiled=True)
        far_a, swap_a, swap_b, seeds = lax.optimization_barrier((far_a, swap_a, swap_b, seeds))
    with jax.named_scope("section_weights"):
        far_b = lax.ppermute(far_a, "core", swap)

    with jax.named_scope("layers"):
        message = call(
            layers_kernel,
            shape((LAYERS, MSG, WIDTH), BF),
            scratch=[
                pltpu.VMEM((LAYERS, WIDTH, 5 * WIDTH), BF),
                pltpu.VMEM((LAYERS, 16, 128), BF),
                pltpu.VMEM((LAYERS, ROWS, 4 * WIDTH), BF),
                pltpu.VMEM((LAYERS, ROWS, 4 * WIDTH), F32),
                pltpu.VMEM((LAYERS, ROWS, WIDTH), F32),
                pltpu.VMEM((LAYERS, ROWS, 128), F32),
                pltpu.VMEM((LAYERS, ROWS, WIDTH), F32),
                pltpu.VMEM((LAYERS, ROWS, 128), F32),
                pltpu.VMEM((LAYERS, PAIRS, ROWS, 128), F32),
                pltpu.VMEM((LAYERS, PAIRS, ROWS, 128), BF),
                pltpu.VMEM((LAYERS, PAIRS, ROWS, 128), F32),
                pltpu.SemaphoreType.DMA((LAYERS, 2)),
                pltpu.SemaphoreType.DMA((LAYERS,)),
            ],
            in_specs=[smem] + [vmem] * 4 + [any_spec] * 8,
            limit=28,
        )(
            balance_plan, events, other_events, count, seeds,
            first, second, near_a, near_b, swap_a, swap_b, far_a, far_b,
        )

    with jax.named_scope("section_exchange"):
        arrived = lax.all_to_all(message, "segment", 0, 0, tiled=True)
    with jax.named_scope("weight_gradient"):
        grads, keep, send = call(
            functools.partial(gradient_kernel, own_rows),
            (
                shape((LAYERS, ROWS, WIDTH), BF),
                shape((half, WIDTH), F32),
                shape((half + 16, WIDTH), BF),
            ),
        )(arrived)
        partner = lax.ppermute(send, "core", swap)
        blocks = call(
            functools.partial(packing_kernel, block_rows, own_rows),
            shape((chips * block_rows, WIDTH), BF),
        )(keep, send, partner)
        blocks = lax.all_to_all(
            blocks.reshape(chips, block_rows, WIDTH), ("z", "y"), 0, 0, tiled=True
        )
        served, weight = call(
            functools.partial(result_kernel, block_rows),
            (shape((SLOTS, 128), BF), shape((own_rows, WIDTH), F32)),
        )(blocks.reshape(chips * block_rows, WIDTH), hot)
    return served[None], grads[None], weight[None]


def solution(mesh):
    devices = mesh.devices
    n_segment, n_dp = devices.shape
    side = 1
    while side * side * 2 < n_dp:
        side *= 2
    fine = Mesh(
        devices.reshape(n_segment, n_dp // (2 * side), side, 2), ("segment",) + DP
    )
    return jax.shard_map(
        body,
        mesh=fine,
        in_specs=(
            P(DP, None, None),
            P(DP),
            P(DP),
            P(DP, None),
            P("segment", None, None),
            P("segment", None, None),
            P("segment", None, None),
            P(DP, None, "segment"),
        ),
        out_specs=(
            P(DP, None, "segment"),
            P("segment", DP, None, None),
            P("segment", DP, None),
        ),
        check_vma=False,
    )
```

```python
import functools

import jax
import jax.numpy as jnp
from jax import lax
from jax.experimental import pallas as pl
from jax.experimental.pallas import tpu as pltpu
from jax.sharding import Mesh, PartitionSpec as P

BF = jnp.bfloat16
F32 = jnp.float32
DP = ("z", "y", "core")
DEV_HIST = 4
ROWS = 64
WIDTH = 512
HEAD_COLS = 64
GROUP = 256
GROUPS = WIDTH // GROUP
LAYERS = 4
SLOTS = 8
MSG = 208
NN = (((1,), (0,)), ((), ()))
NT = (((1,), (1,)), ((), ()))
TN = (((0,), (0,)), ((), ()))


def mm(a, b, dims=NN):
    return lax.dot_general(a, b, dims, preferred_element_type=F32)


def iota(shape, dim):
    return lax.broadcasted_iota(jnp.int32, shape, dim)


def row_mean(a):
    return jnp.mean(a, axis=-1, keepdims=True)


def sigmoid(a):
    return 0.5 * jnp.tanh(0.5 * a) + 0.5


def dp_place():
    ny, nc = lax.axis_size("y"), lax.axis_size("core")
    return (lax.axis_index("z") * ny + lax.axis_index("y")) * nc + lax.axis_index("core")


def wanted_value():
    upper = (lax.axis_index("z") >= lax.axis_size("z") // 2).astype(jnp.int32)
    return upper * DEV_HIST + lax.axis_index("segment")


def packing_start(
    plan_ref, routes_ref, lengths_ref, w_in_ref, w_out_ref, events_ref, bias_ref, cot_ref,
    first_ref, second_ref, outgoing_ref, facts_ref,
    plan, routes, lengths, bias_s, cot_s, sems,
):
    core = lax.axis_index("core")
    half = WIDTH // 2
    small = [(plan_ref, plan), (routes_ref, routes), (lengths_ref, lengths), (bias_ref.at[0], bias_s), (cot_ref.at[0], cot_s)]
    small = [pltpu.make_async_copy(*c, sems.at[n]) for n, c in enumerate(small)]
    for c in small:
        c.start()
    copies = []
    for side, dest in ((core, first_ref), (1 - core, second_ref)):
        for part in range(2):
            rows = pl.ds(pl.multiple_of(side * half + part * (half // 2), half // 2), half // 2)
            to = pl.ds(part * (half // 2), half // 2)
            copies.append((w_in_ref.at[0, rows], dest.at[to, pl.ds(0, 4 * WIDTH)]))
            copies.append((w_out_ref.at[0, rows], dest.at[to, pl.ds(4 * WIDTH, WIDTH)]))
    copies = [pltpu.make_async_copy(*c, sems.at[len(small) + n]) for n, c in enumerate(copies)]
    for c in copies:
        c.start()
    for c in small:
        c.wait()
    partner_value = DEV_HIST + 2 * lax.axis_index("segment") - wanted_value()
    chosen = jnp.int32(0)
    for h in range(DEV_HIST):
        chosen = chosen + jnp.where(plan[h] == partner_value, h, 0)
    copies.append(pltpu.make_async_copy(events_ref.at[chosen], outgoing_ref, sems.at[len(small) + len(copies)]))
    copies[-1].start()

    bias = bias_s[...]
    high = bias.astype(BF).astype(F32)
    middle = (bias - high).astype(BF).astype(F32)
    low = bias - high - middle
    pieces = jnp.concatenate([high, middle, low, jnp.zeros((8, ROWS), F32)]).astype(BF)
    row, head = iota((16, 32), 0), iota((16, 32), 1)
    even = (row // 4) * 8 + 2 * (row % 4)
    used = row < 12
    pick_even = (used & (head == even)).astype(F32).astype(BF)
    pick_odd = (used & (head == even + 1)).astype(F32).astype(BF)
    distance, place = iota((ROWS, 128), 0), iota((ROWS, 128), 1)
    to_even = (place == (128 - distance) % 128).astype(F32).astype(BF)
    to_odd = (place == ROWS - distance).astype(F32).astype(BF)
    base = mm(mm(pick_even, pieces).astype(BF), to_even) + mm(mm(pick_odd, pieces).astype(BF), to_odd)
    first_ref[half : half + 16, 0:128] = base.astype(BF)
    first_ref[half : half + 16, 128 : 5 * WIDTH] = jnp.zeros((16, 5 * WIDTH - 128), BF)

    lane = iota((1, 128), 1)
    facts = jnp.zeros((1, 128), F32)
    for j, ref in enumerate((routes, plan, lengths)):
        for h in range(DEV_HIST):
            facts = jnp.where(lane == 4 * j + h, ref[h].astype(F32), facts)
    cot = cot_s[...].astype(F32)
    blocks = [cot[k : k + 1] for k in range(SLOTS)] + [facts, jnp.zeros((1, 128), F32)]
    lines = [jnp.concatenate(blocks[k : k + 5], axis=1) for k in (0, 5)]
    facts_ref[...] = jnp.broadcast_to(jnp.concatenate(lines).astype(BF)[None], facts_ref.shape)
    for c in copies:
        c.wait()


def routing_kernel(own_rows, table_ref, seeds_ref, hot_ref, count_ref):
    n_dp = table_ref.shape[0]
    hist = n_dp * DEV_HIST
    me = dp_place()
    facts = table_ref[:, SLOTS * 128 : SLOTS * 128 + 128]
    spread = mm(facts, (iota((128, hist), 0) == iota((128, hist), 1) % DEV_HIST).astype(F32).astype(BF))
    own = iota((n_dp, hist), 1) // DEV_HIST == iota((n_dp, hist), 0)
    routes = jnp.sum(jnp.where(own, spread, 0.0), axis=0, keepdims=True)

    routes_wide = jnp.broadcast_to(routes, (16, hist))
    history, mine = iota((16, hist), 1), me * DEV_HIST + iota((16, hist), 0)
    route = jnp.sum(jnp.where(history == mine, routes_wide, 0.0), axis=1, keepdims=True)
    before = (routes_wide == route) & (history < mine)
    slot = jnp.sum(before.astype(F32), axis=1, keepdims=True)
    source = iota((16, n_dp), 1).astype(F32)
    seeds = jnp.zeros((16, 128), F32)
    for k in range(SLOTS):
        pick = jnp.where((source == route) & (slot == float(k)), 1.0, 0.0).astype(BF)
        seeds = seeds + mm(pick, table_ref[:, 128 * k : 128 * k + 128])
    for q in range(LAYERS):
        seeds_ref[q] = jnp.broadcast_to(seeds[q : q + 1], (16, 128)).astype(BF)

    hit = jnp.broadcast_to((routes == me.astype(F32)).astype(F32), (16, hist))
    earlier = (iota((hist, hist), 0) < iota((hist, hist), 1)).astype(F32).astype(BF)
    place_of = mm(hit.astype(BF), earlier)
    hot = jnp.where(place_of == iota((16, hist), 0).astype(F32), hit, 0.0).astype(BF)
    total = hot_ref.shape[2]
    place, history = iota((hist, total), 1), iota((hist, total), 0)
    chip = place // own_rows
    within = place - chip * own_rows
    first = (chip * 2 + within // 2) * DEV_HIST
    for h in range(DEV_HIST):
        valid = (within < 4) & (within % 2 == h // 2)
        move = jnp.where(valid & (history == first + h), 1.0, 0.0).astype(BF)
        hot_ref[h] = mm(hot, move).astype(BF)

    other = lax.rem(me + n_dp // 2, n_dp)
    known = facts.astype(F32)
    ahead = pltpu.roll(known, 124, 1)
    row, lane = iota((n_dp, 128), 0), iota((n_dp, 128), 1)
    fits = ((row == me) | (row == other)) & (lane >= 4) & (lane < 8)
    fits = fits & (known == wanted_value().astype(F32))
    length = jnp.sum(jnp.where(fits, ahead, 0.0), axis=1, keepdims=True)
    length = jnp.sum(length, axis=0, keepdims=True)
    count_ref[...] = jnp.broadcast_to(length, count_ref.shape).astype(jnp.int32)


def layers_kernel(
    plan_ref, events_ref, other_ref, count_ref, cot_ref,
    first, w_in_ref, w_out_ref, near_a, near_b, swap_a, swap_b, far_a, far_b,
    out_ref,
    weights, tables, proj_s, dsilu_s, normed_s, rstd_s, norm_o_s, rstd_o_s, att_s, datt_s, sems, table_sem,
):
    half = WIDTH // 2
    segment, core = lax.axis_index("segment"), lax.axis_index("core")
    near = lax.rem(segment + 1 + 2 * core, LAYERS)
    swap = lax.rem(segment + 3 + 2 * core, LAYERS)
    far = lax.rem(segment + 2, LAYERS)
    held = (
        (near, near_a, core, near_b, 1 - core),
        (swap, swap_a, 1 - core, swap_b, core),
        (far, far_a, core, far_b, 1 - core),
    )
    for l in range(LAYERS):

        @pl.when(segment == l)
        def _():
            pltpu.make_async_copy(first.at[pl.ds(half, 16), pl.ds(0, 128)], tables.at[l], table_sem.at[l]).start()
            for at in range(2):
                rows = pl.ds(at * half, half)
                for piece, cols in ((w_in_ref, pl.ds(0, 4 * WIDTH)), (w_out_ref, pl.ds(4 * WIDTH, WIDTH))):
                    pltpu.make_async_copy(piece.at[0, rows], weights.at[l, rows, cols], sems.at[l, at]).start()

        for slot, one, side, two, other_side in held:

            @pl.when(slot == l)
            def _():
                pltpu.make_async_copy(
                    one.at[pl.ds(half, 16), pl.ds(0, 128)], tables.at[l], table_sem.at[l]
                ).start()
                for piece, at in ((one, side), (two, other_side)):
                    rows = pl.ds(pl.multiple_of(at * half, half), half)
                    pltpu.make_async_copy(piece.at[pl.ds(0, half)], weights.at[l, rows], sems.at[l, at]).start()

    row, lane = iota((ROWS, GROUP), 0), iota((ROWS, GROUP), 1)
    head = lane // HEAD_COLS
    column = lane - head * HEAD_COLS
    own_head = [(head == h).astype(F32).astype(BF) for h in range(GROUP // HEAD_COLS)]
    count = count_ref[...]
    allowed = (column <= row) & (column < count[:, 0:1])

    def block_diagonal(a):
        return jnp.concatenate([a * mask for mask in own_head], axis=0)

    def merge(a):
        total = a[:ROWS]
        for h in range(1, GROUP // HEAD_COLS):
            total = jnp.where(head == h, a[h * ROWS : (h + 1) * ROWS], total)
        return total

    def part(kind, g):
        return pl.ds(kind * WIDTH + g * GROUP, GROUP)

    value = wanted_value()
    found = jnp.int32(0)
    acts = jnp.zeros((ROWS, WIDTH), F32)
    for h in range(DEV_HIST):
        same = (plan_ref[h] == value).astype(jnp.int32)
        found = found + same
        acts = jnp.where(same == 1, events_ref[h].astype(F32), acts)
    acts = jnp.where(found > 0, acts, other_ref[...].astype(F32))

    for l in range(LAYERS):
        average = row_mean(acts)
        centred = acts - average
        rstd = lax.rsqrt(row_mean(centred * centred) + 1e-6)
        normed = centred * rstd
        normed_s[l] = normed
        rstd_s[l] = jnp.broadcast_to(rstd, (ROWS, 128))
        for c in range(2):
            piece = weights.at[l, pl.ds(c * half, half)]
            pltpu.make_async_copy(piece, piece, sems.at[l, c]).wait()
        pltpu.make_async_copy(tables.at[l], tables.at[l], table_sem.at[l]).wait()
        table = tables[l].astype(F32)
        table = table[0:4] + table[4:8] + table[8:12]
        bias = []
        for g in range(GROUPS):
            tiles = [jnp.broadcast_to(table[p : p + 1], (ROWS, 128)) for p in (2 * g, 2 * g + 1)]
            bias.append(jnp.concatenate([pltpu.roll(t, 0, 1, stride=1, stride_axis=0) for t in tiles], axis=1))
        normed_b = normed.astype(BF)
        for kind in range(4):
            cols = pl.ds(kind * WIDTH, WIDTH)
            pre = mm(normed_b, weights[l, :, cols])
            gated = sigmoid(pre)
            silu = pre * gated
            proj_s[l, :, cols] = silu.astype(BF)
            dsilu_s[l, :, cols] = gated + silu * (1.0 - gated)
        keys = [block_diagonal(proj_s[l, :, part(3, g)]) for g in range(GROUPS)]
        values = [block_diagonal(proj_s[l, :, part(1, g)]) for g in range(GROUPS)]
        scores = [mm(proj_s[l, :, part(2, g)], keys[g], NT) * 0.125 + bias[g] for g in range(GROUPS)]
        outs = []
        for g in range(GROUPS):
            gated = sigmoid(scores[g])
            silu = scores[g] * gated
            att = jnp.where(allowed, silu, 0.0).astype(BF)
            att_s[l, g] = att
            datt_s[l, g] = jnp.where(allowed, gated + silu * (1.0 - gated), 0.0) * 0.125
            outs.append(mm(att, values[g]))
        mixed = jnp.concatenate(outs, axis=1)
        centred = mixed - row_mean(mixed)
        rstd = lax.rsqrt(row_mean(centred * centred) + 1e-6)
        norm_o = centred * rstd
        norm_o_s[l] = norm_o
        rstd_o_s[l] = jnp.broadcast_to(rstd, (ROWS, 128))
        branch = (norm_o * proj_s[l, :, pl.ds(0, WIDTH)].astype(F32)).astype(BF)
        out_ref[l, 64:128, :] = branch
        acts = (acts + mm(branch, weights[l, :, pl.ds(4 * WIDTH, WIDTH)])).astype(BF).astype(F32)

    last = iota((ROWS, WIDTH), 0) == count[:, 0:1] - 1
    state = jnp.sum(jnp.where(last, acts, 0.0), axis=0, keepdims=True)
    for q in range(LAYERS):
        quarter = jnp.broadcast_to(state[:, 128 * q : 128 * q + 128], (16, 128))
        out_ref[q, 192:208, :] = jnp.concatenate([quarter] * 4, axis=1).astype(BF)
    seed = jnp.concatenate([cot_ref[q].astype(F32)[0:1] for q in range(LAYERS)], axis=1)
    cot = jnp.where(last, jnp.broadcast_to(seed, (ROWS, WIDTH)), 0.0).astype(BF)

    for l in reversed(range(LAYERS)):
        out_ref[l, 128:192, :] = cot
        d_branch = mm(cot, weights[l, :, pl.ds(4 * WIDTH, WIDTH)], NT).astype(BF).astype(F32)
        norm_o = norm_o_s[l]
        d_gate = (d_branch * norm_o).astype(BF)
        d_norm = d_branch * proj_s[l, :, pl.ds(0, WIDTH)].astype(F32)
        d_mixed = rstd_o_s[l][:, 0:1] * (d_norm - row_mean(d_norm) - norm_o * row_mean(d_norm * norm_o))
        d_mixed = d_mixed.astype(BF)
        d_outs = [d_mixed[:, g * GROUP : (g + 1) * GROUP] for g in range(GROUPS)]
        d_atts = [mm(d_outs[g], block_diagonal(proj_s[l, :, part(1, g)]), NT) for g in range(GROUPS)]
        d_value = [merge(mm(att_s[l, g], d_outs[g], TN)) for g in range(GROUPS)]
        d_scores = [(d_atts[g].astype(BF).astype(F32) * datt_s[l, g]).astype(BF) for g in range(GROUPS)]
        d_query = [mm(d_scores[g], block_diagonal(proj_s[l, :, part(3, g)])) for g in range(GROUPS)]
        d_key = [merge(mm(d_scores[g], proj_s[l, :, part(2, g)], TN)) for g in range(GROUPS)]
        d_normed = jnp.zeros((ROWS, WIDTH), F32)
        for kind, pieces in enumerate(([d_gate], d_value, d_query, d_key)):
            cols = pl.ds(kind * WIDTH, WIDTH)
            whole = pieces[0] if len(pieces) == 1 else jnp.concatenate(pieces, axis=1)
            d_pre = whole.astype(BF).astype(F32) * dsilu_s[l, :, cols]
            d_normed = d_normed + mm(d_pre.astype(BF), weights[l, :, cols], NT)
        d_normed = d_normed.astype(BF).astype(F32)
        normed = normed_s[l]
        d_in = rstd_s[l][:, 0:1] * (d_normed - row_mean(d_normed) - normed * row_mean(d_normed * normed))
        cot = (d_in + cot.astype(F32)).astype(BF)
        out_ref[l, 0:64, :] = cot


def gradient_kernel(own_rows, got_ref, grads_ref, keep_ref, send_ref):
    core = lax.axis_index("core")
    for t in range(LAYERS):
        grads_ref[t] = got_ref[t, 0:64, :]
    branch = jnp.concatenate([got_ref[t, 64:128, :] for t in range(LAYERS)], axis=0)
    cot = jnp.concatenate([got_ref[t, 128:192, :] for t in range(LAYERS)], axis=0)
    half = WIDTH // 2
    to, source = iota((WIDTH, WIDTH), 1), iota((WIDTH, WIDTH), 0)
    side = jnp.where(to < half, core, 1 - core)
    within = jnp.where(to < half, to, to - half)
    wanted = (within // own_rows) * (2 * own_rows) + side * own_rows + within % own_rows
    order = (source == wanted).astype(F32).astype(BF)
    ordered = mm(branch, order).astype(BF)
    keep_ref[...] = mm(ordered[:, :half], cot, TN)
    send_ref[0:half, :] = mm(ordered[:, half:], cot, TN).astype(BF)
    states = [got_ref[t, 192:208, 0:128] for t in range(LAYERS)]
    send_ref[half : half + 16, :] = jnp.concatenate(states, axis=1)


def packing_kernel(own_rows, keep_ref, send_ref, got_ref, out_ref):
    half = WIDTH // 2
    core = lax.axis_index("core")
    own = send_ref[half : half + 16, :].astype(F32)[0:1]
    other = got_ref[half : half + 16, :].astype(F32)[0:1]
    first = jnp.where(core == 0, own, other)
    second = jnp.where(core == 0, other, own)
    at = iota((half, half), 0) % own_rows
    states = jnp.zeros((half, half), F32)
    for r, quarter in enumerate((first[:, :half], first[:, half:], second[:, :half], second[:, half:])):
        states = jnp.where(at == r, quarter, states)
    out_ref[:, 0:WIDTH] = (keep_ref[...] + got_ref[0:half, :].astype(F32)).astype(BF)
    out_ref[:, WIDTH : WIDTH + half] = states.astype(BF)


def result_kernel(got_ref, hot_ref, served_ref, weight_ref):
    rows = got_ref.shape[0]
    own_rows = weight_ref.shape[0]
    lead = max(16, own_rows)
    pick = (iota((lead, rows), 1) % own_rows == iota((lead, rows), 0)).astype(F32).astype(BF)
    weight_ref[...] = mm(pick, got_ref[:, 0:WIDTH])[0:own_rows]
    served = jnp.zeros((16, 128), F32)
    for h in range(DEV_HIST):
        at = WIDTH + 128 * (h % 2)
        served = served + mm(hot_ref[h], got_ref[:, at : at + 128])
    served_ref[...] = served[0:SLOTS].astype(BF)


def shape(dims, dtype):
    return jax.ShapeDtypeStruct(dims, dtype)


def call(kernel, outs, scratch=(), in_specs=None, out_specs=None, limit=48):
    specs = {} if in_specs is None else {"in_specs": in_specs}
    specs |= {} if out_specs is None else {"out_specs": out_specs}
    return pl.pallas_call(
        kernel,
        out_shape=outs,
        scratch_shapes=scratch,
        **specs,
        compiler_params=pltpu.CompilerParams(vmem_limit_bytes=limit * 1024 * 1024),
    )


def body(events, lengths, balance_plan, routes, w_uvqk, w_out, rel_bias, state_cotangent):
    n_z, n_y, n_core = (lax.axis_size(a) for a in DP)
    n_dp = n_z * n_y * n_core
    chips = n_z * n_y
    own_rows = WIDTH // n_dp
    half = WIDTH // 2

    any_spec, vmem = pl.BlockSpec(memory_space=pl.ANY), pl.BlockSpec(memory_space=pltpu.VMEM)
    smem = pl.BlockSpec(memory_space=pltpu.SMEM)
    with jax.named_scope("packing"):
        first, second, outgoing, facts = call(
            packing_start,
            (
                shape((half + 16, 5 * WIDTH), BF),
                shape((half, 5 * WIDTH), BF),
                shape((ROWS, WIDTH), BF),
                shape((n_dp, 2, (SLOTS + 2) * 64), BF),
            ),
            scratch=[
                pltpu.SMEM((DEV_HIST,), jnp.int32),
                pltpu.SMEM((DEV_HIST,), jnp.int32),
                pltpu.SMEM((DEV_HIST,), jnp.int32),
                pltpu.VMEM((8, ROWS), F32),
                pltpu.VMEM((SLOTS, 128), BF),
                pltpu.SemaphoreType.DMA((14,)),
            ],
            in_specs=[any_spec] * 8,
            limit=58,
        )(balance_plan, routes.reshape(DEV_HIST), lengths, w_uvqk, w_out, events, rel_bias, state_cotangent)

    with jax.named_scope("section_weights"):
        ring = [(s * 2, (s - 1) % LAYERS * 2) for s in range(LAYERS)]
        ring += [(s * 2 + 1, (s + 1) % LAYERS * 2 + 1) for s in range(LAYERS)]
        swap = [(0, 1), (1, 0)]
        near_a = lax.ppermute(first, ("segment", "core"), ring)
        near_b = lax.ppermute(second, ("segment", "core"), ring)

    with jax.named_scope("events"):
        other_events = lax.ppermute(outgoing, "z", [(i, (i + n_z // 2) % n_z) for i in range(n_z)])

    with jax.named_scope("routing"):
        facts = lax.all_to_all(facts, DP, 0, 0, tiled=True)
        near_a, other_events, facts = lax.optimization_barrier((near_a, other_events, facts))
        near_b, facts = lax.optimization_barrier((near_b, facts))
        facts = facts.reshape(n_dp, (SLOTS + 2) * 128)

    with jax.named_scope("section_weights"):
        far_a = lax.ppermute(near_a, ("segment", "core"), ring)
        swap_a = lax.ppermute(near_a, "core", swap)
        swap_b = lax.ppermute(near_b, "core", swap)

    with jax.named_scope("routing"):
        seeds, hot, count = call(
            functools.partial(routing_kernel, own_rows),
            (
                shape((LAYERS, 16, 128), BF),
                shape((DEV_HIST, 16, half), BF),
                shape((ROWS, 128), jnp.int32),
            ),
        )(facts)
        seeds = lax.all_to_all(seeds, "segment", 0, 0, tiled=True)
        far_a, swap_a, swap_b, seeds = lax.optimization_barrier((far_a, swap_a, swap_b, seeds))
    with jax.named_scope("section_weights"):
        far_b = lax.ppermute(far_a, "core", swap)

    with jax.named_scope("layers"):
        message = call(
            layers_kernel,
            shape((LAYERS, MSG, WIDTH), BF),
            scratch=[
                pltpu.VMEM((LAYERS, WIDTH, 5 * WIDTH), BF),
                pltpu.VMEM((LAYERS, 16, 128), BF),
                pltpu.VMEM((LAYERS, ROWS, 4 * WIDTH), BF),
                pltpu.VMEM((LAYERS, ROWS, 4 * WIDTH), F32),
                pltpu.VMEM((LAYERS, ROWS, WIDTH), F32),
                pltpu.VMEM((LAYERS, ROWS, 128), F32),
                pltpu.VMEM((LAYERS, ROWS, WIDTH), F32),
                pltpu.VMEM((LAYERS, ROWS, 128), F32),
                pltpu.VMEM((LAYERS, GROUPS, ROWS, GROUP), BF),
                pltpu.VMEM((LAYERS, GROUPS, ROWS, GROUP), F32),
                pltpu.SemaphoreType.DMA((LAYERS, 2)),
                pltpu.SemaphoreType.DMA((LAYERS,)),
            ],
            in_specs=[smem] + [vmem] * 4 + [any_spec] * 9,
            limit=28,
        )(
            balance_plan, events, other_events, count, seeds,
            first, w_uvqk, w_out, near_a, near_b, swap_a, swap_b, far_a, far_b,
        )

    with jax.named_scope("section_exchange"):
        arrived = lax.all_to_all(message, "segment", 0, 0, tiled=True)
    with jax.named_scope("weight_gradient"):
        grads, keep, send = call(
            functools.partial(gradient_kernel, own_rows),
            (
                shape((LAYERS, ROWS, WIDTH), BF),
                shape((half, WIDTH), F32),
                shape((half + 16, WIDTH), BF),
            ),
        )(arrived)
        partner = lax.ppermute(send, "core", swap)
        blocks = call(
            functools.partial(packing_kernel, own_rows),
            shape((half, WIDTH + half), BF),
        )(keep, send, partner)
        blocks = blocks.reshape(chips, own_rows, WIDTH + half)
        blocks = lax.all_to_all(blocks, ("z", "y"), 0, 0, tiled=True)
        served, weight = call(
            result_kernel,
            (shape((SLOTS, 128), BF), shape((own_rows, WIDTH), F32)),
        )(blocks.reshape(half, WIDTH + half), hot)
    return served[None], grads[None], weight[None]


def solution(mesh):
    devices = mesh.devices
    n_segment, n_dp = devices.shape
    side = 1
    while side * side * 2 < n_dp:
        side *= 2
    fine = Mesh(
        devices.reshape(n_segment, n_dp // (2 * side), side, 2), ("segment",) + DP
    )
    return jax.shard_map(
        body,
        mesh=fine,
        in_specs=(
            P(DP, None, None),
            P(DP),
            P(DP),
            P(DP, None),
            P("segment", None, None),
            P("segment", None, None),
            P("segment", None, None),
            P(DP, None, "segment"),
        ),
        out_specs=(
            P(DP, None, "segment"),
            P("segment", DP, None, None),
            P("segment", DP, None),
        ),
        check_vma=False,
    )
```

```python
import functools

import jax
import jax.numpy as jnp
from jax import lax
from jax.experimental import pallas as pl
from jax.experimental.pallas import tpu as pltpu
from jax.sharding import Mesh, PartitionSpec as P

BF = jnp.bfloat16
F32 = jnp.float32
DP = ("z", "y", "core")
DEV_HIST = 4
ROWS = 64
WIDTH = 512
HEAD_COLS = 64
GROUP = 256
GROUPS = WIDTH // GROUP
LAYERS = 4
SLOTS = 8
MSG = 208
NN = (((1,), (0,)), ((), ()))
NT = (((1,), (1,)), ((), ()))
TN = (((0,), (0,)), ((), ()))


def mm(a, b, dims=NN):
    return lax.dot_general(a, b, dims, preferred_element_type=F32)


def iota(shape, dim):
    return lax.broadcasted_iota(jnp.int32, shape, dim)


def row_mean(a):
    return jnp.mean(a, axis=-1, keepdims=True)


def sigmoid(a):
    return 0.5 * jnp.tanh(0.5 * a) + 0.5


def dp_place():
    ny, nc = lax.axis_size("y"), lax.axis_size("core")
    return (lax.axis_index("z") * ny + lax.axis_index("y")) * nc + lax.axis_index("core")


def wanted_value():
    upper = (lax.axis_index("z") >= lax.axis_size("z") // 2).astype(jnp.int32)
    return upper * DEV_HIST + lax.axis_index("segment")


def weights_kernel(w_in_ref, w_out_ref, first_ref, second_ref, sems):
    core = lax.axis_index("core")
    half = WIDTH // 2
    copies = []
    for side, dest in ((core, first_ref), (1 - core, second_ref)):
        for part in range(2):
            rows = pl.ds(pl.multiple_of(side * half + part * (half // 2), half // 2), half // 2)
            to = pl.ds(part * (half // 2), half // 2)
            copies.append((w_in_ref.at[0, rows], dest.at[to, pl.ds(0, 4 * WIDTH)]))
            copies.append((w_out_ref.at[0, rows], dest.at[to, pl.ds(4 * WIDTH, WIDTH)]))
    copies = [pltpu.make_async_copy(*c, sems.at[n]) for n, c in enumerate(copies)]
    for c in copies:
        c.start()
    for c in copies:
        c.wait()


def bias_rows(bias):
    high = bias.astype(BF).astype(F32)
    middle = (bias - high).astype(BF).astype(F32)
    low = bias - high - middle
    pieces = jnp.concatenate([high, middle, low, jnp.zeros((8, ROWS), F32)]).astype(BF)
    row, head = iota((16, 32), 0), iota((16, 32), 1)
    even = (row // 4) * 8 + 2 * (row % 4)
    used = row < 12
    pick_even = (used & (head == even)).astype(F32).astype(BF)
    pick_odd = (used & (head == even + 1)).astype(F32).astype(BF)
    distance, place = iota((ROWS, 128), 0), iota((ROWS, 128), 1)
    to_even = (place == (128 - distance) % 128).astype(F32).astype(BF)
    to_odd = (place == ROWS - distance).astype(F32).astype(BF)
    return mm(mm(pick_even, pieces).astype(BF), to_even) + mm(mm(pick_odd, pieces).astype(BF), to_odd)


def facts_kernel(
    plan_ref, routes_ref, lengths_ref, events_ref, cot_ref, outgoing_ref, facts_ref,
    plan, routes, lengths, cot_s, sems,
):
    small = [(plan_ref, plan), (routes_ref, routes), (lengths_ref, lengths), (cot_ref.at[0], cot_s)]
    small = [pltpu.make_async_copy(*c, sems.at[n]) for n, c in enumerate(small)]
    for c in small:
        c.start()
    for c in small:
        c.wait()
    partner_value = DEV_HIST + 2 * lax.axis_index("segment") - wanted_value()
    chosen = jnp.int32(0)
    for h in range(DEV_HIST):
        chosen = chosen + jnp.where(plan[h] == partner_value, h, 0)
    copy = pltpu.make_async_copy(events_ref.at[chosen], outgoing_ref, sems.at[len(small)])
    copy.start()
    lane = iota((1, 128), 1)
    facts = jnp.zeros((1, 128), F32)
    for j, ref in enumerate((routes, plan, lengths)):
        for h in range(DEV_HIST):
            facts = jnp.where(lane == 4 * j + h, ref[h].astype(F32), facts)
    cot = cot_s[...].astype(F32)
    blocks = [cot[k : k + 1] for k in range(SLOTS)] + [facts, jnp.zeros((1, 128), F32)]
    lines = [jnp.concatenate(blocks[k : k + 5], axis=1) for k in (0, 5)]
    facts_ref[...] = jnp.broadcast_to(jnp.concatenate(lines).astype(BF)[None], facts_ref.shape)
    copy.wait()


def routing_kernel(own_rows, table_ref, bias_ref, seeds_ref, hot_ref, count_ref):
    n_dp = table_ref.shape[0]
    hist = n_dp * DEV_HIST
    me = dp_place()
    facts = table_ref[:, SLOTS * 128 : SLOTS * 128 + 128]
    spread = mm(facts, (iota((128, hist), 0) == iota((128, hist), 1) % DEV_HIST).astype(F32).astype(BF))
    own = iota((n_dp, hist), 1) // DEV_HIST == iota((n_dp, hist), 0)
    routes = jnp.sum(jnp.where(own, spread, 0.0), axis=0, keepdims=True)

    routes_wide = jnp.broadcast_to(routes, (16, hist))
    history, mine = iota((16, hist), 1), me * DEV_HIST + iota((16, hist), 0)
    route = jnp.sum(jnp.where(history == mine, routes_wide, 0.0), axis=1, keepdims=True)
    before = (routes_wide == route) & (history < mine)
    slot = jnp.sum(before.astype(F32), axis=1, keepdims=True)
    source = iota((16, n_dp), 1).astype(F32)
    seeds = jnp.zeros((16, 128), F32)
    for k in range(SLOTS):
        pick = jnp.where((source == route) & (slot == float(k)), 1.0, 0.0).astype(BF)
        seeds = seeds + mm(pick, table_ref[:, 128 * k : 128 * k + 128])
    bias = bias_rows(bias_ref[0]).astype(BF)
    for q in range(LAYERS):
        seeds_ref[q, 0:16, :] = jnp.broadcast_to(seeds[q : q + 1], (16, 128)).astype(BF)
        seeds_ref[q, 16:32, :] = bias

    hit = jnp.broadcast_to((routes == me.astype(F32)).astype(F32), (16, hist))
    earlier = (iota((hist, hist), 0) < iota((hist, hist), 1)).astype(F32).astype(BF)
    place_of = mm(hit.astype(BF), earlier)
    hot = jnp.where(place_of == iota((16, hist), 0).astype(F32), hit, 0.0).astype(BF)
    total = hot_ref.shape[2]
    place, history = iota((hist, total), 1), iota((hist, total), 0)
    chip = place // own_rows
    within = place - chip * own_rows
    first = (chip * 2 + within // 2) * DEV_HIST
    for h in range(DEV_HIST):
        valid = (within < 4) & (within % 2 == h // 2)
        move = jnp.where(valid & (history == first + h), 1.0, 0.0).astype(BF)
        hot_ref[h] = mm(hot, move).astype(BF)

    other = lax.rem(me + n_dp // 2, n_dp)
    known = facts.astype(F32)
    ahead = pltpu.roll(known, 124, 1)
    row, lane = iota((n_dp, 128), 0), iota((n_dp, 128), 1)
    fits = ((row == me) | (row == other)) & (lane >= 4) & (lane < 8)
    fits = fits & (known == wanted_value().astype(F32))
    length = jnp.sum(jnp.where(fits, ahead, 0.0), axis=1, keepdims=True)
    length = jnp.sum(length, axis=0, keepdims=True)
    count_ref[...] = jnp.broadcast_to(length, count_ref.shape).astype(jnp.int32)


def layers_kernel(
    plan_ref, events_ref, other_ref, count_ref, cot_ref,
    w_in_ref, w_out_ref, near_a, near_b, swap_a, swap_b, far_a, far_b,
    out_ref,
    weights, proj_s, dsilu_s, normed_s, rstd_s, norm_o_s, rstd_o_s, att_s, datt_s, sems,
):
    half = WIDTH // 2
    segment, core = lax.axis_index("segment"), lax.axis_index("core")
    near = lax.rem(segment + 1 + 2 * core, LAYERS)
    swap = lax.rem(segment + 3 + 2 * core, LAYERS)
    far = lax.rem(segment + 2, LAYERS)
    held = (
        (near, near_a, core, near_b, 1 - core),
        (swap, swap_a, 1 - core, swap_b, core),
        (far, far_a, core, far_b, 1 - core),
    )
    for l in range(LAYERS):

        @pl.when(segment == l)
        def _():
            for at in range(2):
                rows = pl.ds(at * half, half)
                for piece, cols in ((w_in_ref, pl.ds(0, 4 * WIDTH)), (w_out_ref, pl.ds(4 * WIDTH, WIDTH))):
                    pltpu.make_async_copy(piece.at[0, rows], weights.at[l, rows, cols], sems.at[l, at]).start()

        for slot, one, side, two, other_side in held:

            @pl.when(slot == l)
            def _():
                for piece, at in ((one, side), (two, other_side)):
                    rows = pl.ds(pl.multiple_of(at * half, half), half)
                    pltpu.make_async_copy(piece, weights.at[l, rows], sems.at[l, at]).start()

    row, lane = iota((ROWS, GROUP), 0), iota((ROWS, GROUP), 1)
    head = lane // HEAD_COLS
    column = lane - head * HEAD_COLS
    own_head = [(head == h).astype(F32).astype(BF) for h in range(GROUP // HEAD_COLS)]
    count = count_ref[...]
    allowed = (column <= row) & (column < count[:, 0:1])

    def block_diagonal(a):
        return jnp.concatenate([a * mask for mask in own_head], axis=0)

    def merge(a):
        total = a[:ROWS]
        for h in range(1, GROUP // HEAD_COLS):
            total = jnp.where(head == h, a[h * ROWS : (h + 1) * ROWS], total)
        return total

    def part(kind, g):
        return pl.ds(kind * WIDTH + g * GROUP, GROUP)

    value = wanted_value()
    found = jnp.int32(0)
    acts = jnp.zeros((ROWS, WIDTH), F32)
    for h in range(DEV_HIST):
        same = (plan_ref[h] == value).astype(jnp.int32)
        found = found + same
        acts = jnp.where(same == 1, events_ref[h].astype(F32), acts)
    acts = jnp.where(found > 0, acts, other_ref[...].astype(F32))

    for l in range(LAYERS):
        average = row_mean(acts)
        centred = acts - average
        rstd = lax.rsqrt(row_mean(centred * centred) + 1e-6)
        normed = centred * rstd
        normed_s[l] = normed
        rstd_s[l] = jnp.broadcast_to(rstd, (ROWS, 128))
        for c in range(2):
            piece = weights.at[l, pl.ds(c * half, half)]
            pltpu.make_async_copy(piece, piece, sems.at[l, c]).wait()
        table = cot_ref[l, 16:32, :].astype(F32)
        table = table[0:4] + table[4:8] + table[8:12]
        bias = []
        for g in range(GROUPS):
            tiles = [jnp.broadcast_to(table[p : p + 1], (ROWS, 128)) for p in (2 * g, 2 * g + 1)]
            bias.append(jnp.concatenate([pltpu.roll(t, 0, 1, stride=1, stride_axis=0) for t in tiles], axis=1))
        normed_b = normed.astype(BF)
        for kind in range(4):
            cols = pl.ds(kind * WIDTH, WIDTH)
            pre = mm(normed_b, weights[l, :, cols])
            gated = sigmoid(pre)
            silu = pre * gated
            proj_s[l, :, cols] = silu.astype(BF)
            dsilu_s[l, :, cols] = gated + silu * (1.0 - gated)
        keys = [block_diagonal(proj_s[l, :, part(3, g)]) for g in range(GROUPS)]
        values = [block_diagonal(proj_s[l, :, part(1, g)]) for g in range(GROUPS)]
        scores = [mm(proj_s[l, :, part(2, g)], keys[g], NT) * 0.125 + bias[g] for g in range(GROUPS)]
        outs = []
        for g in range(GROUPS):
            gated = sigmoid(scores[g])
            silu = scores[g] * gated
            att = jnp.where(allowed, silu, 0.0).astype(BF)
            att_s[l, g] = att
            datt_s[l, g] = jnp.where(allowed, gated + silu * (1.0 - gated), 0.0) * 0.125
            outs.append(mm(att, values[g]))
        mixed = jnp.concatenate(outs, axis=1)
        centred = mixed - row_mean(mixed)
        rstd = lax.rsqrt(row_mean(centred * centred) + 1e-6)
        norm_o = centred * rstd
        norm_o_s[l] = norm_o
        rstd_o_s[l] = jnp.broadcast_to(rstd, (ROWS, 128))
        branch = (norm_o * proj_s[l, :, pl.ds(0, WIDTH)].astype(F32)).astype(BF)
        out_ref[l, 64:128, :] = branch
        acts = (acts + mm(branch, weights[l, :, pl.ds(4 * WIDTH, WIDTH)])).astype(BF).astype(F32)

    last = iota((ROWS, WIDTH), 0) == count[:, 0:1] - 1
    state = jnp.sum(jnp.where(last, acts, 0.0), axis=0, keepdims=True)
    for q in range(LAYERS):
        quarter = jnp.broadcast_to(state[:, 128 * q : 128 * q + 128], (16, 128))
        out_ref[q, 192:208, :] = jnp.concatenate([quarter] * 4, axis=1).astype(BF)
    seed = jnp.concatenate([cot_ref[q, 0:16, :].astype(F32)[0:1] for q in range(LAYERS)], axis=1)
    cot = jnp.where(last, jnp.broadcast_to(seed, (ROWS, WIDTH)), 0.0).astype(BF)

    for l in reversed(range(LAYERS)):
        out_ref[l, 128:192, :] = cot
        d_branch = mm(cot, weights[l, :, pl.ds(4 * WIDTH, WIDTH)], NT).astype(BF).astype(F32)
        norm_o = norm_o_s[l]
        d_gate = (d_branch * norm_o).astype(BF)
        d_norm = d_branch * proj_s[l, :, pl.ds(0, WIDTH)].astype(F32)
        d_mixed = rstd_o_s[l][:, 0:1] * (d_norm - row_mean(d_norm) - norm_o * row_mean(d_norm * norm_o))
        d_mixed = d_mixed.astype(BF)
        d_outs = [d_mixed[:, g * GROUP : (g + 1) * GROUP] for g in range(GROUPS)]
        d_atts = [mm(d_outs[g], block_diagonal(proj_s[l, :, part(1, g)]), NT) for g in range(GROUPS)]
        d_value = [merge(mm(att_s[l, g], d_outs[g], TN)) for g in range(GROUPS)]
        d_scores = [(d_atts[g].astype(BF).astype(F32) * datt_s[l, g]).astype(BF) for g in range(GROUPS)]
        d_query = [mm(d_scores[g], block_diagonal(proj_s[l, :, part(3, g)])) for g in range(GROUPS)]
        d_key = [merge(mm(d_scores[g], proj_s[l, :, part(2, g)], TN)) for g in range(GROUPS)]
        d_normed = jnp.zeros((ROWS, WIDTH), F32)
        for kind, pieces in enumerate(([d_gate], d_value, d_query, d_key)):
            cols = pl.ds(kind * WIDTH, WIDTH)
            whole = pieces[0] if len(pieces) == 1 else jnp.concatenate(pieces, axis=1)
            d_pre = whole.astype(BF).astype(F32) * dsilu_s[l, :, cols]
            d_normed = d_normed + mm(d_pre.astype(BF), weights[l, :, cols], NT)
        d_normed = d_normed.astype(BF).astype(F32)
        normed = normed_s[l]
        d_in = rstd_s[l][:, 0:1] * (d_normed - row_mean(d_normed) - normed * row_mean(d_normed * normed))
        cot = (d_in + cot.astype(F32)).astype(BF)
        out_ref[l, 0:64, :] = cot


def gradient_kernel(own_rows, got_ref, grads_ref, keep_ref, send_ref):
    core = lax.axis_index("core")
    for t in range(LAYERS):
        grads_ref[t] = got_ref[t, 0:64, :]
    branch = jnp.concatenate([got_ref[t, 64:128, :] for t in range(LAYERS)], axis=0)
    cot = jnp.concatenate([got_ref[t, 128:192, :] for t in range(LAYERS)], axis=0)
    half = WIDTH // 2
    to, source = iota((WIDTH, WIDTH), 1), iota((WIDTH, WIDTH), 0)
    side = jnp.where(to < half, core, 1 - core)
    within = jnp.where(to < half, to, to - half)
    wanted = (within // own_rows) * (2 * own_rows) + side * own_rows + within % own_rows
    order = (source == wanted).astype(F32).astype(BF)
    ordered = mm(branch, order).astype(BF)
    keep_ref[...] = mm(ordered[:, :half], cot, TN)
    send_ref[0:half, :] = mm(ordered[:, half:], cot, TN).astype(BF)
    states = [got_ref[t, 192:208, 0:128] for t in range(LAYERS)]
    send_ref[half : half + 16, :] = jnp.concatenate(states, axis=1)


def packing_kernel(own_rows, keep_ref, send_ref, got_ref, out_ref):
    half = WIDTH // 2
    core = lax.axis_index("core")
    own = send_ref[half : half + 16, :].astype(F32)[0:1]
    other = got_ref[half : half + 16, :].astype(F32)[0:1]
    first = jnp.where(core == 0, own, other)
    second = jnp.where(core == 0, other, own)
    at = iota((half, half), 0) % own_rows
    states = jnp.zeros((half, half), F32)
    for r, quarter in enumerate((first[:, :half], first[:, half:], second[:, :half], second[:, half:])):
        states = jnp.where(at == r, quarter, states)
    out_ref[:, 0:WIDTH] = (keep_ref[...] + got_ref[0:half, :].astype(F32)).astype(BF)
    out_ref[:, WIDTH : WIDTH + half] = states.astype(BF)


def result_kernel(got_ref, hot_ref, served_ref, weight_ref):
    rows = got_ref.shape[0]
    own_rows = weight_ref.shape[0]
    lead = max(16, own_rows)
    pick = (iota((lead, rows), 1) % own_rows == iota((lead, rows), 0)).astype(F32).astype(BF)
    weight_ref[...] = mm(pick, got_ref[:, 0:WIDTH])[0:own_rows]
    served = jnp.zeros((16, 128), F32)
    for h in range(DEV_HIST):
        at = WIDTH + 128 * (h % 2)
        served = served + mm(hot_ref[h], got_ref[:, at : at + 128])
    served_ref[...] = served[0:SLOTS].astype(BF)


def shape(dims, dtype):
    return jax.ShapeDtypeStruct(dims, dtype)


def call(kernel, outs, scratch=(), in_specs=None, out_specs=None, limit=48):
    specs = {} if in_specs is None else {"in_specs": in_specs}
    specs |= {} if out_specs is None else {"out_specs": out_specs}
    return pl.pallas_call(
        kernel,
        out_shape=outs,
        scratch_shapes=scratch,
        **specs,
        compiler_params=pltpu.CompilerParams(vmem_limit_bytes=limit * 1024 * 1024),
    )


def body(events, lengths, balance_plan, routes, w_uvqk, w_out, rel_bias, state_cotangent):
    n_z, n_y, n_core = (lax.axis_size(a) for a in DP)
    n_dp = n_z * n_y * n_core
    chips = n_z * n_y
    own_rows = WIDTH // n_dp
    half = WIDTH // 2

    any_spec, vmem = pl.BlockSpec(memory_space=pl.ANY), pl.BlockSpec(memory_space=pltpu.VMEM)
    smem = pl.BlockSpec(memory_space=pltpu.SMEM)
    with jax.named_scope("packing"):
        first, second = call(
            weights_kernel,
            (shape((half, 5 * WIDTH), BF), shape((half, 5 * WIDTH), BF)),
            scratch=[pltpu.SemaphoreType.DMA((8,))],
            in_specs=[any_spec] * 2,
            limit=58,
        )(w_uvqk, w_out)
        outgoing, facts = call(
            facts_kernel,
            (shape((ROWS, WIDTH), BF), shape((n_dp, 2, (SLOTS + 2) * 64), BF)),
            scratch=[
                pltpu.SMEM((DEV_HIST,), jnp.int32),
                pltpu.SMEM((DEV_HIST,), jnp.int32),
                pltpu.SMEM((DEV_HIST,), jnp.int32),
                pltpu.VMEM((SLOTS, 128), BF),
                pltpu.SemaphoreType.DMA((5,)),
            ],
            in_specs=[any_spec] * 5,
            limit=58,
        )(balance_plan, routes.reshape(DEV_HIST), lengths, events, state_cotangent)

    with jax.named_scope("section_weights"):
        ring = [(s * 2, (s - 1) % LAYERS * 2) for s in range(LAYERS)]
        ring += [(s * 2 + 1, (s + 1) % LAYERS * 2 + 1) for s in range(LAYERS)]
        swap = [(0, 1), (1, 0)]
        near_a = lax.ppermute(first, ("segment", "core"), ring)
        near_b = lax.ppermute(second, ("segment", "core"), ring)

    with jax.named_scope("events"):
        other_events = lax.ppermute(outgoing, "z", [(i, (i + n_z // 2) % n_z) for i in range(n_z)])

    with jax.named_scope("routing"):
        facts = lax.all_to_all(facts, DP, 0, 0, tiled=True)
        near_a, other_events, facts = lax.optimization_barrier((near_a, other_events, facts))
        near_b, facts = lax.optimization_barrier((near_b, facts))
        facts = facts.reshape(n_dp, (SLOTS + 2) * 128)

    with jax.named_scope("section_weights"):
        far_a = lax.ppermute(near_a, ("segment", "core"), ring)
        swap_a = lax.ppermute(near_a, "core", swap)
        swap_b = lax.ppermute(near_b, "core", swap)

    with jax.named_scope("routing"):
        seeds, hot, count = call(
            functools.partial(routing_kernel, own_rows),
            (
                shape((LAYERS, 32, 128), BF),
                shape((DEV_HIST, 16, half), BF),
                shape((ROWS, 128), jnp.int32),
            ),
        )(facts, rel_bias)
        seeds = lax.all_to_all(seeds, "segment", 0, 0, tiled=True)
        far_a, swap_a, swap_b, seeds = lax.optimization_barrier((far_a, swap_a, swap_b, seeds))
    with jax.named_scope("section_weights"):
        far_b = lax.ppermute(far_a, "core", swap)

    with jax.named_scope("layers"):
        message = call(
            layers_kernel,
            shape((LAYERS, MSG, WIDTH), BF),
            scratch=[
                pltpu.VMEM((LAYERS, WIDTH, 5 * WIDTH), BF),
                pltpu.VMEM((LAYERS, ROWS, 4 * WIDTH), BF),
                pltpu.VMEM((LAYERS, ROWS, 4 * WIDTH), F32),
                pltpu.VMEM((LAYERS, ROWS, WIDTH), F32),
                pltpu.VMEM((LAYERS, ROWS, 128), F32),
                pltpu.VMEM((LAYERS, ROWS, WIDTH), F32),
                pltpu.VMEM((LAYERS, ROWS, 128), F32),
                pltpu.VMEM((LAYERS, GROUPS, ROWS, GROUP), BF),
                pltpu.VMEM((LAYERS, GROUPS, ROWS, GROUP), F32),
                pltpu.SemaphoreType.DMA((LAYERS, 2)),
            ],
            in_specs=[smem] + [vmem] * 4 + [any_spec] * 8,
            limit=28,
        )(
            balance_plan, events, other_events, count, seeds,
            w_uvqk, w_out, near_a, near_b, swap_a, swap_b, far_a, far_b,
        )

    with jax.named_scope("section_exchange"):
        arrived = lax.all_to_all(message, "segment", 0, 0, tiled=True)
    with jax.named_scope("weight_gradient"):
        grads, keep, send = call(
            functools.partial(gradient_kernel, own_rows),
            (
                shape((LAYERS, ROWS, WIDTH), BF),
                shape((half, WIDTH), F32),
                shape((half + 16, WIDTH), BF),
            ),
        )(arrived)
        partner = lax.ppermute(send, "core", swap)
        blocks = call(
            functools.partial(packing_kernel, own_rows),
            shape((half, WIDTH + half), BF),
        )(keep, send, partner)
        blocks = blocks.reshape(chips, own_rows, WIDTH + half)
        blocks = lax.all_to_all(blocks, ("z", "y"), 0, 0, tiled=True)
        served, weight = call(
            result_kernel,
            (shape((SLOTS, 128), BF), shape((own_rows, WIDTH), F32)),
        )(blocks.reshape(half, WIDTH + half), hot)
    return served[None], grads[None], weight[None]


def solution(mesh):
    devices = mesh.devices
    n_segment, n_dp = devices.shape
    side = 1
    while side * side * 2 < n_dp:
        side *= 2
    fine = Mesh(
        devices.reshape(n_segment, n_dp // (2 * side), side, 2), ("segment",) + DP
    )
    return jax.shard_map(
        body,
        mesh=fine,
        in_specs=(
            P(DP, None, None),
            P(DP),
            P(DP),
            P(DP, None),
            P("segment", None, None),
            P("segment", None, None),
            P("segment", None, None),
            P(DP, None, "segment"),
        ),
        out_specs=(
            P(DP, None, "segment"),
            P("segment", DP, None, None),
            P("segment", DP, None),
        ),
        check_vma=False,
    )
```

```python
import functools

import jax
import jax.numpy as jnp
from jax import lax
from jax.experimental import pallas as pl
from jax.experimental.pallas import tpu as pltpu
from jax.sharding import Mesh, PartitionSpec as P

BF = jnp.bfloat16
F32 = jnp.float32
DP = ("z", "y", "core")
DEV_HIST = 4
ROWS = 64
WIDTH = 512
HEAD_COLS = 64
GROUP = 256
GROUPS = WIDTH // GROUP
LAYERS = 4
SLOTS = 8
MSG = 208
NN = (((1,), (0,)), ((), ()))
NT = (((1,), (1,)), ((), ()))
TN = (((0,), (0,)), ((), ()))


def mm(a, b, dims=NN):
    return lax.dot_general(a, b, dims, preferred_element_type=F32)


def iota(shape, dim):
    return lax.broadcasted_iota(jnp.int32, shape, dim)


def row_mean(a):
    return jnp.mean(a, axis=-1, keepdims=True)


def sigmoid(a):
    return 0.5 * jnp.tanh(0.5 * a) + 0.5


def dp_place():
    ny, nc = lax.axis_size("y"), lax.axis_size("core")
    return (lax.axis_index("z") * ny + lax.axis_index("y")) * nc + lax.axis_index("core")


def wanted_value():
    upper = (lax.axis_index("z") >= lax.axis_size("z") // 2).astype(jnp.int32)
    return upper * DEV_HIST + lax.axis_index("segment")


def weight_copies(w_in_ref, w_out_ref, dest_ref, start, sems):
    rows = dest_ref.shape[0] // 2
    copies = []
    for part in range(2):
        source = pl.ds(pl.multiple_of(start + part * rows, rows), rows)
        to = pl.ds(part * rows, rows)
        copies.append((w_in_ref.at[0, source], dest_ref.at[to, pl.ds(0, 4 * WIDTH)]))
        copies.append((w_out_ref.at[0, source], dest_ref.at[to, pl.ds(4 * WIDTH, WIDTH)]))
    return [pltpu.make_async_copy(*c, sems.at[n]) for n, c in enumerate(copies)]


def weights_kernel(w_in_ref, w_out_ref, first_ref, sems):
    copies = weight_copies(w_in_ref, w_out_ref, first_ref, lax.axis_index("core") * (WIDTH // 2), sems)
    for c in copies:
        c.start()
    for c in copies:
        c.wait()


def bias_rows(bias):
    high = bias.astype(BF).astype(F32)
    middle = (bias - high).astype(BF).astype(F32)
    low = bias - high - middle
    pieces = jnp.concatenate([high, middle, low, jnp.zeros((8, ROWS), F32)]).astype(BF)
    row, head = iota((16, 32), 0), iota((16, 32), 1)
    even = (row // 4) * 8 + 2 * (row % 4)
    used = row < 12
    pick_even = (used & (head == even)).astype(F32).astype(BF)
    pick_odd = (used & (head == even + 1)).astype(F32).astype(BF)
    distance, place = iota((ROWS, 128), 0), iota((ROWS, 128), 1)
    to_even = (place == (128 - distance) % 128).astype(F32).astype(BF)
    to_odd = (place == ROWS - distance).astype(F32).astype(BF)
    return mm(mm(pick_even, pieces).astype(BF), to_even) + mm(mm(pick_odd, pieces).astype(BF), to_odd)


def facts_kernel(
    plan_ref, routes_ref, lengths_ref, events_ref, cot_ref, w_in_ref, w_out_ref, second_ref, outgoing_ref, facts_ref,
    plan, routes, lengths, cot_s, sems, weight_sems,
):
    quarter = WIDTH // 4
    start = (1 - lax.axis_index("core")) * (2 * quarter) + lax.rem(lax.axis_index("y"), 2) * quarter
    copies = weight_copies(w_in_ref, w_out_ref, second_ref, start, weight_sems)
    small = [(plan_ref, plan), (routes_ref, routes), (lengths_ref, lengths), (cot_ref.at[0], cot_s)]
    small = [pltpu.make_async_copy(*c, sems.at[n]) for n, c in enumerate(small)]
    for c in small + copies:
        c.start()
    for c in small:
        c.wait()
    partner_value = DEV_HIST + 2 * lax.axis_index("segment") - wanted_value()
    chosen = jnp.int32(0)
    for h in range(DEV_HIST):
        chosen = chosen + jnp.where(plan[h] == partner_value, h, 0)
    copy = pltpu.make_async_copy(events_ref.at[chosen], outgoing_ref, sems.at[len(small)])
    copy.start()
    lane = iota((1, 128), 1)
    facts = jnp.zeros((1, 128), F32)
    for j, ref in enumerate((routes, plan, lengths)):
        for h in range(DEV_HIST):
            facts = jnp.where(lane == 4 * j + h, ref[h].astype(F32), facts)
    cot = cot_s[...].astype(F32)
    blocks = [cot[k : k + 1] for k in range(SLOTS)] + [facts, jnp.zeros((1, 128), F32)]
    lines = [jnp.concatenate(blocks[k : k + 5], axis=1) for k in (0, 5)]
    facts_ref[...] = jnp.broadcast_to(jnp.concatenate(lines).astype(BF)[None], facts_ref.shape)
    for c in copies:
        c.wait()
    copy.wait()


def routing_kernel(own_rows, table_ref, bias_ref, seeds_ref, hot_ref, count_ref):
    n_dp = table_ref.shape[0]
    hist = n_dp * DEV_HIST
    me = dp_place()
    facts = table_ref[:, SLOTS * 128 : SLOTS * 128 + 128]
    spread = mm(facts, (iota((128, hist), 0) == iota((128, hist), 1) % DEV_HIST).astype(F32).astype(BF))
    own = iota((n_dp, hist), 1) // DEV_HIST == iota((n_dp, hist), 0)
    routes = jnp.sum(jnp.where(own, spread, 0.0), axis=0, keepdims=True)

    routes_wide = jnp.broadcast_to(routes, (16, hist))
    history, mine = iota((16, hist), 1), me * DEV_HIST + iota((16, hist), 0)
    route = jnp.sum(jnp.where(history == mine, routes_wide, 0.0), axis=1, keepdims=True)
    before = (routes_wide == route) & (history < mine)
    slot = jnp.sum(before.astype(F32), axis=1, keepdims=True)
    source = iota((16, n_dp), 1).astype(F32)
    seeds = jnp.zeros((16, 128), F32)
    for k in range(SLOTS):
        pick = jnp.where((source == route) & (slot == float(k)), 1.0, 0.0).astype(BF)
        seeds = seeds + mm(pick, table_ref[:, 128 * k : 128 * k + 128])
    bias = bias_rows(bias_ref[0]).astype(BF)
    for q in range(LAYERS):
        seeds_ref[q, 0:16, :] = jnp.broadcast_to(seeds[q : q + 1], (16, 128)).astype(BF)
        seeds_ref[q, 16:32, :] = bias

    hit = jnp.broadcast_to((routes == me.astype(F32)).astype(F32), (16, hist))
    earlier = (iota((hist, hist), 0) < iota((hist, hist), 1)).astype(F32).astype(BF)
    place_of = mm(hit.astype(BF), earlier)
    hot = jnp.where(place_of == iota((16, hist), 0).astype(F32), hit, 0.0).astype(BF)
    total = hot_ref.shape[2]
    place, history = iota((hist, total), 1), iota((hist, total), 0)
    chip = place // own_rows
    within = place - chip * own_rows
    first = (chip * 2 + within // 2) * DEV_HIST
    for h in range(DEV_HIST):
        valid = (within < 4) & (within % 2 == h // 2)
        move = jnp.where(valid & (history == first + h), 1.0, 0.0).astype(BF)
        hot_ref[h] = mm(hot, move).astype(BF)

    other = lax.rem(me + n_dp // 2, n_dp)
    known = facts.astype(F32)
    ahead = pltpu.roll(known, 124, 1)
    row, lane = iota((n_dp, 128), 0), iota((n_dp, 128), 1)
    fits = ((row == me) | (row == other)) & (lane >= 4) & (lane < 8)
    fits = fits & (known == wanted_value().astype(F32))
    length = jnp.sum(jnp.where(fits, ahead, 0.0), axis=1, keepdims=True)
    length = jnp.sum(length, axis=0, keepdims=True)
    count_ref[...] = jnp.broadcast_to(length, count_ref.shape).astype(jnp.int32)


def layers_kernel(
    plan_ref, events_ref, other_ref, count_ref, cot_ref,
    w_in_ref, w_out_ref, near_a, near_b, near_y, swap_a, swap_b, swap_y, far_a, far_b,
    out_ref,
    weights, proj_s, dsilu_s, normed_s, rstd_s, norm_o_s, rstd_o_s, att_s, datt_s, sems,
):
    half = WIDTH // 2
    segment, core = lax.axis_index("segment"), lax.axis_index("core")
    near = lax.rem(segment + 1 + 2 * core, LAYERS)
    swap = lax.rem(segment + 3 + 2 * core, LAYERS)
    far = lax.rem(segment + 2, LAYERS)
    quarter = half // 2
    side = lax.rem(lax.axis_index("y"), 2) * quarter
    mine, others = core * half, (1 - core) * half
    held = (
        (near, ((near_a, mine, core), (near_b, others + side, 1 - core), (near_y, others + quarter - side, 1 - core))),
        (swap, ((swap_a, others, 1 - core), (swap_b, mine + side, core), (swap_y, mine + quarter - side, core))),
        (far, ((far_a, mine, core), (far_b, others, 1 - core))),
    )
    for l in range(LAYERS):

        @pl.when(segment == l)
        def _():
            for at in range(2):
                rows = pl.ds(at * half, half)
                for piece, cols in ((w_in_ref, pl.ds(0, 4 * WIDTH)), (w_out_ref, pl.ds(4 * WIDTH, WIDTH))):
                    pltpu.make_async_copy(piece.at[0, rows], weights.at[l, rows, cols], sems.at[l, at]).start()

        for slot, pieces in held:

            @pl.when(slot == l)
            def _():
                for piece, at, which in pieces:
                    rows = pl.ds(pl.multiple_of(at, quarter), piece.shape[0])
                    pltpu.make_async_copy(piece, weights.at[l, rows], sems.at[l, which]).start()

    row, lane = iota((ROWS, GROUP), 0), iota((ROWS, GROUP), 1)
    head = lane // HEAD_COLS
    column = lane - head * HEAD_COLS
    own_head = [(head == h).astype(F32).astype(BF) for h in range(GROUP // HEAD_COLS)]
    count = count_ref[...]
    allowed = (column <= row) & (column < count[:, 0:1])

    def block_diagonal(a):
        return jnp.concatenate([a * mask for mask in own_head], axis=0)

    def merge(a):
        total = a[:ROWS]
        for h in range(1, GROUP // HEAD_COLS):
            total = jnp.where(head == h, a[h * ROWS : (h + 1) * ROWS], total)
        return total

    def part(kind, g):
        return pl.ds(kind * WIDTH + g * GROUP, GROUP)

    value = wanted_value()
    found = jnp.int32(0)
    acts = jnp.zeros((ROWS, WIDTH), F32)
    for h in range(DEV_HIST):
        same = (plan_ref[h] == value).astype(jnp.int32)
        found = found + same
        acts = jnp.where(same == 1, events_ref[h].astype(F32), acts)
    acts = jnp.where(found > 0, acts, other_ref[...].astype(F32))

    for l in range(LAYERS):
        average = row_mean(acts)
        centred = acts - average
        rstd = lax.rsqrt(row_mean(centred * centred) + 1e-6)
        normed = centred * rstd
        normed_s[l] = normed
        rstd_s[l] = jnp.broadcast_to(rstd, (ROWS, 128))
        for c in range(2):
            piece = weights.at[l, pl.ds(c * half, half)]
            pltpu.make_async_copy(piece, piece, sems.at[l, c]).wait()
        table = cot_ref[l, 16:32, :].astype(F32)
        table = table[0:4] + table[4:8] + table[8:12]
        bias = []
        for g in range(GROUPS):
            tiles = [jnp.broadcast_to(table[p : p + 1], (ROWS, 128)) for p in (2 * g, 2 * g + 1)]
            bias.append(jnp.concatenate([pltpu.roll(t, 0, 1, stride=1, stride_axis=0) for t in tiles], axis=1))
        normed_b = normed.astype(BF)
        for kind in range(4):
            cols = pl.ds(kind * WIDTH, WIDTH)
            pre = mm(normed_b, weights[l, :, cols])
            gated = sigmoid(pre)
            silu = pre * gated
            proj_s[l, :, cols] = silu.astype(BF)
            dsilu_s[l, :, cols] = gated + silu * (1.0 - gated)
        keys = [block_diagonal(proj_s[l, :, part(3, g)]) for g in range(GROUPS)]
        values = [block_diagonal(proj_s[l, :, part(1, g)]) for g in range(GROUPS)]
        scores = [mm(proj_s[l, :, part(2, g)], keys[g], NT) * 0.125 + bias[g] for g in range(GROUPS)]
        outs = []
        for g in range(GROUPS):
            gated = sigmoid(scores[g])
            silu = scores[g] * gated
            att = jnp.where(allowed, silu, 0.0).astype(BF)
            att_s[l, g] = att
            datt_s[l, g] = jnp.where(allowed, gated + silu * (1.0 - gated), 0.0) * 0.125
            outs.append(mm(att, values[g]))
        mixed = jnp.concatenate(outs, axis=1)
        centred = mixed - row_mean(mixed)
        rstd = lax.rsqrt(row_mean(centred * centred) + 1e-6)
        norm_o = centred * rstd
        norm_o_s[l] = norm_o
        rstd_o_s[l] = jnp.broadcast_to(rstd, (ROWS, 128))
        branch = (norm_o * proj_s[l, :, pl.ds(0, WIDTH)].astype(F32)).astype(BF)
        out_ref[l, 64:128, :] = branch
        acts = (acts + mm(branch, weights[l, :, pl.ds(4 * WIDTH, WIDTH)])).astype(BF).astype(F32)

    last = iota((ROWS, WIDTH), 0) == count[:, 0:1] - 1
    state = jnp.sum(jnp.where(last, acts, 0.0), axis=0, keepdims=True)
    for q in range(LAYERS):
        quarter = jnp.broadcast_to(state[:, 128 * q : 128 * q + 128], (16, 128))
        out_ref[q, 192:208, :] = jnp.concatenate([quarter] * 4, axis=1).astype(BF)
    seed = jnp.concatenate([cot_ref[q, 0:16, :].astype(F32)[0:1] for q in range(LAYERS)], axis=1)
    cot = jnp.where(last, jnp.broadcast_to(seed, (ROWS, WIDTH)), 0.0).astype(BF)

    for l in reversed(range(LAYERS)):
        out_ref[l, 128:192, :] = cot
        d_branch = mm(cot, weights[l, :, pl.ds(4 * WIDTH, WIDTH)], NT).astype(BF).astype(F32)
        norm_o = norm_o_s[l]
        d_gate = (d_branch * norm_o).astype(BF)
        d_norm = d_branch * proj_s[l, :, pl.ds(0, WIDTH)].astype(F32)
        d_mixed = rstd_o_s[l][:, 0:1] * (d_norm - row_mean(d_norm) - norm_o * row_mean(d_norm * norm_o))
        d_mixed = d_mixed.astype(BF)
        d_outs = [d_mixed[:, g * GROUP : (g + 1) * GROUP] for g in range(GROUPS)]
        d_atts = [mm(d_outs[g], block_diagonal(proj_s[l, :, part(1, g)]), NT) for g in range(GROUPS)]
        d_value = [merge(mm(att_s[l, g], d_outs[g], TN)) for g in range(GROUPS)]
        d_scores = [(d_atts[g].astype(BF).astype(F32) * datt_s[l, g]).astype(BF) for g in range(GROUPS)]
        d_query = [mm(d_scores[g], block_diagonal(proj_s[l, :, part(3, g)])) for g in range(GROUPS)]
        d_key = [merge(mm(d_scores[g], proj_s[l, :, part(2, g)], TN)) for g in range(GROUPS)]
        d_normed = jnp.zeros((ROWS, WIDTH), F32)
        for kind, pieces in enumerate(([d_gate], d_value, d_query, d_key)):
            cols = pl.ds(kind * WIDTH, WIDTH)
            whole = pieces[0] if len(pieces) == 1 else jnp.concatenate(pieces, axis=1)
            d_pre = whole.astype(BF).astype(F32) * dsilu_s[l, :, cols]
            d_normed = d_normed + mm(d_pre.astype(BF), weights[l, :, cols], NT)
        d_normed = d_normed.astype(BF).astype(F32)
        normed = normed_s[l]
        d_in = rstd_s[l][:, 0:1] * (d_normed - row_mean(d_normed) - normed * row_mean(d_normed * normed))
        cot = (d_in + cot.astype(F32)).astype(BF)
        out_ref[l, 0:64, :] = cot


def gradient_kernel(own_rows, got_ref, grads_ref, keep_ref, send_ref):
    core = lax.axis_index("core")
    for t in range(LAYERS):
        grads_ref[t] = got_ref[t, 0:64, :]
    branch = jnp.concatenate([got_ref[t, 64:128, :] for t in range(LAYERS)], axis=0)
    cot = jnp.concatenate([got_ref[t, 128:192, :] for t in range(LAYERS)], axis=0)
    half = WIDTH // 2
    to, source = iota((WIDTH, WIDTH), 1), iota((WIDTH, WIDTH), 0)
    side = jnp.where(to < half, core, 1 - core)
    within = jnp.where(to < half, to, to - half)
    wanted = (within // own_rows) * (2 * own_rows) + side * own_rows + within % own_rows
    order = (source == wanted).astype(F32).astype(BF)
    ordered = mm(branch, order).astype(BF)
    keep_ref[...] = mm(ordered[:, :half], cot, TN)
    send_ref[0:half, :] = mm(ordered[:, half:], cot, TN).astype(BF)
    states = [got_ref[t, 192:208, 0:128] for t in range(LAYERS)]
    send_ref[half : half + 16, :] = jnp.concatenate(states, axis=1)


def packing_kernel(own_rows, keep_ref, send_ref, got_ref, out_ref):
    half = WIDTH // 2
    core = lax.axis_index("core")
    own = send_ref[half : half + 16, :].astype(F32)[0:1]
    other = got_ref[half : half + 16, :].astype(F32)[0:1]
    first = jnp.where(core == 0, own, other)
    second = jnp.where(core == 0, other, own)
    at = iota((half, half), 0) % own_rows
    states = jnp.zeros((half, half), F32)
    for r, quarter in enumerate((first[:, :half], first[:, half:], second[:, :half], second[:, half:])):
        states = jnp.where(at == r, quarter, states)
    out_ref[:, 0:WIDTH] = (keep_ref[...] + got_ref[0:half, :].astype(F32)).astype(BF)
    out_ref[:, WIDTH : WIDTH + half] = states.astype(BF)


def result_kernel(got_ref, hot_ref, served_ref, weight_ref):
    rows = got_ref.shape[0]
    own_rows = weight_ref.shape[0]
    lead = max(16, own_rows)
    pick = (iota((lead, rows), 1) % own_rows == iota((lead, rows), 0)).astype(F32).astype(BF)
    weight_ref[...] = mm(pick, got_ref[:, 0:WIDTH])[0:own_rows]
    served = jnp.zeros((16, 128), F32)
    for h in range(DEV_HIST):
        at = WIDTH + 128 * (h % 2)
        served = served + mm(hot_ref[h], got_ref[:, at : at + 128])
    served_ref[...] = served[0:SLOTS].astype(BF)


def shape(dims, dtype):
    return jax.ShapeDtypeStruct(dims, dtype)


def call(kernel, outs, scratch=(), in_specs=None, out_specs=None, limit=24):
    specs = {} if in_specs is None else {"in_specs": in_specs}
    specs |= {} if out_specs is None else {"out_specs": out_specs}
    return pl.pallas_call(
        kernel,
        out_shape=outs,
        scratch_shapes=scratch,
        **specs,
        compiler_params=pltpu.CompilerParams(vmem_limit_bytes=limit * 1024 * 1024),
    )


def body(events, lengths, balance_plan, routes, w_uvqk, w_out, rel_bias, state_cotangent):
    n_z, n_y, n_core = (lax.axis_size(a) for a in DP)
    n_dp = n_z * n_y * n_core
    chips = n_z * n_y
    own_rows = WIDTH // n_dp
    half = WIDTH // 2

    any_spec, vmem = pl.BlockSpec(memory_space=pl.ANY), pl.BlockSpec(memory_space=pltpu.VMEM)
    smem = pl.BlockSpec(memory_space=pltpu.SMEM)
    with jax.named_scope("packing"):
        first = call(
            weights_kernel,
            shape((half, 5 * WIDTH), BF),
            scratch=[pltpu.SemaphoreType.DMA((4,))],
            in_specs=[any_spec] * 2,
            limit=58,
        )(w_uvqk, w_out)
        second, outgoing, facts = call(
            facts_kernel,
            (
                shape((half // 2, 5 * WIDTH), BF),
                shape((ROWS, WIDTH), BF),
                shape((n_dp, 2, (SLOTS + 2) * 64), BF),
            ),
            scratch=[
                pltpu.SMEM((DEV_HIST,), jnp.int32),
                pltpu.SMEM((DEV_HIST,), jnp.int32),
                pltpu.SMEM((DEV_HIST,), jnp.int32),
                pltpu.VMEM((SLOTS, 128), BF),
                pltpu.SemaphoreType.DMA((5,)),
                pltpu.SemaphoreType.DMA((4,)),
            ],
            in_specs=[any_spec] * 7,
            limit=58,
        )(balance_plan, routes.reshape(DEV_HIST), lengths, events, state_cotangent, w_uvqk, w_out)

    with jax.named_scope("section_weights"):
        ring = [(s * 2, (s - 1) % LAYERS * 2) for s in range(LAYERS)]
        ring += [(s * 2 + 1, (s + 1) % LAYERS * 2 + 1) for s in range(LAYERS)]
        swap = [(0, 1), (1, 0)]
        near_a = lax.ppermute(first, ("segment", "core"), ring)
        near_b = lax.ppermute(second, ("segment", "core"), ring)

    with jax.named_scope("events"):
        other_events = lax.ppermute(outgoing, "z", [(i, (i + n_z // 2) % n_z) for i in range(n_z)])

    with jax.named_scope("routing"):
        facts = lax.all_to_all(facts, DP, 0, 0, tiled=True)
        near_a, near_b, other_events, facts = lax.optimization_barrier((near_a, near_b, other_events, facts))
        facts = facts.reshape(n_dp, (SLOTS + 2) * 128)

    with jax.named_scope("section_weights"):
        near_y = lax.ppermute(near_b, "y", [(i, i ^ 1) for i in range(n_y)])
        far_a = lax.ppermute(near_a, ("segment", "core"), ring)
        swap_a = lax.ppermute(near_a, "core", swap)
        swap_b = lax.ppermute(near_b, "core", swap)

    with jax.named_scope("routing"):
        seeds, hot, count = call(
            functools.partial(routing_kernel, own_rows),
            (
                shape((LAYERS, 32, 128), BF),
                shape((DEV_HIST, 16, half), BF),
                shape((ROWS, 128), jnp.int32),
            ),
        )(facts, rel_bias)
        seeds = lax.all_to_all(seeds, "segment", 0, 0, tiled=True)
        far_a, swap_a, swap_b, near_y, seeds = lax.optimization_barrier((far_a, swap_a, swap_b, near_y, seeds))
    with jax.named_scope("section_weights"):
        swap_y = lax.ppermute(near_y, "core", swap)
        far_b = lax.ppermute(far_a, "core", swap)

    with jax.named_scope("layers"):
        message = call(
            layers_kernel,
            shape((LAYERS, MSG, WIDTH), BF),
            scratch=[
                pltpu.VMEM((LAYERS, WIDTH, 5 * WIDTH), BF),
                pltpu.VMEM((LAYERS, ROWS, 4 * WIDTH), BF),
                pltpu.VMEM((LAYERS, ROWS, 4 * WIDTH), F32),
                pltpu.VMEM((LAYERS, ROWS, WIDTH), F32),
                pltpu.VMEM((LAYERS, ROWS, 128), F32),
                pltpu.VMEM((LAYERS, ROWS, WIDTH), F32),
                pltpu.VMEM((LAYERS, ROWS, 128), F32),
                pltpu.VMEM((LAYERS, GROUPS, ROWS, GROUP), BF),
                pltpu.VMEM((LAYERS, GROUPS, ROWS, GROUP), F32),
                pltpu.SemaphoreType.DMA((LAYERS, 2)),
            ],
            in_specs=[smem] + [vmem] * 4 + [any_spec] * 10,
            limit=28,
        )(
            balance_plan, events, other_events, count, seeds,
            w_uvqk, w_out, near_a, near_b, near_y, swap_a, swap_b, swap_y, far_a, far_b,
        )

    with jax.named_scope("section_exchange"):
        arrived = lax.all_to_all(message, "segment", 0, 0, tiled=True)
    with jax.named_scope("weight_gradient"):
        grads, keep, send = call(
            functools.partial(gradient_kernel, own_rows),
            (
                shape((LAYERS, ROWS, WIDTH), BF),
                shape((half, WIDTH), F32),
                shape((half + 16, WIDTH), BF),
            ),
        )(arrived)
        partner = lax.ppermute(send, "core", swap)
        blocks = call(
            functools.partial(packing_kernel, own_rows),
            shape((half, WIDTH + half), BF),
        )(keep, send, partner)
        blocks = blocks.reshape(chips, own_rows, WIDTH + half)
        blocks = lax.all_to_all(blocks, ("z", "y"), 0, 0, tiled=True)
        served, weight = call(
            result_kernel,
            (shape((SLOTS, 128), BF), shape((own_rows, WIDTH), F32)),
        )(blocks.reshape(half, WIDTH + half), hot)
    return served[None], grads[None], weight[None]


def solution(mesh):
    devices = mesh.devices
    n_segment, n_dp = devices.shape
    side = 1
    while side * side * 2 < n_dp:
        side *= 2
    fine = Mesh(
        devices.reshape(n_segment, n_dp // (2 * side), side, 2), ("segment",) + DP
    )
    return jax.shard_map(
        body,
        mesh=fine,
        in_specs=(
            P(DP, None, None),
            P(DP),
            P(DP),
            P(DP, None),
            P("segment", None, None),
            P("segment", None, None),
            P("segment", None, None),
            P(DP, None, "segment"),
        ),
        out_specs=(
            P(DP, None, "segment"),
            P("segment", DP, None, None),
            P("segment", DP, None),
        ),
        check_vma=False,
    )
```

```python
import functools

import jax
import jax.numpy as jnp
from jax import lax
from jax.experimental import pallas as pl
from jax.experimental.pallas import tpu as pltpu
from jax.sharding import Mesh, PartitionSpec as P

BF = jnp.bfloat16
F32 = jnp.float32
DP = ("z", "y", "core")
DEV_HIST = 4
ROWS = 64
WIDTH = 512
HEAD_COLS = 64
GROUP = 256
GROUPS = WIDTH // GROUP
LAYERS = 4
SLOTS = 8
MSG = 208
NN = (((1,), (0,)), ((), ()))
NT = (((1,), (1,)), ((), ()))
TN = (((0,), (0,)), ((), ()))


def mm(a, b, dims=NN):
    return lax.dot_general(a, b, dims, preferred_element_type=F32)


def iota(shape, dim):
    return lax.broadcasted_iota(jnp.int32, shape, dim)


def row_mean(a):
    return jnp.mean(a, axis=-1, keepdims=True)


def sigmoid(a):
    return 0.5 * jnp.tanh(0.5 * a) + 0.5


def dp_place():
    ny, nc = lax.axis_size("y"), lax.axis_size("core")
    return (lax.axis_index("z") * ny + lax.axis_index("y")) * nc + lax.axis_index("core")


def wanted_value():
    upper = (lax.axis_index("z") >= lax.axis_size("z") // 2).astype(jnp.int32)
    return upper * DEV_HIST + lax.axis_index("segment")


def weight_copies(w_in_ref, w_out_ref, dest_ref, start, sems):
    rows = dest_ref.shape[0] // 2
    copies = []
    for part in range(2):
        source = pl.ds(pl.multiple_of(start + part * rows, rows), rows)
        to = pl.ds(part * rows, rows)
        copies.append((w_in_ref.at[0, source], dest_ref.at[to, pl.ds(0, 4 * WIDTH)]))
        copies.append((w_out_ref.at[0, source], dest_ref.at[to, pl.ds(4 * WIDTH, WIDTH)]))
    return [pltpu.make_async_copy(*c, sems.at[n]) for n, c in enumerate(copies)]


def weights_kernel(w_in_ref, w_out_ref, first_ref, sems):
    copies = weight_copies(w_in_ref, w_out_ref, first_ref, lax.axis_index("core") * (WIDTH // 2), sems)
    for c in copies:
        c.start()
    for c in copies:
        c.wait()


def bias_rows(bias):
    high = bias.astype(BF).astype(F32)
    middle = (bias - high).astype(BF).astype(F32)
    low = bias - high - middle
    pieces = jnp.concatenate([high, middle, low, jnp.zeros((8, ROWS), F32)]).astype(BF)
    row, head = iota((16, 32), 0), iota((16, 32), 1)
    even = (row // 4) * 8 + 2 * (row % 4)
    used = row < 12
    pick_even = (used & (head == even)).astype(F32).astype(BF)
    pick_odd = (used & (head == even + 1)).astype(F32).astype(BF)
    distance, place = iota((ROWS, 128), 0), iota((ROWS, 128), 1)
    to_even = (place == (128 - distance) % 128).astype(F32).astype(BF)
    to_odd = (place == ROWS - distance).astype(F32).astype(BF)
    return mm(mm(pick_even, pieces).astype(BF), to_even) + mm(mm(pick_odd, pieces).astype(BF), to_odd)


def facts_kernel(
    plan_ref, routes_ref, lengths_ref, events_ref, cot_ref, w_in_ref, w_out_ref, second_ref, outgoing_ref, facts_ref,
    plan, routes, lengths, cot_s, sems, weight_sems,
):
    start = (1 - lax.axis_index("core")) * (WIDTH // 2)
    copies = weight_copies(w_in_ref, w_out_ref, second_ref, start, weight_sems)
    small = [(plan_ref, plan), (routes_ref, routes), (lengths_ref, lengths), (cot_ref.at[0], cot_s)]
    small = [pltpu.make_async_copy(*c, sems.at[n]) for n, c in enumerate(small)]
    for c in small + copies:
        c.start()
    for c in small:
        c.wait()
    partner_value = DEV_HIST + 2 * lax.axis_index("segment") - wanted_value()
    chosen = jnp.int32(0)
    for h in range(DEV_HIST):
        chosen = chosen + jnp.where(plan[h] == partner_value, h, 0)
    copy = pltpu.make_async_copy(events_ref.at[chosen], outgoing_ref, sems.at[len(small)])
    copy.start()
    lane = iota((1, 128), 1)
    facts = jnp.zeros((1, 128), F32)
    for j, ref in enumerate((routes, plan, lengths)):
        for h in range(DEV_HIST):
            facts = jnp.where(lane == 4 * j + h, ref[h].astype(F32), facts)
    cot = cot_s[...].astype(F32)
    blocks = [cot[k : k + 1] for k in range(SLOTS)] + [facts, jnp.zeros((1, 128), F32)]
    lines = [jnp.concatenate(blocks[k : k + 5], axis=1) for k in (0, 5)]
    facts_ref[...] = jnp.broadcast_to(jnp.concatenate(lines).astype(BF)[None], facts_ref.shape)
    for c in copies:
        c.wait()
    copy.wait()


def routing_kernel(own_rows, table_ref, bias_ref, seeds_ref, hot_ref, count_ref):
    n_dp = table_ref.shape[0]
    hist = n_dp * DEV_HIST
    me = dp_place()
    facts = table_ref[:, SLOTS * 128 : SLOTS * 128 + 128]
    spread = mm(facts, (iota((128, hist), 0) == iota((128, hist), 1) % DEV_HIST).astype(F32).astype(BF))
    own = iota((n_dp, hist), 1) // DEV_HIST == iota((n_dp, hist), 0)
    routes = jnp.sum(jnp.where(own, spread, 0.0), axis=0, keepdims=True)

    routes_wide = jnp.broadcast_to(routes, (16, hist))
    history, mine = iota((16, hist), 1), me * DEV_HIST + iota((16, hist), 0)
    route = jnp.sum(jnp.where(history == mine, routes_wide, 0.0), axis=1, keepdims=True)
    before = (routes_wide == route) & (history < mine)
    slot = jnp.sum(before.astype(F32), axis=1, keepdims=True)
    source = iota((16, n_dp), 1).astype(F32)
    seeds = jnp.zeros((16, 128), F32)
    for k in range(SLOTS):
        pick = jnp.where((source == route) & (slot == float(k)), 1.0, 0.0).astype(BF)
        seeds = seeds + mm(pick, table_ref[:, 128 * k : 128 * k + 128])
    bias = bias_rows(bias_ref[0]).astype(BF)
    for q in range(LAYERS):
        seeds_ref[q, 0:16, :] = jnp.broadcast_to(seeds[q : q + 1], (16, 128)).astype(BF)
        seeds_ref[q, 16:32, :] = bias

    hit = jnp.broadcast_to((routes == me.astype(F32)).astype(F32), (16, hist))
    earlier = (iota((hist, hist), 0) < iota((hist, hist), 1)).astype(F32).astype(BF)
    place_of = mm(hit.astype(BF), earlier)
    hot = jnp.where(place_of == iota((16, hist), 0).astype(F32), hit, 0.0).astype(BF)
    total = hot_ref.shape[2]
    place, history = iota((hist, total), 1), iota((hist, total), 0)
    chip = place // own_rows
    within = place - chip * own_rows
    first = (chip * 2 + within // 2) * DEV_HIST
    for h in range(DEV_HIST):
        valid = (within < 4) & (within % 2 == h // 2)
        move = jnp.where(valid & (history == first + h), 1.0, 0.0).astype(BF)
        hot_ref[h] = mm(hot, move).astype(BF)

    other = lax.rem(me + n_dp // 2, n_dp)
    known = facts.astype(F32)
    ahead = pltpu.roll(known, 124, 1)
    row, lane = iota((n_dp, 128), 0), iota((n_dp, 128), 1)
    fits = ((row == me) | (row == other)) & (lane >= 4) & (lane < 8)
    fits = fits & (known == wanted_value().astype(F32))
    length = jnp.sum(jnp.where(fits, ahead, 0.0), axis=1, keepdims=True)
    length = jnp.sum(length, axis=0, keepdims=True)
    count_ref[...] = jnp.broadcast_to(length, count_ref.shape).astype(jnp.int32)


def layers_kernel(
    plan_ref, events_ref, other_ref, count_ref, cot_ref,
    w_in_ref, w_out_ref, near_a, near_b, swap_a, swap_b, far_a, far_b,
    out_ref,
    weights, proj_s, dsilu_s, normed_s, rstd_s, norm_o_s, rstd_o_s, att_s, datt_s, sems,
):
    half = WIDTH // 2
    segment, core = lax.axis_index("segment"), lax.axis_index("core")
    near = lax.rem(segment + 1 + 2 * core, LAYERS)
    swap = lax.rem(segment + 3 + 2 * core, LAYERS)
    far = lax.rem(segment + 2, LAYERS)
    mine, others = core * half, (1 - core) * half
    held = (
        (near, ((near_a, mine, core), (near_b, others, 1 - core))),
        (swap, ((swap_a, others, 1 - core), (swap_b, mine, core))),
        (far, ((far_a, mine, core), (far_b, others, 1 - core))),
    )
    for l in range(LAYERS):

        @pl.when(segment == l)
        def _():
            for at in range(2):
                rows = pl.ds(at * half, half)
                for piece, cols in ((w_in_ref, pl.ds(0, 4 * WIDTH)), (w_out_ref, pl.ds(4 * WIDTH, WIDTH))):
                    pltpu.make_async_copy(piece.at[0, rows], weights.at[l, rows, cols], sems.at[l, at]).start()

        for slot, pieces in held:

            @pl.when(slot == l)
            def _():
                for piece, at, which in pieces:
                    rows = pl.ds(pl.multiple_of(at, half), half)
                    pltpu.make_async_copy(piece, weights.at[l, rows], sems.at[l, which]).start()

    row, lane = iota((ROWS, GROUP), 0), iota((ROWS, GROUP), 1)
    head = lane // HEAD_COLS
    column = lane - head * HEAD_COLS
    own_head = [(head == h).astype(F32).astype(BF) for h in range(GROUP // HEAD_COLS)]
    count = count_ref[...]
    allowed = (column <= row) & (column < count[:, 0:1])

    def block_diagonal(a):
        return jnp.concatenate([a * mask for mask in own_head], axis=0)

    def merge(a):
        total = a[:ROWS]
        for h in range(1, GROUP // HEAD_COLS):
            total = jnp.where(head == h, a[h * ROWS : (h + 1) * ROWS], total)
        return total

    def part(kind, g):
        return pl.ds(kind * WIDTH + g * GROUP, GROUP)

    value = wanted_value()
    found = jnp.int32(0)
    acts = jnp.zeros((ROWS, WIDTH), F32)
    for h in range(DEV_HIST):
        same = (plan_ref[h] == value).astype(jnp.int32)
        found = found + same
        acts = jnp.where(same == 1, events_ref[h].astype(F32), acts)
    acts = jnp.where(found > 0, acts, other_ref[...].astype(F32))

    for l in range(LAYERS):
        average = row_mean(acts)
        centred = acts - average
        rstd = lax.rsqrt(row_mean(centred * centred) + 1e-6)
        normed = centred * rstd
        normed_s[l] = normed
        rstd_s[l] = jnp.broadcast_to(rstd, (ROWS, 128))
        for c in range(2):
            piece = weights.at[l, pl.ds(c * half, half)]
            pltpu.make_async_copy(piece, piece, sems.at[l, c]).wait()
        table = cot_ref[l, 16:32, :].astype(F32)
        table = table[0:4] + table[4:8] + table[8:12]
        bias = []
        for g in range(GROUPS):
            tiles = [jnp.broadcast_to(table[p : p + 1], (ROWS, 128)) for p in (2 * g, 2 * g + 1)]
            bias.append(jnp.concatenate([pltpu.roll(t, 0, 1, stride=1, stride_axis=0) for t in tiles], axis=1))
        normed_b = normed.astype(BF)
        for kind in range(4):
            cols = pl.ds(kind * WIDTH, WIDTH)
            pre = mm(normed_b, weights[l, :, cols])
            gated = sigmoid(pre)
            silu = pre * gated
            proj_s[l, :, cols] = silu.astype(BF)
            dsilu_s[l, :, cols] = gated + silu * (1.0 - gated)
        keys = [block_diagonal(proj_s[l, :, part(3, g)]) for g in range(GROUPS)]
        values = [block_diagonal(proj_s[l, :, part(1, g)]) for g in range(GROUPS)]
        scores = [mm(proj_s[l, :, part(2, g)], keys[g], NT) * 0.125 + bias[g] for g in range(GROUPS)]
        outs = []
        for g in range(GROUPS):
            gated = sigmoid(scores[g])
            silu = scores[g] * gated
            att = jnp.where(allowed, silu, 0.0).astype(BF)
            att_s[l, g] = att
            datt_s[l, g] = jnp.where(allowed, gated + silu * (1.0 - gated), 0.0) * 0.125
            outs.append(mm(att, values[g]))
        mixed = jnp.concatenate(outs, axis=1)
        centred = mixed - row_mean(mixed)
        rstd = lax.rsqrt(row_mean(centred * centred) + 1e-6)
        norm_o = centred * rstd
        norm_o_s[l] = norm_o
        rstd_o_s[l] = jnp.broadcast_to(rstd, (ROWS, 128))
        branch = (norm_o * proj_s[l, :, pl.ds(0, WIDTH)].astype(F32)).astype(BF)
        out_ref[l, 64:128, :] = branch
        acts = (acts + mm(branch, weights[l, :, pl.ds(4 * WIDTH, WIDTH)])).astype(BF).astype(F32)

    last = iota((ROWS, WIDTH), 0) == count[:, 0:1] - 1
    state = jnp.sum(jnp.where(last, acts, 0.0), axis=0, keepdims=True)
    for q in range(LAYERS):
        quarter = jnp.broadcast_to(state[:, 128 * q : 128 * q + 128], (16, 128))
        out_ref[q, 192:208, :] = jnp.concatenate([quarter] * 4, axis=1).astype(BF)
    seed = jnp.concatenate([cot_ref[q, 0:16, :].astype(F32)[0:1] for q in range(LAYERS)], axis=1)
    cot = jnp.where(last, jnp.broadcast_to(seed, (ROWS, WIDTH)), 0.0).astype(BF)

    for l in reversed(range(LAYERS)):
        out_ref[l, 128:192, :] = cot
        d_branch = mm(cot, weights[l, :, pl.ds(4 * WIDTH, WIDTH)], NT).astype(BF).astype(F32)
        norm_o = norm_o_s[l]
        d_gate = (d_branch * norm_o).astype(BF)
        d_norm = d_branch * proj_s[l, :, pl.ds(0, WIDTH)].astype(F32)
        d_mixed = rstd_o_s[l][:, 0:1] * (d_norm - row_mean(d_norm) - norm_o * row_mean(d_norm * norm_o))
        d_mixed = d_mixed.astype(BF)
        d_outs = [d_mixed[:, g * GROUP : (g + 1) * GROUP] for g in range(GROUPS)]
        d_atts = [mm(d_outs[g], block_diagonal(proj_s[l, :, part(1, g)]), NT) for g in range(GROUPS)]
        d_value = [merge(mm(att_s[l, g], d_outs[g], TN)) for g in range(GROUPS)]
        d_scores = [(d_atts[g].astype(BF).astype(F32) * datt_s[l, g]).astype(BF) for g in range(GROUPS)]
        d_query = [mm(d_scores[g], block_diagonal(proj_s[l, :, part(3, g)])) for g in range(GROUPS)]
        d_key = [merge(mm(d_scores[g], proj_s[l, :, part(2, g)], TN)) for g in range(GROUPS)]
        d_normed = jnp.zeros((ROWS, WIDTH), F32)
        for kind, pieces in enumerate(([d_gate], d_value, d_query, d_key)):
            cols = pl.ds(kind * WIDTH, WIDTH)
            whole = pieces[0] if len(pieces) == 1 else jnp.concatenate(pieces, axis=1)
            d_pre = whole.astype(BF).astype(F32) * dsilu_s[l, :, cols]
            d_normed = d_normed + mm(d_pre.astype(BF), weights[l, :, cols], NT)
        d_normed = d_normed.astype(BF).astype(F32)
        normed = normed_s[l]
        d_in = rstd_s[l][:, 0:1] * (d_normed - row_mean(d_normed) - normed * row_mean(d_normed * normed))
        cot = (d_in + cot.astype(F32)).astype(BF)
        out_ref[l, 0:64, :] = cot


def gradient_kernel(own_rows, got_ref, grads_ref, keep_ref, send_ref):
    core = lax.axis_index("core")
    for t in range(LAYERS):
        grads_ref[t] = got_ref[t, 0:64, :]
    branch = jnp.concatenate([got_ref[t, 64:128, :] for t in range(LAYERS)], axis=0)
    cot = jnp.concatenate([got_ref[t, 128:192, :] for t in range(LAYERS)], axis=0)
    half = WIDTH // 2
    to, source = iota((WIDTH, WIDTH), 1), iota((WIDTH, WIDTH), 0)
    side = jnp.where(to < half, core, 1 - core)
    within = jnp.where(to < half, to, to - half)
    wanted = (within // own_rows) * (2 * own_rows) + side * own_rows + within % own_rows
    order = (source == wanted).astype(F32).astype(BF)
    ordered = mm(branch, order).astype(BF)
    keep_ref[...] = mm(ordered[:, :half], cot, TN)
    send_ref[0:half, :] = mm(ordered[:, half:], cot, TN).astype(BF)
    states = [got_ref[t, 192:208, 0:128] for t in range(LAYERS)]
    send_ref[half : half + 16, :] = jnp.concatenate(states, axis=1)


def packing_kernel(own_rows, keep_ref, send_ref, got_ref, out_ref):
    half = WIDTH // 2
    core = lax.axis_index("core")
    own = send_ref[half : half + 16, :].astype(F32)[0:1]
    other = got_ref[half : half + 16, :].astype(F32)[0:1]
    first = jnp.where(core == 0, own, other)
    second = jnp.where(core == 0, other, own)
    at = iota((half, half), 0) % own_rows
    states = jnp.zeros((half, half), F32)
    for r, quarter in enumerate((first[:, :half], first[:, half:], second[:, :half], second[:, half:])):
        states = jnp.where(at == r, quarter, states)
    out_ref[:, 0:WIDTH] = (keep_ref[...] + got_ref[0:half, :].astype(F32)).astype(BF)
    out_ref[:, WIDTH : WIDTH + half] = states.astype(BF)


def result_kernel(got_ref, hot_ref, served_ref, weight_ref):
    rows = got_ref.shape[0]
    own_rows = weight_ref.shape[0]
    lead = max(16, own_rows)
    pick = (iota((lead, rows), 1) % own_rows == iota((lead, rows), 0)).astype(F32).astype(BF)
    weight_ref[...] = mm(pick, got_ref[:, 0:WIDTH])[0:own_rows]
    served = jnp.zeros((16, 128), F32)
    for h in range(DEV_HIST):
        at = WIDTH + 128 * (h % 2)
        served = served + mm(hot_ref[h], got_ref[:, at : at + 128])
    served_ref[...] = served[0:SLOTS].astype(BF)


def shape(dims, dtype):
    return jax.ShapeDtypeStruct(dims, dtype)


def call(kernel, outs, scratch=(), in_specs=None, out_specs=None, limit=24):
    specs = {} if in_specs is None else {"in_specs": in_specs}
    specs |= {} if out_specs is None else {"out_specs": out_specs}
    return pl.pallas_call(
        kernel,
        out_shape=outs,
        scratch_shapes=scratch,
        **specs,
        compiler_params=pltpu.CompilerParams(vmem_limit_bytes=limit * 1024 * 1024),
    )


def body(events, lengths, balance_plan, routes, w_uvqk, w_out, rel_bias, state_cotangent):
    n_z, n_y, n_core = (lax.axis_size(a) for a in DP)
    n_dp = n_z * n_y * n_core
    chips = n_z * n_y
    own_rows = WIDTH // n_dp
    half = WIDTH // 2

    any_spec, vmem = pl.BlockSpec(memory_space=pl.ANY), pl.BlockSpec(memory_space=pltpu.VMEM)
    smem = pl.BlockSpec(memory_space=pltpu.SMEM)
    with jax.named_scope("packing"):
        first = call(
            weights_kernel,
            shape((half, 5 * WIDTH), BF),
            scratch=[pltpu.SemaphoreType.DMA((4,))],
            in_specs=[any_spec] * 2,
            limit=58,
        )(w_uvqk, w_out)
        second, outgoing, facts = call(
            facts_kernel,
            (
                shape((half, 5 * WIDTH), BF),
                shape((ROWS, WIDTH), BF),
                shape((n_dp, 2, (SLOTS + 2) * 64), BF),
            ),
            scratch=[
                pltpu.SMEM((DEV_HIST,), jnp.int32),
                pltpu.SMEM((DEV_HIST,), jnp.int32),
                pltpu.SMEM((DEV_HIST,), jnp.int32),
                pltpu.VMEM((SLOTS, 128), BF),
                pltpu.SemaphoreType.DMA((5,)),
                pltpu.SemaphoreType.DMA((4,)),
            ],
            in_specs=[any_spec] * 7,
            limit=58,
        )(balance_plan, routes.reshape(DEV_HIST), lengths, events, state_cotangent, w_uvqk, w_out)

    with jax.named_scope("section_weights"):
        ring = [(s * 2, (s - 1) % LAYERS * 2) for s in range(LAYERS)]
        ring += [(s * 2 + 1, (s + 1) % LAYERS * 2 + 1) for s in range(LAYERS)]
        swap = [(0, 1), (1, 0)]
        near_a = lax.ppermute(first, ("segment", "core"), ring)
        near_b = lax.ppermute(second, ("segment", "core"), ring)

    with jax.named_scope("events"):
        other_events = lax.ppermute(outgoing, "z", [(i, (i + n_z // 2) % n_z) for i in range(n_z)])

    with jax.named_scope("routing"):
        facts = lax.all_to_all(facts, DP, 0, 0, tiled=True)
        near_a, other_events, facts = lax.optimization_barrier((near_a, other_events, facts))
        near_b, facts = lax.optimization_barrier((near_b, facts))
        facts = facts.reshape(n_dp, (SLOTS + 2) * 128)

    with jax.named_scope("section_weights"):
        far_a = lax.ppermute(near_a, ("segment", "core"), ring)
        swap_a = lax.ppermute(near_a, "core", swap)
        swap_b = lax.ppermute(near_b, "core", swap)

    with jax.named_scope("routing"):
        seeds, hot, count = call(
            functools.partial(routing_kernel, own_rows),
            (
                shape((LAYERS, 32, 128), BF),
                shape((DEV_HIST, 16, half), BF),
                shape((ROWS, 128), jnp.int32),
            ),
        )(facts, rel_bias)
        seeds = lax.all_to_all(seeds, "segment", 0, 0, tiled=True)
        far_a, swap_b, seeds = lax.optimization_barrier((far_a, swap_b, seeds))
    with jax.named_scope("section_weights"):
        far_b = lax.ppermute(far_a, "core", swap)

    with jax.named_scope("layers"):
        message = call(
            layers_kernel,
            shape((LAYERS, MSG, WIDTH), BF),
            scratch=[
                pltpu.VMEM((LAYERS, WIDTH, 5 * WIDTH), BF),
                pltpu.VMEM((LAYERS, ROWS, 4 * WIDTH), BF),
                pltpu.VMEM((LAYERS, ROWS, 4 * WIDTH), F32),
                pltpu.VMEM((LAYERS, ROWS, WIDTH), F32),
                pltpu.VMEM((LAYERS, ROWS, 128), F32),
                pltpu.VMEM((LAYERS, ROWS, WIDTH), F32),
                pltpu.VMEM((LAYERS, ROWS, 128), F32),
                pltpu.VMEM((LAYERS, GROUPS, ROWS, GROUP), BF),
                pltpu.VMEM((LAYERS, GROUPS, ROWS, GROUP), F32),
                pltpu.SemaphoreType.DMA((LAYERS, 2)),
            ],
            in_specs=[smem] + [vmem] * 4 + [any_spec] * 8,
            limit=28,
        )(
            balance_plan, events, other_events, count, seeds,
            w_uvqk, w_out, near_a, near_b, swap_a, swap_b, far_a, far_b,
        )

    with jax.named_scope("section_exchange"):
        arrived = lax.all_to_all(message, "segment", 0, 0, tiled=True)
    with jax.named_scope("weight_gradient"):
        grads, keep, send = call(
            functools.partial(gradient_kernel, own_rows),
            (
                shape((LAYERS, ROWS, WIDTH), BF),
                shape((half, WIDTH), F32),
                shape((half + 16, WIDTH), BF),
            ),
        )(arrived)
        partner = lax.ppermute(send, "core", swap)
        blocks = call(
            functools.partial(packing_kernel, own_rows),
            shape((half, WIDTH + half), BF),
        )(keep, send, partner)
        blocks = blocks.reshape(chips, own_rows, WIDTH + half)
        blocks = lax.all_to_all(blocks, ("z", "y"), 0, 0, tiled=True)
        served, weight = call(
            result_kernel,
            (shape((SLOTS, 128), BF), shape((own_rows, WIDTH), F32)),
        )(blocks.reshape(half, WIDTH + half), hot)
    return served[None], grads[None], weight[None]


def solution(mesh):
    devices = mesh.devices
    n_segment, n_dp = devices.shape
    side = 1
    while side * side * 2 < n_dp:
        side *= 2
    fine = Mesh(
        devices.reshape(n_segment, n_dp // (2 * side), side, 2), ("segment",) + DP
    )
    return jax.shard_map(
        body,
        mesh=fine,
        in_specs=(
            P(DP, None, None),
            P(DP),
            P(DP),
            P(DP, None),
            P("segment", None, None),
            P("segment", None, None),
            P("segment", None, None),
            P(DP, None, "segment"),
        ),
        out_specs=(
            P(DP, None, "segment"),
            P("segment", DP, None, None),
            P("segment", DP, None),
        ),
        check_vma=False,
    )
```

```python
import functools

import jax
import jax.numpy as jnp
from jax import lax
from jax.experimental import pallas as pl
from jax.experimental.pallas import tpu as pltpu
from jax.sharding import Mesh, PartitionSpec as P

BF = jnp.bfloat16
F32 = jnp.float32
DP = ("z", "y", "core")
DEV_HIST = 4
ROWS = 64
WIDTH = 512
HEAD_COLS = 64
GROUP = 256
GROUPS = WIDTH // GROUP
LAYERS = 4
SLOTS = 8
MSG = 208
NN = (((1,), (0,)), ((), ()))
NT = (((1,), (1,)), ((), ()))
TN = (((0,), (0,)), ((), ()))


def mm(a, b, dims=NN):
    return lax.dot_general(a, b, dims, preferred_element_type=F32)


def iota(shape, dim):
    return lax.broadcasted_iota(jnp.int32, shape, dim)


def row_mean(a):
    return jnp.mean(a, axis=-1, keepdims=True)


def sigmoid(a):
    return 0.5 * jnp.tanh(0.5 * a) + 0.5


def dp_place():
    ny, nc = lax.axis_size("y"), lax.axis_size("core")
    return (lax.axis_index("z") * ny + lax.axis_index("y")) * nc + lax.axis_index("core")


def wanted_value():
    upper = (lax.axis_index("z") >= lax.axis_size("z") // 2).astype(jnp.int32)
    return upper * DEV_HIST + lax.axis_index("segment")


def bias_rows(bias):
    high = bias.astype(BF).astype(F32)
    middle = (bias - high).astype(BF).astype(F32)
    low = bias - high - middle
    pieces = jnp.concatenate([high, middle, low, jnp.zeros((8, ROWS), F32)]).astype(BF)
    row, head = iota((16, 32), 0), iota((16, 32), 1)
    even = (row // 4) * 8 + 2 * (row % 4)
    used = row < 12
    pick_even = (used & (head == even)).astype(F32).astype(BF)
    pick_odd = (used & (head == even + 1)).astype(F32).astype(BF)
    distance, place = iota((ROWS, 128), 0), iota((ROWS, 128), 1)
    to_even = (place == (128 - distance) % 128).astype(F32).astype(BF)
    to_odd = (place == ROWS - distance).astype(F32).astype(BF)
    return mm(mm(pick_even, pieces).astype(BF), to_even) + mm(mm(pick_odd, pieces).astype(BF), to_odd)


def facts_kernel(
    plan_ref, routes_ref, lengths_ref, events_ref, cot_ref, outgoing_ref, facts_ref,
    plan, routes, lengths, cot_s, sems,
):
    small = [(plan_ref, plan), (routes_ref, routes), (lengths_ref, lengths), (cot_ref.at[0], cot_s)]
    small = [pltpu.make_async_copy(*c, sems.at[n]) for n, c in enumerate(small)]
    for c in small:
        c.start()
    for c in small:
        c.wait()
    partner_value = DEV_HIST + 2 * lax.axis_index("segment") - wanted_value()
    chosen = jnp.int32(0)
    for h in range(DEV_HIST):
        chosen = chosen + jnp.where(plan[h] == partner_value, h, 0)
    copy = pltpu.make_async_copy(events_ref.at[chosen], outgoing_ref, sems.at[len(small)])
    copy.start()
    lane = iota((1, 128), 1)
    facts = jnp.zeros((1, 128), F32)
    for j, ref in enumerate((routes, plan, lengths)):
        for h in range(DEV_HIST):
            facts = jnp.where(lane == 4 * j + h, ref[h].astype(F32), facts)
    cot = cot_s[...].astype(F32)
    blocks = [cot[k : k + 1] for k in range(SLOTS)] + [facts, jnp.zeros((1, 128), F32)]
    lines = [jnp.concatenate(blocks[k : k + 5], axis=1) for k in (0, 5)]
    facts_ref[...] = jnp.broadcast_to(jnp.concatenate(lines).astype(BF)[None], facts_ref.shape)
    copy.wait()


def routing_kernel(own_rows, table_ref, bias_ref, seeds_ref, hot_ref, count_ref):
    n_dp = table_ref.shape[0]
    hist = n_dp * DEV_HIST
    me = dp_place()
    facts = table_ref[:, SLOTS * 128 : SLOTS * 128 + 128]
    spread = mm(facts, (iota((128, hist), 0) == iota((128, hist), 1) % DEV_HIST).astype(F32).astype(BF))
    own = iota((n_dp, hist), 1) // DEV_HIST == iota((n_dp, hist), 0)
    routes = jnp.sum(jnp.where(own, spread, 0.0), axis=0, keepdims=True)

    routes_wide = jnp.broadcast_to(routes, (16, hist))
    history, mine = iota((16, hist), 1), me * DEV_HIST + iota((16, hist), 0)
    route = jnp.sum(jnp.where(history == mine, routes_wide, 0.0), axis=1, keepdims=True)
    before = (routes_wide == route) & (history < mine)
    slot = jnp.sum(before.astype(F32), axis=1, keepdims=True)
    source = iota((16, n_dp), 1).astype(F32)
    seeds = jnp.zeros((16, 128), F32)
    for k in range(SLOTS):
        pick = jnp.where((source == route) & (slot == float(k)), 1.0, 0.0).astype(BF)
        seeds = seeds + mm(pick, table_ref[:, 128 * k : 128 * k + 128])
    bias = bias_rows(bias_ref[0]).astype(BF)
    for q in range(LAYERS):
        seeds_ref[q, 0:16, :] = jnp.broadcast_to(seeds[q : q + 1], (16, 128)).astype(BF)
        seeds_ref[q, 16:32, :] = bias

    hit = jnp.broadcast_to((routes == me.astype(F32)).astype(F32), (16, hist))
    earlier = (iota((hist, hist), 0) < iota((hist, hist), 1)).astype(F32).astype(BF)
    place_of = mm(hit.astype(BF), earlier)
    hot = jnp.where(place_of == iota((16, hist), 0).astype(F32), hit, 0.0).astype(BF)
    total = hot_ref.shape[2]
    place, history = iota((hist, total), 1), iota((hist, total), 0)
    chip = place // own_rows
    within = place - chip * own_rows
    first = (chip * 2 + within // 2) * DEV_HIST
    for h in range(DEV_HIST):
        valid = (within < 4) & (within % 2 == h // 2)
        move = jnp.where(valid & (history == first + h), 1.0, 0.0).astype(BF)
        hot_ref[h] = mm(hot, move).astype(BF)

    other = lax.rem(me + n_dp // 2, n_dp)
    known = facts.astype(F32)
    ahead = pltpu.roll(known, 124, 1)
    row, lane = iota((n_dp, 128), 0), iota((n_dp, 128), 1)
    fits = ((row == me) | (row == other)) & (lane >= 4) & (lane < 8)
    fits = fits & (known == wanted_value().astype(F32))
    length = jnp.sum(jnp.where(fits, ahead, 0.0), axis=1, keepdims=True)
    length = jnp.sum(length, axis=0, keepdims=True)
    count_ref[...] = jnp.broadcast_to(length, count_ref.shape).astype(jnp.int32)


def layers_kernel(
    plan_ref, events_ref, other_ref, count_ref, cot_ref,
    w_in_ref, w_out_ref, near_a, near_b, swap_a, swap_b, far_a, far_b, far_c, far_d,
    out_ref,
    weights, proj_s, dsilu_s, normed_s, rstd_s, norm_o_s, rstd_o_s, att_s, datt_s, sems,
):
    half = WIDTH // 2
    segment, core = lax.axis_index("segment"), lax.axis_index("core")
    near = lax.rem(segment + 1 + 2 * core, LAYERS)
    swap = lax.rem(segment + 3 + 2 * core, LAYERS)
    far = lax.rem(segment + 2, LAYERS)
    whole = ((segment, w_in_ref.at[0], w_out_ref.at[0]), (near, near_a, near_b), (swap, swap_a, swap_b))
    for l in range(LAYERS):
        for slot, w_in, w_out in whole:

            @pl.when(slot == l)
            def _():
                for at in range(2):
                    rows = pl.ds(at * half, half)
                    for piece, cols in ((w_in, pl.ds(0, 4 * WIDTH)), (w_out, pl.ds(4 * WIDTH, WIDTH))):
                        pltpu.make_async_copy(piece.at[rows], weights.at[l, rows, cols], sems.at[l, at]).start()

        @pl.when(far == l)
        def _():
            for w_in, w_out, at in ((far_a, far_c, core), (far_b, far_d, 1 - core)):
                rows = pl.ds(pl.multiple_of(at * half, half), half)
                for piece, cols in ((w_in, pl.ds(0, 4 * WIDTH)), (w_out, pl.ds(4 * WIDTH, WIDTH))):
                    pltpu.make_async_copy(piece, weights.at[l, rows, cols], sems.at[l, at]).start()

    row, lane = iota((ROWS, GROUP), 0), iota((ROWS, GROUP), 1)
    head = lane // HEAD_COLS
    column = lane - head * HEAD_COLS
    own_head = [(head == h).astype(F32).astype(BF) for h in range(GROUP // HEAD_COLS)]
    count = count_ref[...]
    allowed = (column <= row) & (column < count[:, 0:1])

    def block_diagonal(a):
        return jnp.concatenate([a * mask for mask in own_head], axis=0)

    def merge(a):
        total = a[:ROWS]
        for h in range(1, GROUP // HEAD_COLS):
            total = jnp.where(head == h, a[h * ROWS : (h + 1) * ROWS], total)
        return total

    def part(kind, g):
        return pl.ds(kind * WIDTH + g * GROUP, GROUP)

    value = wanted_value()
    found = jnp.int32(0)
    acts = jnp.zeros((ROWS, WIDTH), F32)
    for h in range(DEV_HIST):
        same = (plan_ref[h] == value).astype(jnp.int32)
        found = found + same
        acts = jnp.where(same == 1, events_ref[h].astype(F32), acts)
    acts = jnp.where(found > 0, acts, other_ref[...].astype(F32))

    for l in range(LAYERS):
        average = row_mean(acts)
        centred = acts - average
        rstd = lax.rsqrt(row_mean(centred * centred) + 1e-6)
        normed = centred * rstd
        normed_s[l] = normed
        rstd_s[l] = jnp.broadcast_to(rstd, (ROWS, 128))
        for c in range(2):
            piece = weights.at[l, pl.ds(c * half, half)]
            pltpu.make_async_copy(piece, piece, sems.at[l, c]).wait()
        table = cot_ref[l, 16:32, :].astype(F32)
        table = table[0:4] + table[4:8] + table[8:12]
        bias = []
        for g in range(GROUPS):
            tiles = [jnp.broadcast_to(table[p : p + 1], (ROWS, 128)) for p in (2 * g, 2 * g + 1)]
            bias.append(jnp.concatenate([pltpu.roll(t, 0, 1, stride=1, stride_axis=0) for t in tiles], axis=1))
        normed_b = normed.astype(BF)
        proj = {}
        for kind in (3, 2, 1, 0):
            cols = pl.ds(kind * WIDTH, WIDTH)
            pre = mm(normed_b, weights[l, :, cols])
            gated = sigmoid(pre)
            silu = pre * gated
            proj[kind] = silu.astype(BF)
            proj_s[l, :, cols] = proj[kind]
            dsilu_s[l, :, cols] = gated + silu * (1.0 - gated)
        cut = [slice(g * GROUP, (g + 1) * GROUP) for g in range(GROUPS)]
        keys = [block_diagonal(proj[3][:, c]) for c in cut]
        values = [block_diagonal(proj[1][:, c]) for c in cut]
        scores = [mm(proj[2][:, cut[g]], keys[g], NT) * 0.125 + bias[g] for g in range(GROUPS)]
        outs = []
        for g in range(GROUPS):
            gated = sigmoid(scores[g])
            silu = scores[g] * gated
            att = jnp.where(allowed, silu, 0.0).astype(BF)
            att_s[l, g] = att
            datt_s[l, g] = jnp.where(allowed, gated + silu * (1.0 - gated), 0.0) * 0.125
            outs.append(mm(att, values[g]))
        mixed = jnp.concatenate(outs, axis=1)
        centred = mixed - row_mean(mixed)
        rstd = lax.rsqrt(row_mean(centred * centred) + 1e-6)
        norm_o = centred * rstd
        norm_o_s[l] = norm_o
        rstd_o_s[l] = jnp.broadcast_to(rstd, (ROWS, 128))
        branch = (norm_o * proj[0].astype(F32)).astype(BF)
        out_ref[l, 64:128, :] = branch
        acts = (acts + mm(branch, weights[l, :, pl.ds(4 * WIDTH, WIDTH)])).astype(BF).astype(F32)

    last = iota((ROWS, WIDTH), 0) == count[:, 0:1] - 1
    state = jnp.sum(jnp.where(last, acts, 0.0), axis=0, keepdims=True)
    for q in range(LAYERS):
        quarter = jnp.broadcast_to(state[:, 128 * q : 128 * q + 128], (16, 128))
        out_ref[q, 192:208, :] = jnp.concatenate([quarter] * 4, axis=1).astype(BF)
    seed = jnp.concatenate([cot_ref[q, 0:16, :].astype(F32)[0:1] for q in range(LAYERS)], axis=1)
    cot = jnp.where(last, jnp.broadcast_to(seed, (ROWS, WIDTH)), 0.0).astype(BF)

    for l in reversed(range(LAYERS)):
        out_ref[l, 128:192, :] = cot
        d_branch = mm(cot, weights[l, :, pl.ds(4 * WIDTH, WIDTH)], NT).astype(BF).astype(F32)
        norm_o = norm_o_s[l]
        d_gate = (d_branch * norm_o).astype(BF)
        d_norm = d_branch * proj_s[l, :, pl.ds(0, WIDTH)].astype(F32)
        d_mixed = rstd_o_s[l][:, 0:1] * (d_norm - row_mean(d_norm) - norm_o * row_mean(d_norm * norm_o))
        d_mixed = d_mixed.astype(BF)
        d_outs = [d_mixed[:, g * GROUP : (g + 1) * GROUP] for g in range(GROUPS)]
        d_atts = [mm(d_outs[g], block_diagonal(proj_s[l, :, part(1, g)]), NT) for g in range(GROUPS)]
        d_value = [merge(mm(att_s[l, g], d_outs[g], TN)) for g in range(GROUPS)]
        d_scores = [(d_atts[g].astype(BF).astype(F32) * datt_s[l, g]).astype(BF) for g in range(GROUPS)]
        d_query = [mm(d_scores[g], block_diagonal(proj_s[l, :, part(3, g)])) for g in range(GROUPS)]
        d_key = [merge(mm(d_scores[g], proj_s[l, :, part(2, g)], TN)) for g in range(GROUPS)]
        d_normed = jnp.zeros((ROWS, WIDTH), F32)
        for kind, pieces in enumerate(([d_gate], d_value, d_query, d_key)):
            cols = pl.ds(kind * WIDTH, WIDTH)
            whole = pieces[0] if len(pieces) == 1 else jnp.concatenate(pieces, axis=1)
            d_pre = whole.astype(BF).astype(F32) * dsilu_s[l, :, cols]
            d_normed = d_normed + mm(d_pre.astype(BF), weights[l, :, cols], NT)
        d_normed = d_normed.astype(BF).astype(F32)
        normed = normed_s[l]
        d_in = rstd_s[l][:, 0:1] * (d_normed - row_mean(d_normed) - normed * row_mean(d_normed * normed))
        cot = (d_in + cot.astype(F32)).astype(BF)
        out_ref[l, 0:64, :] = cot


def gradient_kernel(own_rows, got_ref, grads_ref, keep_ref, send_ref):
    core = lax.axis_index("core")
    for t in range(LAYERS):
        grads_ref[t] = got_ref[t, 0:64, :]
    branch = jnp.concatenate([got_ref[t, 64:128, :] for t in range(LAYERS)], axis=0)
    cot = jnp.concatenate([got_ref[t, 128:192, :] for t in range(LAYERS)], axis=0)
    half = WIDTH // 2
    to, source = iota((WIDTH, WIDTH), 1), iota((WIDTH, WIDTH), 0)
    side = jnp.where(to < half, core, 1 - core)
    within = jnp.where(to < half, to, to - half)
    wanted = (within // own_rows) * (2 * own_rows) + side * own_rows + within % own_rows
    order = (source == wanted).astype(F32).astype(BF)
    ordered = mm(branch, order).astype(BF)
    keep_ref[...] = mm(ordered[:, :half], cot, TN)
    send_ref[0:half, :] = mm(ordered[:, half:], cot, TN).astype(BF)
    states = [got_ref[t, 192:208, 0:128] for t in range(LAYERS)]
    send_ref[half : half + 16, :] = jnp.concatenate(states, axis=1)


def packing_kernel(own_rows, keep_ref, send_ref, got_ref, out_ref):
    half = WIDTH // 2
    core = lax.axis_index("core")
    own = send_ref[half : half + 16, :].astype(F32)[0:1]
    other = got_ref[half : half + 16, :].astype(F32)[0:1]
    first = jnp.where(core == 0, own, other)
    second = jnp.where(core == 0, other, own)
    at = iota((half, half), 0) % own_rows
    states = jnp.zeros((half, half), F32)
    for r, quarter in enumerate((first[:, :half], first[:, half:], second[:, :half], second[:, half:])):
        states = jnp.where(at == r, quarter, states)
    out_ref[:, 0:WIDTH] = (keep_ref[...] + got_ref[0:half, :].astype(F32)).astype(BF)
    out_ref[:, WIDTH : WIDTH + half] = states.astype(BF)


def result_kernel(got_ref, hot_ref, served_ref, weight_ref):
    rows = got_ref.shape[0]
    own_rows = weight_ref.shape[0]
    lead = max(16, own_rows)
    pick = (iota((lead, rows), 1) % own_rows == iota((lead, rows), 0)).astype(F32).astype(BF)
    weight_ref[...] = mm(pick, got_ref[:, 0:WIDTH])[0:own_rows]
    served = jnp.zeros((16, 128), F32)
    for h in range(DEV_HIST):
        at = WIDTH + 128 * (h % 2)
        served = served + mm(hot_ref[h], got_ref[:, at : at + 128])
    served_ref[...] = served[0:SLOTS].astype(BF)


def shape(dims, dtype):
    return jax.ShapeDtypeStruct(dims, dtype)


def call(kernel, outs, scratch=(), in_specs=None, out_specs=None, limit=24):
    specs = {} if in_specs is None else {"in_specs": in_specs}
    specs |= {} if out_specs is None else {"out_specs": out_specs}
    return pl.pallas_call(
        kernel,
        out_shape=outs,
        scratch_shapes=scratch,
        **specs,
        compiler_params=pltpu.CompilerParams(vmem_limit_bytes=limit * 1024 * 1024),
    )


def body(events, lengths, balance_plan, routes, w_uvqk, w_out, rel_bias, state_cotangent):
    n_z, n_y, n_core = (lax.axis_size(a) for a in DP)
    n_dp = n_z * n_y * n_core
    chips = n_z * n_y
    own_rows = WIDTH // n_dp
    half = WIDTH // 2

    any_spec, vmem = pl.BlockSpec(memory_space=pl.ANY), pl.BlockSpec(memory_space=pltpu.VMEM)
    smem = pl.BlockSpec(memory_space=pltpu.SMEM)
    with jax.named_scope("packing"):
        outgoing, facts = call(
            facts_kernel,
            (
                shape((ROWS, WIDTH), BF),
                shape((n_dp, 2, (SLOTS + 2) * 64), BF),
            ),
            scratch=[
                pltpu.SMEM((DEV_HIST,), jnp.int32),
                pltpu.SMEM((DEV_HIST,), jnp.int32),
                pltpu.SMEM((DEV_HIST,), jnp.int32),
                pltpu.VMEM((SLOTS, 128), BF),
                pltpu.SemaphoreType.DMA((5,)),
            ],
            in_specs=[any_spec] * 5,
            limit=58,
        )(balance_plan, routes.reshape(DEV_HIST), lengths, events, state_cotangent)

    with jax.named_scope("section_weights"):
        ring = [(s * 2, (s - 1) % LAYERS * 2) for s in range(LAYERS)]
        ring += [(s * 2 + 1, (s + 1) % LAYERS * 2 + 1) for s in range(LAYERS)]
        swap = [(0, 1), (1, 0)]
        near_a = lax.ppermute(w_uvqk[0], ("segment", "core"), ring)
        near_b = lax.ppermute(w_out[0], ("segment", "core"), ring)

    with jax.named_scope("events"):
        other_events = lax.ppermute(outgoing, "z", [(i, (i + n_z // 2) % n_z) for i in range(n_z)])

    with jax.named_scope("routing"):
        facts = lax.all_to_all(facts, DP, 0, 0, tiled=True)
        near_a, other_events, facts = lax.optimization_barrier((near_a, other_events, facts))
        near_b, near_c, facts = lax.optimization_barrier((near_b, near_a, facts))
        facts = facts.reshape(n_dp, (SLOTS + 2) * 128)

    with jax.named_scope("section_weights"):
        lower = lax.axis_index("core") == 0
        onward = [jnp.where(lower, a[:half], a[half:]) for a in (near_a, near_b)]
        far_a, far_c = (lax.ppermute(a, ("segment", "core"), ring) for a in onward)
        swap_a = lax.ppermute(near_c, "core", swap)
        swap_b = lax.ppermute(near_b, "core", swap)

    with jax.named_scope("routing"):
        seeds, hot, count = call(
            functools.partial(routing_kernel, own_rows),
            (
                shape((LAYERS, 32, 128), BF),
                shape((DEV_HIST, 16, half), BF),
                shape((ROWS, 128), jnp.int32),
            ),
        )(facts, rel_bias)
        seeds = lax.all_to_all(seeds, "segment", 0, 0, tiled=True)
        far_a, far_c, swap_b, seeds = lax.optimization_barrier((far_a, far_c, swap_b, seeds))
    with jax.named_scope("section_weights"):
        far_b, far_d = (lax.ppermute(a, "core", swap) for a in (far_a, far_c))

    with jax.named_scope("layers"):
        message = call(
            layers_kernel,
            shape((LAYERS, MSG, WIDTH), BF),
            scratch=[
                pltpu.VMEM((LAYERS, WIDTH, 5 * WIDTH), BF),
                pltpu.VMEM((LAYERS, ROWS, 4 * WIDTH), BF),
                pltpu.VMEM((LAYERS, ROWS, 4 * WIDTH), F32),
                pltpu.VMEM((LAYERS, ROWS, WIDTH), F32),
                pltpu.VMEM((LAYERS, ROWS, 128), F32),
                pltpu.VMEM((LAYERS, ROWS, WIDTH), F32),
                pltpu.VMEM((LAYERS, ROWS, 128), F32),
                pltpu.VMEM((LAYERS, GROUPS, ROWS, GROUP), BF),
                pltpu.VMEM((LAYERS, GROUPS, ROWS, GROUP), F32),
                pltpu.SemaphoreType.DMA((LAYERS, 2)),
            ],
            in_specs=[smem] + [vmem] * 4 + [any_spec] * 10,
            limit=28,
        )(
            balance_plan, events, other_events, count, seeds,
            w_uvqk, w_out, near_a, near_b, swap_a, swap_b, far_a, far_b, far_c, far_d,
        )

    with jax.named_scope("section_exchange"):
        arrived = lax.all_to_all(message, "segment", 0, 0, tiled=True)
    with jax.named_scope("weight_gradient"):
        grads, keep, send = call(
            functools.partial(gradient_kernel, own_rows),
            (
                shape((LAYERS, ROWS, WIDTH), BF),
                shape((half, WIDTH), F32),
                shape((half + 16, WIDTH), BF),
            ),
        )(arrived)
        partner = lax.ppermute(send, "core", swap)
        blocks = call(
            functools.partial(packing_kernel, own_rows),
            shape((half, WIDTH + half), BF),
        )(keep, send, partner)
        blocks = blocks.reshape(chips, own_rows, WIDTH + half)
        blocks = lax.all_to_all(blocks, ("z", "y"), 0, 0, tiled=True)
        served, weight = call(
            result_kernel,
            (shape((SLOTS, 128), BF), shape((own_rows, WIDTH), F32)),
        )(blocks.reshape(half, WIDTH + half), hot)
    return served[None], grads[None], weight[None]


def solution(mesh):
    devices = mesh.devices
    n_segment, n_dp = devices.shape
    side = 1
    while side * side * 2 < n_dp:
        side *= 2
    fine = Mesh(
        devices.reshape(n_segment, n_dp // (2 * side), side, 2), ("segment",) + DP
    )
    return jax.shard_map(
        body,
        mesh=fine,
        in_specs=(
            P(DP, None, None),
            P(DP),
            P(DP),
            P(DP, None),
            P("segment", None, None),
            P("segment", None, None),
            P("segment", None, None),
            P(DP, None, "segment"),
        ),
        out_specs=(
            P(DP, None, "segment"),
            P("segment", DP, None, None),
            P("segment", DP, None),
        ),
        check_vma=False,
    )
```

```python
import functools

import jax
import jax.numpy as jnp
from jax import lax
from jax.experimental import pallas as pl
from jax.experimental.pallas import tpu as pltpu
from jax.sharding import Mesh, PartitionSpec as P

BF = jnp.bfloat16
F32 = jnp.float32
DP = ("z", "y", "core")
DEV_HIST = 4
ROWS = 64
WIDTH = 512
HEAD_COLS = 64
GROUP = 256
GROUPS = WIDTH // GROUP
LAYERS = 4
SLOTS = 8
MSG = 208
NN = (((1,), (0,)), ((), ()))
NT = (((1,), (1,)), ((), ()))
TN = (((0,), (0,)), ((), ()))


def mm(a, b, dims=NN):
    return lax.dot_general(a, b, dims, preferred_element_type=F32)


def iota(shape, dim):
    return lax.broadcasted_iota(jnp.int32, shape, dim)


def row_mean(a):
    return jnp.mean(a, axis=-1, keepdims=True)


def sigmoid(a):
    return 0.5 * jnp.tanh(0.5 * a) + 0.5


def dp_place():
    ny, nc = lax.axis_size("y"), lax.axis_size("core")
    return (lax.axis_index("z") * ny + lax.axis_index("y")) * nc + lax.axis_index("core")


def wanted_value():
    upper = (lax.axis_index("z") >= lax.axis_size("z") // 2).astype(jnp.int32)
    return upper * DEV_HIST + lax.axis_index("segment")


def bias_rows(bias):
    high = bias.astype(BF).astype(F32)
    middle = (bias - high).astype(BF).astype(F32)
    low = bias - high - middle
    pieces = jnp.concatenate([high, middle, low, jnp.zeros((8, ROWS), F32)]).astype(BF)
    row, head = iota((16, 32), 0), iota((16, 32), 1)
    even = (row // 4) * 8 + 2 * (row % 4)
    used = row < 12
    pick_even = (used & (head == even)).astype(F32).astype(BF)
    pick_odd = (used & (head == even + 1)).astype(F32).astype(BF)
    distance, place = iota((ROWS, 128), 0), iota((ROWS, 128), 1)
    to_even = (place == (128 - distance) % 128).astype(F32).astype(BF)
    to_odd = (place == ROWS - distance).astype(F32).astype(BF)
    return mm(mm(pick_even, pieces).astype(BF), to_even) + mm(mm(pick_odd, pieces).astype(BF), to_odd)


def facts_kernel(
    plan_ref, routes_ref, lengths_ref, events_ref, cot_ref, outgoing_ref, facts_ref,
    plan, routes, lengths, sems,
):
    small = [(plan_ref, plan), (routes_ref, routes), (lengths_ref, lengths)]
    small = [pltpu.make_async_copy(*c, sems.at[n]) for n, c in enumerate(small)]
    for c in small:
        c.start()
    for c in small:
        c.wait()
    partner_value = DEV_HIST + 2 * lax.axis_index("segment") - wanted_value()
    chosen = jnp.int32(0)
    for h in range(DEV_HIST):
        chosen = chosen + jnp.where(plan[h] == partner_value, h, 0)
    copy = pltpu.make_async_copy(events_ref.at[chosen], outgoing_ref, sems.at[len(small)])
    copy.start()
    lane = iota((1, 128), 1)
    facts = jnp.zeros((1, 128), F32)
    for j, ref in enumerate((routes, plan, lengths)):
        for h in range(DEV_HIST):
            facts = jnp.where(lane == 4 * j + h, ref[h].astype(F32), facts)
    cot = cot_ref[0].astype(F32)
    blocks = [cot[k : k + 1] for k in range(SLOTS)] + [facts, jnp.zeros((1, 128), F32)]
    lines = [jnp.concatenate(blocks[k : k + 5], axis=1) for k in (0, 5)]
    facts_ref[...] = jnp.broadcast_to(jnp.concatenate(lines).astype(BF)[None], facts_ref.shape)
    copy.wait()


def routing_kernel(own_rows, table_ref, bias_ref, seeds_ref, hot_ref, count_ref):
    n_dp = table_ref.shape[0]
    hist = n_dp * DEV_HIST
    me = dp_place()
    facts = table_ref[:, SLOTS * 128 : SLOTS * 128 + 128]
    spread = mm(facts, (iota((128, hist), 0) == iota((128, hist), 1) % DEV_HIST).astype(F32).astype(BF))
    own = iota((n_dp, hist), 1) // DEV_HIST == iota((n_dp, hist), 0)
    routes = jnp.sum(jnp.where(own, spread, 0.0), axis=0, keepdims=True)

    routes_wide = jnp.broadcast_to(routes, (16, hist))
    history, mine = iota((16, hist), 1), me * DEV_HIST + iota((16, hist), 0)
    route = jnp.sum(jnp.where(history == mine, routes_wide, 0.0), axis=1, keepdims=True)
    before = (routes_wide == route) & (history < mine)
    slot = jnp.sum(before.astype(F32), axis=1, keepdims=True)
    source = iota((16, n_dp), 1).astype(F32)
    seeds = jnp.zeros((16, 128), F32)
    for k in range(SLOTS):
        pick = jnp.where((source == route) & (slot == float(k)), 1.0, 0.0).astype(BF)
        seeds = seeds + mm(pick, table_ref[:, 128 * k : 128 * k + 128])
    bias = bias_rows(bias_ref[0]).astype(BF)
    for q in range(LAYERS):
        seeds_ref[q, 0:16, :] = jnp.broadcast_to(seeds[q : q + 1], (16, 128)).astype(BF)
        seeds_ref[q, 16:32, :] = bias

    hit = jnp.broadcast_to((routes == me.astype(F32)).astype(F32), (16, hist))
    earlier = (iota((hist, hist), 0) < iota((hist, hist), 1)).astype(F32).astype(BF)
    place_of = mm(hit.astype(BF), earlier)
    hot = jnp.where(place_of == iota((16, hist), 0).astype(F32), hit, 0.0).astype(BF)
    total = hot_ref.shape[2]
    place, history = iota((hist, total), 1), iota((hist, total), 0)
    chip = place // own_rows
    within = place - chip * own_rows
    first = (chip * 2 + within // 2) * DEV_HIST
    for h in range(DEV_HIST):
        valid = (within < 4) & (within % 2 == h // 2)
        move = jnp.where(valid & (history == first + h), 1.0, 0.0).astype(BF)
        hot_ref[h] = mm(hot, move).astype(BF)

    other = lax.rem(me + n_dp // 2, n_dp)
    known = facts.astype(F32)
    ahead = pltpu.roll(known, 124, 1)
    row, lane = iota((n_dp, 128), 0), iota((n_dp, 128), 1)
    fits = ((row == me) | (row == other)) & (lane >= 4) & (lane < 8)
    fits = fits & (known == wanted_value().astype(F32))
    length = jnp.sum(jnp.where(fits, ahead, 0.0), axis=1, keepdims=True)
    length = jnp.sum(length, axis=0, keepdims=True)
    count_ref[...] = jnp.broadcast_to(length, count_ref.shape).astype(jnp.int32)


def layers_kernel(
    plan_ref, events_ref, other_ref, count_ref, cot_ref,
    w_in_ref, w_out_ref, near_a, near_b, swap_a, swap_b, far_a, far_b, far_c, far_d,
    out_ref,
    weights, proj_s, dsilu_s, normed_s, rstd_s, norm_o_s, rstd_o_s, att_s, datt_s, sems,
):
    half = WIDTH // 2
    segment, core = lax.axis_index("segment"), lax.axis_index("core")
    near = lax.rem(segment + 1 + 2 * core, LAYERS)
    swap = lax.rem(segment + 3 + 2 * core, LAYERS)
    far = lax.rem(segment + 2, LAYERS)
    whole = ((segment, w_in_ref.at[0], w_out_ref.at[0]), (near, near_a, near_b), (swap, swap_a, swap_b))
    for l in range(LAYERS):
        for slot, w_in, w_out in whole:

            @pl.when(slot == l)
            def _():
                for at in range(2):
                    rows = pl.ds(at * half, half)
                    for piece, cols in ((w_in, pl.ds(0, 4 * WIDTH)), (w_out, pl.ds(4 * WIDTH, WIDTH))):
                        pltpu.make_async_copy(piece.at[rows], weights.at[l, rows, cols], sems.at[l, at]).start()

        @pl.when(far == l)
        def _():
            for w_in, w_out, at in ((far_a, far_c, core), (far_b, far_d, 1 - core)):
                rows = pl.ds(pl.multiple_of(at * half, half), half)
                for piece, cols in ((w_in, pl.ds(0, 4 * WIDTH)), (w_out, pl.ds(4 * WIDTH, WIDTH))):
                    pltpu.make_async_copy(piece, weights.at[l, rows, cols], sems.at[l, at]).start()

    row, lane = iota((ROWS, GROUP), 0), iota((ROWS, GROUP), 1)
    head = lane // HEAD_COLS
    column = lane - head * HEAD_COLS
    own_head = [(head == h).astype(F32).astype(BF) for h in range(GROUP // HEAD_COLS)]
    count = count_ref[...]
    allowed = (column <= row) & (column < count[:, 0:1])

    def block_diagonal(a):
        return jnp.concatenate([a * mask for mask in own_head], axis=0)

    def merge(a):
        total = a[:ROWS]
        for h in range(1, GROUP // HEAD_COLS):
            total = jnp.where(head == h, a[h * ROWS : (h + 1) * ROWS], total)
        return total

    def part(kind, g):
        return pl.ds(kind * WIDTH + g * GROUP, GROUP)

    value = wanted_value()
    found = jnp.int32(0)
    acts = jnp.zeros((ROWS, WIDTH), F32)
    for h in range(DEV_HIST):
        same = (plan_ref[h] == value).astype(jnp.int32)
        found = found + same
        acts = jnp.where(same == 1, events_ref[h].astype(F32), acts)
    acts = jnp.where(found > 0, acts, other_ref[...].astype(F32))

    for l in range(LAYERS):
        average = row_mean(acts)
        centred = acts - average
        rstd = lax.rsqrt(row_mean(centred * centred) + 1e-6)
        normed = centred * rstd
        normed_s[l] = normed
        rstd_s[l] = jnp.broadcast_to(rstd, (ROWS, 128))
        for c in range(2):
            piece = weights.at[l, pl.ds(c * half, half)]
            pltpu.make_async_copy(piece, piece, sems.at[l, c]).wait()
        table = cot_ref[l, 16:32, :].astype(F32)
        table = table[0:4] + table[4:8] + table[8:12]
        bias = []
        for g in range(GROUPS):
            tiles = [jnp.broadcast_to(table[p : p + 1], (ROWS, 128)) for p in (2 * g, 2 * g + 1)]
            bias.append(jnp.concatenate([pltpu.roll(t, 0, 1, stride=1, stride_axis=0) for t in tiles], axis=1))
        normed_b = normed.astype(BF)
        proj = {}
        for kind in (3, 2, 1, 0):
            cols = pl.ds(kind * WIDTH, WIDTH)
            pre = mm(normed_b, weights[l, :, cols])
            gated = sigmoid(pre)
            silu = pre * gated
            proj[kind] = silu.astype(BF)
            proj_s[l, :, cols] = proj[kind]
            dsilu_s[l, :, cols] = gated + silu * (1.0 - gated)
        cut = [slice(g * GROUP, (g + 1) * GROUP) for g in range(GROUPS)]
        keys = [block_diagonal(proj[3][:, c]) for c in cut]
        values = [block_diagonal(proj[1][:, c]) for c in cut]
        scores = [mm(proj[2][:, cut[g]], keys[g], NT) * 0.125 + bias[g] for g in range(GROUPS)]
        outs = []
        for g in range(GROUPS):
            gated = sigmoid(scores[g])
            silu = scores[g] * gated
            att = jnp.where(allowed, silu, 0.0).astype(BF)
            att_s[l, g] = att
            datt_s[l, g] = jnp.where(allowed, gated + silu * (1.0 - gated), 0.0) * 0.125
            outs.append(mm(att, values[g]))
        mixed = jnp.concatenate(outs, axis=1)
        centred = mixed - row_mean(mixed)
        rstd = lax.rsqrt(row_mean(centred * centred) + 1e-6)
        norm_o = centred * rstd
        norm_o_s[l] = norm_o
        rstd_o_s[l] = jnp.broadcast_to(rstd, (ROWS, 128))
        branch = (norm_o * proj[0].astype(F32)).astype(BF)
        out_ref[l, 64:128, :] = branch
        acts = (acts + mm(branch, weights[l, :, pl.ds(4 * WIDTH, WIDTH)])).astype(BF).astype(F32)

    last = iota((ROWS, WIDTH), 0) == count[:, 0:1] - 1
    state = jnp.sum(jnp.where(last, acts, 0.0), axis=0, keepdims=True)
    for q in range(LAYERS):
        quarter = jnp.broadcast_to(state[:, 128 * q : 128 * q + 128], (16, 128))
        out_ref[q, 192:208, :] = jnp.concatenate([quarter] * 4, axis=1).astype(BF)
    seed = jnp.concatenate([cot_ref[q, 0:16, :].astype(F32)[0:1] for q in range(LAYERS)], axis=1)
    cot = jnp.where(last, jnp.broadcast_to(seed, (ROWS, WIDTH)), 0.0).astype(BF)

    for l in reversed(range(LAYERS)):
        out_ref[l, 128:192, :] = cot
        d_branch = mm(cot, weights[l, :, pl.ds(4 * WIDTH, WIDTH)], NT).astype(BF).astype(F32)
        norm_o = norm_o_s[l]
        d_gate = (d_branch * norm_o).astype(BF)
        d_norm = d_branch * proj_s[l, :, pl.ds(0, WIDTH)].astype(F32)
        d_mixed = rstd_o_s[l][:, 0:1] * (d_norm - row_mean(d_norm) - norm_o * row_mean(d_norm * norm_o))
        d_mixed = d_mixed.astype(BF)
        d_outs = [d_mixed[:, g * GROUP : (g + 1) * GROUP] for g in range(GROUPS)]
        d_atts = [mm(d_outs[g], block_diagonal(proj_s[l, :, part(1, g)]), NT) for g in range(GROUPS)]
        d_value = [merge(mm(att_s[l, g], d_outs[g], TN)) for g in range(GROUPS)]
        d_scores = [(d_atts[g].astype(BF).astype(F32) * datt_s[l, g]).astype(BF) for g in range(GROUPS)]
        d_query = [mm(d_scores[g], block_diagonal(proj_s[l, :, part(3, g)])) for g in range(GROUPS)]
        d_key = [merge(mm(d_scores[g], proj_s[l, :, part(2, g)], TN)) for g in range(GROUPS)]
        d_normed = jnp.zeros((ROWS, WIDTH), F32)
        for kind, pieces in enumerate(([d_gate], d_value, d_query, d_key)):
            cols = pl.ds(kind * WIDTH, WIDTH)
            whole = pieces[0] if len(pieces) == 1 else jnp.concatenate(pieces, axis=1)
            d_pre = whole.astype(BF).astype(F32) * dsilu_s[l, :, cols]
            d_normed = d_normed + mm(d_pre.astype(BF), weights[l, :, cols], NT)
        d_normed = d_normed.astype(BF).astype(F32)
        normed = normed_s[l]
        d_in = rstd_s[l][:, 0:1] * (d_normed - row_mean(d_normed) - normed * row_mean(d_normed * normed))
        cot = (d_in + cot.astype(F32)).astype(BF)
        out_ref[l, 0:64, :] = cot


def gradient_kernel(own_rows, got_ref, grads_ref, keep_ref, send_ref):
    core = lax.axis_index("core")
    for t in range(LAYERS):
        grads_ref[t] = got_ref[t, 0:64, :]
    branch = jnp.concatenate([got_ref[t, 64:128, :] for t in range(LAYERS)], axis=0)
    cot = jnp.concatenate([got_ref[t, 128:192, :] for t in range(LAYERS)], axis=0)
    half = WIDTH // 2
    to, source = iota((WIDTH, WIDTH), 1), iota((WIDTH, WIDTH), 0)
    side = jnp.where(to < half, core, 1 - core)
    within = jnp.where(to < half, to, to - half)
    wanted = (within // own_rows) * (2 * own_rows) + side * own_rows + within % own_rows
    order = (source == wanted).astype(F32).astype(BF)
    ordered = mm(branch, order).astype(BF)
    keep_ref[...] = mm(ordered[:, :half], cot, TN)
    send_ref[0:half, :] = mm(ordered[:, half:], cot, TN).astype(BF)
    states = [got_ref[t, 192:208, 0:128] for t in range(LAYERS)]
    send_ref[half : half + 16, :] = jnp.concatenate(states, axis=1)


def packing_kernel(own_rows, keep_ref, send_ref, got_ref, out_ref):
    half = WIDTH // 2
    core = lax.axis_index("core")
    own = send_ref[half : half + 16, :].astype(F32)[0:1]
    other = got_ref[half : half + 16, :].astype(F32)[0:1]
    first = jnp.where(core == 0, own, other)
    second = jnp.where(core == 0, other, own)
    at = iota((half, half), 0) % own_rows
    states = jnp.zeros((half, half), F32)
    for r, quarter in enumerate((first[:, :half], first[:, half:], second[:, :half], second[:, half:])):
        states = jnp.where(at == r, quarter, states)
    out_ref[:, 0:WIDTH] = (keep_ref[...] + got_ref[0:half, :].astype(F32)).astype(BF)
    out_ref[:, WIDTH : WIDTH + half] = states.astype(BF)


def result_kernel(got_ref, hot_ref, served_ref, weight_ref):
    rows = got_ref.shape[0]
    own_rows = weight_ref.shape[0]
    lead = max(16, own_rows)
    pick = (iota((lead, rows), 1) % own_rows == iota((lead, rows), 0)).astype(F32).astype(BF)
    weight_ref[...] = mm(pick, got_ref[:, 0:WIDTH])[0:own_rows]
    served = jnp.zeros((16, 128), F32)
    for h in range(DEV_HIST):
        at = WIDTH + 128 * (h % 2)
        served = served + mm(hot_ref[h], got_ref[:, at : at + 128])
    served_ref[...] = served[0:SLOTS].astype(BF)


def shape(dims, dtype):
    return jax.ShapeDtypeStruct(dims, dtype)


def call(kernel, outs, scratch=(), in_specs=None, out_specs=None, limit=24):
    specs = {} if in_specs is None else {"in_specs": in_specs}
    specs |= {} if out_specs is None else {"out_specs": out_specs}
    return pl.pallas_call(
        kernel,
        out_shape=outs,
        scratch_shapes=scratch,
        **specs,
        compiler_params=pltpu.CompilerParams(vmem_limit_bytes=limit * 1024 * 1024),
    )


def body(events, lengths, balance_plan, routes, w_uvqk, w_out, rel_bias, state_cotangent):
    n_z, n_y, n_core = (lax.axis_size(a) for a in DP)
    n_dp = n_z * n_y * n_core
    chips = n_z * n_y
    own_rows = WIDTH // n_dp
    half = WIDTH // 2

    any_spec, vmem = pl.BlockSpec(memory_space=pl.ANY), pl.BlockSpec(memory_space=pltpu.VMEM)
    smem = pl.BlockSpec(memory_space=pltpu.SMEM)
    with jax.named_scope("packing"):
        outgoing, facts = call(
            facts_kernel,
            (
                shape((ROWS, WIDTH), BF),
                shape((n_dp, 2, (SLOTS + 2) * 64), BF),
            ),
            scratch=[
                pltpu.SMEM((DEV_HIST,), jnp.int32),
                pltpu.SMEM((DEV_HIST,), jnp.int32),
                pltpu.SMEM((DEV_HIST,), jnp.int32),
                pltpu.SemaphoreType.DMA((4,)),
            ],
            in_specs=[any_spec] * 4 + [vmem],
            limit=58,
        )(balance_plan, routes.reshape(DEV_HIST), lengths, events, state_cotangent)

    with jax.named_scope("section_weights"):
        ring = [(s * 2, (s - 1) % LAYERS * 2) for s in range(LAYERS)]
        ring += [(s * 2 + 1, (s + 1) % LAYERS * 2 + 1) for s in range(LAYERS)]
        swap = [(0, 1), (1, 0)]
        near_a = lax.ppermute(w_uvqk[0], ("segment", "core"), ring)
        near_b = lax.ppermute(w_out[0], ("segment", "core"), ring)

    with jax.named_scope("events"):
        other_events = lax.ppermute(outgoing, "z", [(i, (i + n_z // 2) % n_z) for i in range(n_z)])

    with jax.named_scope("routing"):
        facts = lax.all_to_all(facts, DP, 0, 0, tiled=True)
        near_a, other_events, facts = lax.optimization_barrier((near_a, other_events, facts))
        near_b, near_c, facts = lax.optimization_barrier((near_b, near_a, facts))
        facts = facts.reshape(n_dp, (SLOTS + 2) * 128)

    with jax.named_scope("section_weights"):
        lower = lax.axis_index("core") == 0
        onward = [jnp.where(lower, a[:half], a[half:]) for a in (near_a, near_b)]
        far_a, far_c = (lax.ppermute(a, ("segment", "core"), ring) for a in onward)
        swap_a = lax.ppermute(near_c, "core", swap)
        swap_b = lax.ppermute(near_b, "core", swap)

    with jax.named_scope("routing"):
        seeds, hot, count = call(
            functools.partial(routing_kernel, own_rows),
            (
                shape((LAYERS, 32, 128), BF),
                shape((DEV_HIST, 16, half), BF),
                shape((ROWS, 128), jnp.int32),
            ),
        )(facts, rel_bias)
        seeds = lax.all_to_all(seeds, "segment", 0, 0, tiled=True)
        far_a, far_c, swap_b, seeds = lax.optimization_barrier((far_a, far_c, swap_b, seeds))
    with jax.named_scope("section_weights"):
        far_b, far_d = (lax.ppermute(a, "core", swap) for a in (far_a, far_c))

    with jax.named_scope("layers"):
        message = call(
            layers_kernel,
            shape((LAYERS, MSG, WIDTH), BF),
            scratch=[
                pltpu.VMEM((LAYERS, WIDTH, 5 * WIDTH), BF),
                pltpu.VMEM((LAYERS, ROWS, 4 * WIDTH), BF),
                pltpu.VMEM((LAYERS, ROWS, 4 * WIDTH), F32),
                pltpu.VMEM((LAYERS, ROWS, WIDTH), F32),
                pltpu.VMEM((LAYERS, ROWS, 128), F32),
                pltpu.VMEM((LAYERS, ROWS, WIDTH), F32),
                pltpu.VMEM((LAYERS, ROWS, 128), F32),
                pltpu.VMEM((LAYERS, GROUPS, ROWS, GROUP), BF),
                pltpu.VMEM((LAYERS, GROUPS, ROWS, GROUP), F32),
                pltpu.SemaphoreType.DMA((LAYERS, 2)),
            ],
            in_specs=[smem] + [vmem] * 4 + [any_spec] * 10,
            limit=28,
        )(
            balance_plan, events, other_events, count, seeds,
            w_uvqk, w_out, near_a, near_b, swap_a, swap_b, far_a, far_b, far_c, far_d,
        )

    with jax.named_scope("section_exchange"):
        arrived = lax.all_to_all(message, "segment", 0, 0, tiled=True)
    with jax.named_scope("weight_gradient"):
        grads, keep, send = call(
            functools.partial(gradient_kernel, own_rows),
            (
                shape((LAYERS, ROWS, WIDTH), BF),
                shape((half, WIDTH), F32),
                shape((half + 16, WIDTH), BF),
            ),
        )(arrived)
        partner = lax.ppermute(send, "core", swap)
        blocks = call(
            functools.partial(packing_kernel, own_rows),
            shape((half, WIDTH + half), BF),
        )(keep, send, partner)
        blocks = blocks.reshape(chips, own_rows, WIDTH + half)
        blocks = lax.all_to_all(blocks, ("z", "y"), 0, 0, tiled=True)
        served, weight = call(
            result_kernel,
            (shape((SLOTS, 128), BF), shape((own_rows, WIDTH), F32)),
        )(blocks.reshape(half, WIDTH + half), hot)
    return served[None], grads[None], weight[None]


def solution(mesh):
    devices = mesh.devices
    n_segment, n_dp = devices.shape
    side = 1
    while side * side * 2 < n_dp:
        side *= 2
    fine = Mesh(
        devices.reshape(n_segment, n_dp // (2 * side), side, 2), ("segment",) + DP
    )
    return jax.shard_map(
        body,
        mesh=fine,
        in_specs=(
            P(DP, None, None),
            P(DP),
            P(DP),
            P(DP, None),
            P("segment", None, None),
            P("segment", None, None),
            P("segment", None, None),
            P(DP, None, "segment"),
        ),
        out_specs=(
            P(DP, None, "segment"),
            P("segment", DP, None, None),
            P("segment", DP, None),
        ),
        check_vma=False,
    )
```
